32 devices in a mesh: seed: 4 (over y, x), fsdp: 2 (over core), seq: 4 (over z).
Axes of the slice: x: 2, y: 2, z: 4, core: 2. Of those that a mesh axis runs over, the one named last changes fastest.
Arguments:
- mel_frames: bfloat16 [2, 16384, 80], P('fsdp', 'seq'), may hold values from -6 to 6
- lengths: int32 [2], P('fsdp'), may hold values from 1 to 4096, 5120 in all
- targets: int32 [2, 4096], P('fsdp', 'seq'), may hold values from 0 to 511
- frame_mask: int32 [2, 4096], P('fsdp', 'seq'), may hold values 0 or 1
- stem_weight: bfloat16 [4, 640, 1536], P('seed'), may hold values from -0.25 to 0.25
- conv_in_weight: bfloat16 [4, 1536, 1536], P('seed', ('fsdp', 'seq')), may hold values from -0.15625 to 0.15625
- conv_out_weight: bfloat16 [4, 768, 1536], P('seed', ('fsdp', 'seq')), may hold values from -0.21875 to 0.21875
- depth_weight: bfloat16 [4, 31, 768], P('seed'), may hold values from -1 to 1
- head_weight: bfloat16 [4, 1536, 512], P('seed', ('fsdp', 'seq')), may hold values from -80 to 80
- norm_gain: float32 [4, 2, 1536], P('seed'), may hold values from 0.5 to 1.5
Outputs:
- frame_error: float32 [2, 4096], P('fsdp', 'seq')
- utt_score: float32 [2], P('fsdp')
The draws below stay inside these ranges and needn't reach their ends.
Inputs may be any that keep to these rules, and one draw needn't show every extreme that they name: `lengths`: some utterance has exactly 4096 valid frames.
All inputs are finite; a program needn't handle non-finite values. No bound on the sum of `lengths` or of `frame_mask` on one device may be relied on, other than what follows from the above.
Results may differ from the reference program's by a relative error of at most 0.0022.
Values may be sent and summed in bfloat16 or wider, within the bound.
No kernel may reach another device: no remote copies, remote signals or barrier semaphores. Data moves between devices by JAX's collectives and lax.ppermute only.
A program may use at most 64 MiB of HBM per device.

```python
import math
import jax
import jax.numpy as jnp
import numpy as np
from jax import lax

D = 1536
CONV = 768
VOCAB = 512
MELS = 80
KERNEL = 31
SEEDS = 4
UTTS = 2
FRAMES = 4096
MEL_FRAMES = 16384
N_FSDP = 2


def draw_head_weight(key, part):
    base_key = jax.random.fold_in(key, 0)
    shape = (SEEDS, D, VOCAB)
    base = jax.random.truncated_normal(base_key, -4.0, 4.0, shape, jnp.float32)
    weight = base * (3.0 / math.sqrt(D))
    return weight.astype(jnp.bfloat16)


def with_ends(values, key, least, top_value):
    shape = values.shape
    index_at = [jax.random.randint(jax.random.fold_in(key, axis), (), 0, shape[axis]) for axis in range(len(shape))]
    values = values.at[tuple(index_at)].set(least)
    longest = shape.index(max(shape))
    index_at[longest] = (index_at[longest] + 1) % shape[longest]
    return values.at[tuple(index_at)].set(top_value)


def levels(key, dims, cuts, low, high):
    loudness = 1.0
    for dim, blocks in cuts:
        draws = jax.random.uniform(jax.random.fold_in(jax.random.fold_in(key, 6), dim), (blocks,), jnp.float32, low / len(cuts), high / len(cuts))
        loudness = loudness * jnp.repeat(jnp.exp(draws), dims[dim] // blocks).reshape((-1,) + (1,) * (len(dims) - 1 - dim))
    return loudness


def split_up(number_of, total, bound, skew):
    loads = [(1 << 20) // math.isqrt(rank ** skew) + 1 for rank in range(2, number_of + 1)]
    spare, counts = total - bound - (number_of - 1), [1] * (number_of - 1)
    while spare > 0:
        free = [i for i in range(number_of - 1) if counts[i] < bound]
        mass, remaining = sum([loads[i] for i in free]), spare
        for i in free:
            extra = min(bound - counts[i], max(1, remaining * loads[i] // mass), spare)
            counts[i] = counts[i] + extra
            spare = spare - extra
    return np.array([bound] + counts)


def ragged(own_key, number_of, total, most, lean):
    if number_of == 2:
        one = jax.random.randint(own_key, (), max(1, total - most), min(most, total - 1) + 1)
        return jnp.stack([one, total - one])
    tallies = jnp.asarray(split_up(number_of, total, most, lean), jnp.int32)
    pairs = (number_of - 1) // 2
    source_of, receiver = tallies[1:1 + 2 * pairs:2], tallies[2:2 + 2 * pairs:2]
    slack = jnp.minimum(source_of - 1, most - receiver)
    moved = jax.random.randint(jax.random.fold_in(own_key, 1), (pairs,), 0, 1 << 20) % (slack + 1)
    tallies = tallies.at[1:1 + 2 * pairs:2].set(source_of - moved).at[2:2 + 2 * pairs:2].set(receiver + moved)
    return tallies[jax.random.permutation(jax.random.fold_in(own_key, 2), number_of)]


def noise(rng, shape, scale, bound, shards=(), dtype=jnp.bfloat16):
    factor_of = levels(rng, shape, shards, -0.22, 0.18) if shards else 1.0
    values = jax.random.normal(rng, shape, jnp.float32) * scale * factor_of
    return jnp.minimum(jnp.maximum(values, -bound), bound).astype(dtype)


def setup_inputs(seed: int = 0) -> dict:
    arg_keys = jax.random.split(jax.random.key(seed), 11)
    mel_frames = noise(arg_keys[0], (UTTS, MEL_FRAMES, MELS), 1.0, 6.0, ((0, 2), (1, 4)))
    lengths = ragged(arg_keys[1], UTTS, N_FSDP * FRAMES * 5 // 8, FRAMES, 2).astype(jnp.int32)
    targets = with_ends(jax.random.randint(arg_keys[2], (UTTS, FRAMES), 0, VOCAB), jax.random.fold_in(arg_keys[2], 1), 0, VOCAB - 1).astype(jnp.int32)
    frame_mask = with_ends((jax.random.randint(arg_keys[3], (UTTS, FRAMES), 0, 8) < 7).astype(jnp.int32), jax.random.fold_in(arg_keys[3], 1), 0, 1)
    stem_weight = noise(arg_keys[4], (SEEDS, 8 * MELS, D), (8 * MELS) ** -0.5, 0.25, ((0, 4),))
    conv_in_weight = noise(arg_keys[5], (SEEDS, D, 2 * CONV), D ** -0.5, 0.15625, ((0, 4), (1, 8)))
    conv_out_weight = noise(arg_keys[6], (SEEDS, CONV, D), CONV ** -0.5, 0.21875, ((0, 4), (1, 8)))
    depth_weight = noise(arg_keys[7], (SEEDS, KERNEL, CONV), KERNEL ** -0.5, 1.0, ((0, 4),))
    head_weight = draw_head_weight(jax.random.fold_in(arg_keys[10], 71), 0)
    norm_gain = jnp.clip(1.0 + 0.1 * jax.random.normal(arg_keys[9], (SEEDS, 2, D), jnp.float32), 0.5, 1.5)
    return {"mel_frames": mel_frames, "lengths": lengths, "targets": targets, "frame_mask": frame_mask, "stem_weight": stem_weight, "conv_in_weight": conv_in_weight, "conv_out_weight": conv_out_weight, "depth_weight": depth_weight, "head_weight": head_weight, "norm_gain": norm_gain}


def layer_norm(values, gain_row):
    row_mean = lax.optimization_barrier(jnp.mean(values, axis=-1, keepdims=True))
    centred = values - row_mean
    row_var = lax.optimization_barrier(jnp.mean(centred * centred, axis=-1, keepdims=True))
    return (centred * lax.rsqrt(row_var + 1e-05) * gain_row).astype(jnp.bfloat16)

def utterance(weights, mel_block, length, target_ids, mask_row):
    stem_matrix, gate_matrix, back_matrix, depth_taps, head_matrix, gain_rows = weights
    frame_count = target_ids.shape[0]
    blocks = mel_block.reshape(frame_count, -1)
    following = jnp.concatenate([blocks[1:], jnp.zeros_like(blocks[:1])], 0)
    half_width = blocks.shape[1]
    stem_out = (jnp.dot(blocks, stem_matrix[:half_width], preferred_element_type=jnp.float32) + jnp.dot(following, stem_matrix[half_width:], preferred_element_type=jnp.float32)).astype(jnp.bfloat16)
    positions = jnp.arange(frame_count).astype(jnp.int32)
    frame_live = positions < length
    live_column = frame_live[:, None].astype(jnp.float32)
    normed_one = layer_norm(stem_out.astype(jnp.float32), gain_rows[0])
    mixed_rows = jnp.dot(normed_one, gate_matrix, preferred_element_type=jnp.float32)
    gated_rows = (mixed_rows[:, :CONV] * jax.nn.sigmoid(mixed_rows[:, CONV:]) * live_column).astype(jnp.bfloat16)
    halo_width = KERNEL // 2
    padded = jnp.pad(gated_rows, ((halo_width, halo_width), (0, 0)))
    depthwise = jnp.zeros((frame_count, CONV), jnp.float32)
    for tap_index in range(KERNEL):
        depthwise = depthwise + padded[tap_index:tap_index + frame_count].astype(jnp.float32) * depth_taps[tap_index].astype(jnp.float32)
    swished = jax.nn.silu(depthwise).astype(jnp.bfloat16)
    after_conv = stem_out.astype(jnp.float32) + jnp.dot(swished, back_matrix, preferred_element_type=jnp.float32)
    normed_two = layer_norm(after_conv, gain_rows[1])
    logits = jnp.dot(normed_two, head_matrix, preferred_element_type=jnp.float32)
    posterior = jax.nn.softmax(logits, axis=-1)
    onehot = (jnp.arange(logits.shape[1]).astype(jnp.int32)[None, :] == target_ids[:, None]).astype(jnp.float32)
    differ = posterior - onehot
    frame_err = jnp.sqrt(lax.optimization_barrier(jnp.sum(differ * differ, axis=-1)))
    return frame_err * frame_live.astype(jnp.float32) * mask_row.astype(jnp.float32)

def reference(mel_frames, lengths, targets, frame_mask, stem_weight, conv_in_weight, conv_out_weight, depth_weight, head_weight, norm_gain):

    def per_seed(seed_index):
        weights = (stem_weight[seed_index], conv_in_weight[seed_index], conv_out_weight[seed_index], depth_weight[seed_index], head_weight[seed_index], norm_gain[seed_index])

        def per_utt(utt_index):
            return utterance(weights, mel_frames[utt_index], lengths[utt_index], targets[utt_index], frame_mask[utt_index])
        return lax.map(per_utt, jnp.arange(UTTS).astype(jnp.int32))
    errors = lax.map(per_seed, jnp.arange(SEEDS).astype(jnp.int32))
    frame_error = lax.optimization_barrier(jnp.sum(errors, axis=0)) / jnp.float32(SEEDS)
    utt_score = lax.optimization_barrier(jnp.sum(frame_error, axis=-1)) / lengths.astype(jnp.float32)
    return (frame_error, utt_score)
```

```python
import jax
import jax.numpy as jnp
from jax import lax
from jax.experimental import pallas as pl
from jax.experimental.pallas import tpu as pltpu
from jax.sharding import PartitionSpec as P

LANES = 128
EDGE = 16
VMEM_BYTES = 56 * 1024 * 1024


def norm_rows(values, gain_row):
    row_mean = jnp.mean(values, axis=-1, keepdims=True)
    centred = values - row_mean
    row_var = jnp.mean(centred * centred, axis=-1, keepdims=True)
    return (centred * lax.rsqrt(row_var + 1e-05) * gain_row).astype(jnp.bfloat16)


def stem_kernel(meta, pairs_ref, stem_ref, gain_ref, stem_out_ref, normed_ref):
    slot = pl.program_id(0)
    rows = pairs_ref.shape[1]
    part = rows // 2

    @pl.when(meta[8 + slot] > 0)
    def _():
        for at in (0, part):
            here = slice(at, at + part)
            stem_out = jnp.dot(
                pairs_ref[0, here, :], stem_ref[...], preferred_element_type=jnp.float32
            ).astype(jnp.bfloat16)
            stem_out_ref[0, here, :] = stem_out
            normed_ref[0, here, :] = norm_rows(stem_out.astype(jnp.float32), gain_ref[0:1, :])


def conv_kernel(
    meta,
    normed_ref,
    taps_ref,
    own_ref,
    near_ref,
    hub_ref,
    far_ref,
    mate_own_ref,
    mate_rest_ref,
    swished_ref,
    weight,
    gated_a,
    gated_b,
    convolved,
    sems,
):
    slot = pl.program_id(0)
    rows = normed_ref.shape[1]
    frames = swished_ref.shape[1]
    channels = swished_ref.shape[2]
    tap_count = taps_ref.shape[0]
    piece = own_ref.shape[0]
    side = meta[16]

    @pl.when(jnp.logical_and(slot == 0, meta[17] > 0))
    def _():
        copies = []
        for i, (ref, first, other) in enumerate(
            (
                (own_ref, 0, 0),
                (near_ref, 0, 0),
                (hub_ref, 0, 0),
                (far_ref, 0, 0),
                (mate_own_ref, 0, 1),
                (mate_rest_ref, 0, 1),
                (mate_rest_ref, piece, 1),
                (mate_rest_ref, 2 * piece, 1),
            )
        ):
            core = 1 - side if other else side
            block = core * 4 + meta[12 + i % 4]
            copies.append(
                pltpu.make_async_copy(
                    ref.at[pl.ds(first, piece)],
                    weight.at[pl.ds(pl.multiple_of(block * piece, 16), piece)],
                    sems.at[i],
                )
            )
        for copy in copies:
            copy.start()
        for copy in copies:
            copy.wait()

    @pl.when(meta[8 + slot] > 0)
    def _():
        at = meta[slot] - EDGE + lax.broadcasted_iota(jnp.int32, (rows, 1), 0)
        live = jnp.logical_and(at >= 0, at < meta[4 + slot]).astype(jnp.float32)
        stride = frames // 8
        run = 16
        buffers = (gated_a, gated_b)

        def gate(block, into):
            low = block * LANES
            right = jnp.concatenate(
                [weight[:, low : low + LANES], weight[:, channels + low : channels + low + LANES]], axis=1
            )
            mixed = jnp.dot(normed_ref[0], right, preferred_element_type=jnp.float32)
            gated = mixed[:, :LANES] * jax.nn.sigmoid(mixed[:, LANES:]) * live
            into[...] = gated.astype(jnp.bfloat16).astype(jnp.float32)

        def convolve(block, source):
            low = block * LANES
            for start in range(0, stride, run):
                sums = [None] * run
                for row in range(start, start + run + tap_count - 1):
                    value = source[pl.ds(row + EDGE - tap_count // 2, 8, stride=stride), :]
                    for m in range(max(start, row - tap_count + 1), min(start + run, row + 1)):
                        term = value * taps_ref[row - m, :, low : low + LANES]
                        k = m - start
                        sums[k] = term if sums[k] is None else sums[k] + term
                for k in range(run):
                    total = sums[k]
                    convolved[pl.ds(start + k, 8, stride=stride), :] = total * jax.nn.sigmoid(total)
            swished_ref[0, :, low : low + LANES] = convolved[...].astype(jnp.bfloat16)

        blocks = channels // LANES
        gate(0, buffers[0])
        for block in range(blocks):
            if block + 1 < blocks:
                gate(block + 1, buffers[(block + 1) % 2])
            convolve(block, buffers[block % 2])


def head_kernel(
    meta,
    swished_ref,
    stem_out_ref,
    code_ref,
    gain_ref,
    own_ref,
    near_ref,
    hub_ref,
    far_ref,
    mate_own_ref,
    mate_rest_ref,
    error_ref,
    back,
    head,
    sems,
):
    slot = pl.program_id(0)
    frames = swished_ref.shape[1]
    vocab = head.shape[1]
    groups = back.shape[1] // vocab
    piece = own_ref.shape[0]
    back_rows = back.shape[0] // 8
    head_rows = head.shape[0] // 8
    group_rows = head_rows // groups
    side = meta[16]

    @pl.when(jnp.logical_and(slot == 0, meta[17] > 0))
    def _():
        copies = []
        for i, (ref, first, other) in enumerate(
            (
                (own_ref, 0, 0),
                (near_ref, 0, 0),
                (hub_ref, 0, 0),
                (far_ref, 0, 0),
                (mate_own_ref, 0, 1),
                (mate_rest_ref, 0, 1),
                (mate_rest_ref, piece, 1),
                (mate_rest_ref, 2 * piece, 1),
            )
        ):
            core = 1 - side if other else side
            block = core * 4 + meta[12 + i % 4]
            copies.append(
                pltpu.make_async_copy(
                    ref.at[pl.ds(first, back_rows)],
                    back.at[pl.ds(pl.multiple_of(block * back_rows, 16), back_rows)],
                    sems.at[i, 0],
                )
            )
            for g in range(groups):
                copies.append(
                    pltpu.make_async_copy(
                        ref.at[pl.ds(first + back_rows, group_rows), pl.ds(g * vocab, vocab)],
                        head.at[pl.ds(pl.multiple_of(block * head_rows + g * group_rows, 16), group_rows)],
                        sems.at[i, 1 + g],
                    )
                )
        for copy in copies:
            copy.start()
        for copy in copies:
            copy.wait()

    @pl.when(meta[8 + slot] <= 0)
    def _():
        error_ref[...] = jnp.zeros_like(error_ref)

    @pl.when(meta[8 + slot] > 0)
    def _():
        part = 256
        diagonal = lax.broadcasted_iota(jnp.int32, (LANES, LANES), 0) == lax.broadcasted_iota(
            jnp.int32, (LANES, LANES), 1
        )
        for at in range(0, frames, part):
            here = slice(at, at + part)
            after = jnp.dot(swished_ref[0, here, :], back[...], preferred_element_type=jnp.float32)
            after = after + stem_out_ref[0, EDGE + at : EDGE + at + part, :].astype(jnp.float32)
            normed = norm_rows(after, gain_ref[1:2, :])
            logits = jnp.dot(normed, head[...], preferred_element_type=jnp.float32)
            top = jnp.max(logits, axis=-1, keepdims=True)
            grown = jnp.exp(logits - top)
            posterior = grown / jnp.sum(grown, axis=-1, keepdims=True)
            code = code_ref[0, here, :]
            onehot = (lax.broadcasted_iota(jnp.int32, (part, vocab), 1) == code).astype(jnp.float32)
            differ = posterior - onehot
            error = jnp.sqrt(jnp.sum(differ * differ, axis=-1, keepdims=True))
            error = jnp.where(code >= 0, error, 0.0)
            for row in range(0, part, LANES):
                column = error[row : row + LANES, :]
                error_ref[0, :, at + row : at + row + LANES] = jnp.sum(
                    jnp.where(diagonal, column, 0.0), axis=0, keepdims=True
                )


def call(kernel, grid, in_specs, out_specs, out_shape, scratch, flops, moved, operands):
    return pl.pallas_call(
        kernel,
        grid_spec=pltpu.PrefetchScalarGridSpec(
            num_scalar_prefetch=1,
            grid=grid,
            in_specs=in_specs,
            out_specs=out_specs,
            scratch_shapes=scratch,
        ),
        out_shape=out_shape,
        compiler_params=pltpu.CompilerParams(
            dimension_semantics=("arbitrary",), vmem_limit_bytes=VMEM_BYTES
        ),
        cost_estimate=pl.CostEstimate(flops=flops, bytes_accessed=moved, transcendentals=0),
    )(*operands)


def whole(shape):
    return pl.BlockSpec(shape, lambda i, meta: (0,) * len(shape))


def by_slot(shape):
    return pl.BlockSpec((1,) + shape, lambda i, meta: (i,) + (0,) * len(shape))


OUTWARD = [(0, 1), (3, 2)]
ACROSS = [(1, 2), (2, 1)]
BEYOND = [(0, 2), (3, 1)]
SWAP = [(0, 1), (1, 0)]


def to_hub(x, pairs):
    return lax.ppermute(x, "seq", pairs)


def to_mate(x):
    pairs = [(a * 4 + z, b * 4 + z) for a, b in SWAP for z in (1, 2)]
    return lax.ppermute(x, ("fsdp", "seq"), pairs)


def hub_body(
    mel_frames,
    lengths,
    targets,
    frame_mask,
    stem_weight,
    conv_in_weight,
    conv_out_weight,
    depth_weight,
    head_weight,
    norm_gain,
):
    chip = lax.axis_index("seq")
    side = lax.axis_index("fsdp")
    seed = lax.axis_index("seed")
    seeds = lax.axis_size("seed")
    rows = targets.shape[1]
    width = stem_weight.shape[2]
    channels = depth_weight.shape[2]
    vocab = head_weight.shape[2]
    tile = rows // 2
    low = chip == 1
    is_hub = jnp.logical_or(low, chip == 2)

    first = conv_in_weight[0]
    groups = width // vocab
    head_rows = head_weight.shape[1]
    second = jnp.concatenate(
        [
            conv_out_weight[0],
            jnp.concatenate(jnp.split(head_weight[0], groups, axis=0), axis=1),
        ],
        axis=0,
    )
    first_in = [to_hub(first, pairs) for pairs in (OUTWARD, ACROSS, BEYOND)]
    first_mate = to_mate(first)
    second_mate = to_mate(second)

    blocks = mel_frames[0].reshape(rows, -1)
    share = rows // seeds
    quarter = lax.dynamic_slice_in_dim(blocks, seed * share, share, 0)
    outer = lax.all_gather(to_hub(quarter, OUTWARD), "seed", axis=0, tiled=True)
    edge = to_hub(jnp.where(low, blocks[-EDGE:], blocks[:EDGE]), ACROSS)
    none = jnp.zeros_like(edge)
    frames = jnp.concatenate(
        [
            jnp.where(low, none, edge),
            jnp.where(low, outer, blocks),
            jnp.where(low, blocks, outer),
            jnp.where(low, edge, none),
            none,
        ],
        axis=0,
    )
    reach = tile + 3 * EDGE
    tiles = [frames[k * tile : k * tile + reach] for k in range(4)]
    mine = jnp.stack([tiles[0], tiles[2]])
    lent = to_mate(jnp.stack([tiles[1], tiles[3]]))
    held = jnp.concatenate([mine, lent], axis=0)
    deep = tile + 2 * EDGE
    pairs = jnp.concatenate([held[:, :deep], held[:, 1 : deep + 1]], axis=2)

    length = lengths[0]
    positions = chip * rows + jnp.arange(rows, dtype=jnp.int32)
    counted = jnp.logical_and(frame_mask[0] > 0, positions < length)
    code = jnp.where(counted, targets[0], -1)
    outer_code = to_hub(code, OUTWARD)
    codes = jnp.concatenate(
        [jnp.where(low, outer_code, code), jnp.where(low, code, outer_code)]
    ).reshape(4, tile)
    lent_ints = to_mate(jnp.concatenate([codes[1], codes[3], lengths]))
    code_slots = jnp.stack([codes[0], codes[2], lent_ints[:tile], lent_ints[tile : 2 * tile]])
    mate_length = lent_ints[2 * tile]

    base = (chip - 1) * 2 * rows
    starts = base + tile * jnp.array([0, 2, 1, 3], jnp.int32)
    spans = jnp.stack([length, length, mate_length, mate_length])
    alive = jnp.logical_and(is_hub, starts < spans).astype(jnp.int32)
    hub = jnp.clip(chip, 1, 2)
    meta = jnp.concatenate(
        [
            starts,
            spans,
            alive,
            jnp.stack([hub, 3 * (hub - 1), 3 - hub, 3 * (2 - hub)]),
            jnp.stack([side, jnp.max(alive)]),
        ]
    ).astype(jnp.int32)

    slots = 4
    gains = norm_gain[0]
    stem_out, normed = call(
        stem_kernel,
        (slots,),
        [by_slot((deep, pairs.shape[2])), whole(stem_weight.shape[1:]), whole(gains.shape)],
        [by_slot((deep, width))] * 2,
        [jax.ShapeDtypeStruct((slots, deep, width), jnp.bfloat16)] * 2,
        [],
        2 * slots * deep * pairs.shape[2] * width,
        slots * deep * (pairs.shape[2] + 2 * width) * 2,
        (meta, pairs, stem_weight[0], gains),
    )

    first_rest = to_mate(jnp.concatenate(first_in, axis=0))
    second_held, _ = lax.optimization_barrier((second, first_in))
    second_in = [to_hub(second_held, pairs_) for pairs_ in (OUTWARD, ACROSS, BEYOND)]

    taps = jnp.broadcast_to(
        depth_weight[0].astype(jnp.float32)[:, None, :], (depth_weight.shape[1], 8, channels)
    )
    apart = pl.BlockSpec(memory_space=pl.ANY)
    swished = call(
        conv_kernel,
        (slots,),
        [by_slot((deep, width)), whole(taps.shape)] + [apart] * 6,
        by_slot((tile, channels)),
        jax.ShapeDtypeStruct((slots, tile, channels), jnp.bfloat16),
        [
            pltpu.VMEM((8 * first.shape[0], first.shape[1]), jnp.bfloat16),
            pltpu.VMEM((deep, LANES), jnp.float32),
            pltpu.VMEM((deep, LANES), jnp.float32),
            pltpu.VMEM((tile, LANES), jnp.float32),
            pltpu.SemaphoreType.DMA((8,)),
        ],
        2 * slots * deep * width * 2 * channels,
        slots * deep * width * 2 + 8 * first.size * 2,
        (meta, normed, taps, first, *first_in, first_mate, first_rest),
    )

    second_rest = to_mate(jnp.concatenate(second_in, axis=0))
    errors = call(
        head_kernel,
        (slots,),
        [by_slot((tile, channels)), by_slot((deep, width)), by_slot((tile, 1)), whole(gains.shape)] + [apart] * 6,
        by_slot((1, tile)),
        jax.ShapeDtypeStruct((slots, 1, tile), jnp.float32),
        [
            pltpu.VMEM((8 * conv_out_weight.shape[1], width), jnp.bfloat16),
            pltpu.VMEM((8 * head_rows, vocab), jnp.bfloat16),
            pltpu.SemaphoreType.DMA((8, 1 + groups)),
        ],
        2 * slots * tile * (channels + vocab) * width,
        slots * tile * (channels + width) * 2,
        (meta, swished, stem_out, code_slots[:, :, None], gains, second, *second_in, second_mate, second_rest),
    )

    errors = errors.reshape(2, 2, tile)
    zero = jnp.zeros_like(errors[0])
    own_part = jnp.stack([errors[0], zero], axis=1)
    lent_part = jnp.stack([zero, errors[1]], axis=1)
    by_utt = jnp.stack(
        [jnp.where(side == 0, own_part, lent_part), jnp.where(side == 0, lent_part, own_part)]
    )
    by_hub = jnp.stack(
        [jnp.where(low, by_utt, 0.0), jnp.where(chip == 2, by_utt, 0.0)], axis=1
    ).reshape(2, 4 * rows)
    total = lax.psum(by_hub, ("seed", "fsdp", "seq")) / jnp.float32(seeds)
    mine_total = lax.dynamic_index_in_dim(total, side, 0, keepdims=True)
    frame_error = lax.dynamic_slice_in_dim(mine_total, chip * rows, rows, 1)
    utt_score = jnp.sum(mine_total) / length.astype(jnp.float32)
    return (frame_error, utt_score.reshape(1))


def from_behind(x, axis, by):
    count = lax.axis_size(axis)
    pairs = [(i, i + by) for i in range(count) if 0 <= i + by < count]
    return lax.ppermute(x, axis, pairs)


def extended(x, sides, width):
    for axis, dim in sides:
        count, length = (lax.axis_size(axis), x.shape[dim])
        up = [(i, (i + 1) % count) for i in range(count - 1)]
        down = [(j, i) for i, j in up]
        last = lax.slice_in_dim(x, length - width, length, axis=dim)
        first = lax.slice_in_dim(x, 0, width, axis=dim)
        before = lax.ppermute(last, axis, up)
        after = lax.ppermute(first, axis, down)
        x = jnp.concatenate([before, x, after], axis=dim)
    return x


def layer_norm(values, gain_row):
    row_mean = jnp.mean(values, axis=-1, keepdims=True)
    centred = values - row_mean
    row_var = jnp.mean(centred * centred, axis=-1, keepdims=True)
    return (centred * lax.rsqrt(row_var + 1e-05) * gain_row).astype(jnp.bfloat16)


def block_product(left_rows, right_matrix):
    return jnp.dot(left_rows, right_matrix, preferred_element_type=jnp.float32)


def row_product(activations, shard_piece):
    return block_product(activations, shard_piece[0])


def body(
    mel_frames,
    lengths,
    targets,
    frame_mask,
    stem_weight,
    conv_in_weight,
    conv_out_weight,
    depth_weight,
    head_weight,
    norm_gain,
):
    frame_rows = targets.shape[1]
    blocks = mel_frames[0].reshape(frame_rows, -1)
    next_block = from_behind(blocks[:1], "seq", -1)
    following = jnp.concatenate([blocks[1:], next_block], 0)
    half_width = blocks.shape[1]
    stem_matrix = stem_weight[0]
    stem_out = (
        jnp.dot(blocks, stem_matrix[:half_width], preferred_element_type=jnp.float32)
        + jnp.dot(following, stem_matrix[half_width:], preferred_element_type=jnp.float32)
    ).astype(jnp.bfloat16)
    offset = lax.axis_index("seq") * frame_rows
    length = lengths[0]
    positions = offset + jnp.arange(frame_rows, dtype=jnp.int32)
    frame_live = positions < length
    gain_rows = norm_gain[0]
    normed_one = layer_norm(stem_out.astype(jnp.float32), gain_rows[0])
    tap_count = depth_weight.shape[1]
    channels = depth_weight.shape[2]
    halo_width = tap_count // 2
    conv_input = extended(normed_one, (("seq", 0),), halo_width)
    mixed_rows = row_product(
        conv_input, lax.all_gather(conv_in_weight, ("fsdp", "seq"), axis=1, tiled=True)
    )
    input_positions = offset - halo_width + jnp.arange(conv_input.shape[0], dtype=jnp.int32)
    input_live = jnp.logical_and(input_positions >= 0, input_positions < length)
    gated_rows = (
        mixed_rows[:, :channels]
        * jax.nn.sigmoid(mixed_rows[:, channels:])
        * input_live[:, None].astype(jnp.float32)
    ).astype(jnp.bfloat16)
    depthwise = jnp.zeros((frame_rows, channels), jnp.float32)
    for tap_index in range(tap_count):
        depthwise = depthwise + gated_rows[tap_index : tap_index + frame_rows].astype(
            jnp.float32
        ) * depth_weight[0, tap_index].astype(jnp.float32)
    swished = jax.nn.silu(depthwise).astype(jnp.bfloat16)
    conv_proj = row_product(
        swished, lax.all_gather(conv_out_weight, ("fsdp", "seq"), axis=1, tiled=True)
    )
    after_conv = stem_out.astype(jnp.float32) + conv_proj
    normed_two = layer_norm(after_conv, gain_rows[1])
    logits = row_product(
        normed_two, lax.all_gather(head_weight, ("fsdp", "seq"), axis=1, tiled=True)
    )
    posterior = jax.nn.softmax(logits, axis=-1)
    vocab_size = logits.shape[1]
    onehot = (jnp.arange(vocab_size, dtype=jnp.int32)[None, :] == targets[0][:, None]).astype(
        jnp.float32
    )
    differ = posterior - onehot
    frame_err = (
        jnp.sqrt(jnp.sum(differ * differ, axis=-1))
        * frame_live.astype(jnp.float32)
        * frame_mask[0].astype(jnp.float32)
    )
    seed_count = lax.axis_size("seed")
    frame_error = lax.psum(frame_err, "seed") / jnp.float32(seed_count)
    numerator = lax.psum(jnp.sum(frame_error), "seq")
    utt_score = numerator / length.astype(jnp.float32)
    return (frame_error[None, :], utt_score.reshape(1))


def solution(mesh):
    in_specs = (
        P("fsdp", "seq", None),
        P("fsdp"),
        P("fsdp", "seq"),
        P("fsdp", "seq"),
        P("seed", None, None),
        P("seed", ("fsdp", "seq"), None),
        P("seed", ("fsdp", "seq"), None),
        P("seed", None, None),
        P("seed", ("fsdp", "seq"), None),
        P("seed", None, None),
    )
    out_specs = (P("fsdp", "seq"), P("fsdp"))
    hubs = mesh.shape["seq"] == 4 and mesh.shape["fsdp"] == 2
    return jax.shard_map(
        hub_body if hubs else body, mesh=mesh, in_specs=in_specs, out_specs=out_specs, check_vma=False
    )
```

```python
import functools

import jax
import jax.numpy as jnp
from jax import lax
from jax.experimental import pallas as pl
from jax.experimental.pallas import tpu as pltpu
from jax.sharding import PartitionSpec as P

LANES = 128
CHUNKS = 8
EDGE = 16
VMEM_BYTES = 56 * 1024 * 1024


def norm_rows(values, gain_row):
    row_mean = jnp.mean(values, axis=-1, keepdims=True)
    centred = values - row_mean
    row_var = jnp.mean(centred * centred, axis=-1, keepdims=True)
    return (centred * lax.rsqrt(row_var + 1e-05) * gain_row).astype(jnp.bfloat16)


def sigmoid(x):
    return 0.5 * jnp.tanh(0.5 * x) + 0.5


def stem_kernel(meta, pairs_ref, stem_ref, gain_ref, stem_out_ref, normed_ref):
    slot = pl.program_id(0)
    rows = pairs_ref.shape[1]
    part = rows // 2

    @pl.when(meta[5 + slot] > 0)
    def _():
        parts = (slice(0, part), slice(part, rows))
        made = [
            jnp.dot(pairs_ref[0, here, :], stem_ref[...], preferred_element_type=jnp.float32).astype(jnp.bfloat16)
            for here in parts
        ]
        for here, stem_out in zip(parts, made):
            stem_out_ref[0, here, :] = stem_out
            normed_ref[0, here, :] = norm_rows(stem_out.astype(jnp.float32), gain_ref[0:1, :])


def shards(meta, pieces):
    side = meta[13]
    length = pieces[0].shape[0]
    mine = [(pieces[i], 0, side * 4 + meta[9 + i]) for i in range(4)]
    return mine + [(pieces[4], i * length, (1 - side) * 4 + meta[9 + i]) for i in range(4)]


def conv_kernel(first_slot, meta, normed_ref, taps_ref, *rest):
    pieces = rest[:5]
    swished_ref, weight, gated_a, gated_b, margin, mask, sems = rest[-7:]
    slot = pl.program_id(0) + first_slot
    rows = normed_ref.shape[1]
    frames = swished_ref.shape[1]
    channels = swished_ref.shape[2]
    tap_count = taps_ref.shape[0]
    reach = tap_count // 2
    piece = pieces[0].shape[0]
    run_length = frames // CHUNKS

    @pl.when(jnp.logical_and(pl.program_id(0) == 0, meta[14] > 0))
    def _():
        copies = [
            pltpu.make_async_copy(
                ref.at[pl.ds(at, piece)], weight.at[pl.ds(pl.multiple_of(block * piece, 16), piece)], sems.at[i]
            )
            for i, (ref, at, block) in enumerate(shards(meta, pieces))
        ]
        for copy in copies:
            copy.start()
        for copy in copies:
            copy.wait()

    @pl.when(meta[5 + slot] > 0)
    def _():
        row = lax.broadcasted_iota(jnp.int32, (rows, LANES), 0)
        inner = (row % CHUNKS) * run_length + row // CHUNKS
        outer = jnp.where(row < frames + EDGE, row - frames - EDGE, row - EDGE)
        at = meta[slot] + jnp.where(row < frames, inner, outer)
        mask[...] = jnp.logical_and(at >= 0, at < meta[4]).astype(jnp.float32)
        sublane = lax.broadcasted_iota(jnp.int32, (CHUNKS, LANES), 0)
        buffers = (gated_a, gated_b)

        def gate(block, into):
            low = block * LANES
            right = jnp.concatenate(
                [weight[:, low : low + LANES], weight[:, channels + low : channels + low + LANES]], axis=1
            )
            mixed = jnp.dot(normed_ref[0], right, preferred_element_type=jnp.float32)
            gated = mixed[:, :LANES] * sigmoid(mixed[:, LANES:]) * mask[...]
            gated = gated.astype(jnp.bfloat16).astype(jnp.float32)
            into[reach : reach + run_length] = gated[:frames].reshape(run_length, CHUNKS, LANES)
            margin[...] = gated[frames:]
            for i in range(reach):
                before = pltpu.roll(into[run_length + i], 1, 0)
                edge = margin[EDGE - reach + i : EDGE - reach + i + 1, :]
                into[i] = jnp.where(sublane == 0, edge, before)
                after = pltpu.roll(into[reach + i], CHUNKS - 1, 0)
                edge = margin[EDGE + i : EDGE + i + 1, :]
                into[reach + run_length + i] = jnp.where(sublane == CHUNKS - 1, edge, after)

        def convolve(block, source):
            low = block * LANES
            run = 16
            for start in range(0, run_length, run):
                sums = [None] * run
                for at in range(start, start + run + tap_count - 1):
                    value = source[at]
                    for m in range(max(start, at - tap_count + 1), min(start + run, at + 1)):
                        term = value * taps_ref[at - m, :, low : low + LANES]
                        k = m - start
                        sums[k] = term if sums[k] is None else sums[k] + term
                for k in range(0, run, 2):
                    total = jnp.concatenate(sums[k : k + 2], axis=0)
                    first = (start + k) * CHUNKS
                    swished_ref[0, first : first + 2 * CHUNKS, low : low + LANES] = (
                        total * sigmoid(total)
                    ).astype(jnp.bfloat16)

        blocks = channels // LANES
        gate(0, buffers[0])
        for block in range(blocks):
            if block + 1 < blocks:
                gate(block + 1, buffers[(block + 1) % 2])
            convolve(block, buffers[block % 2])


def head_kernel(meta, swished_ref, stem_out_ref, code_ref, gain_ref, *rest):
    pieces = rest[:5]
    error_ref, back, head, sems = rest[5:]
    slot = pl.program_id(0)
    frames = swished_ref.shape[1]
    vocab = head.shape[1]
    groups = back.shape[1] // vocab
    back_rows = back.shape[0] // 8
    head_rows = head.shape[0] // 8
    group_rows = head_rows // groups

    @pl.when(jnp.logical_and(pl.program_id(0) == 0, meta[14] > 0))
    def _():
        copies = []
        for i, (ref, at, block) in enumerate(shards(meta, pieces)):
            copies.append(
                pltpu.make_async_copy(
                    ref.at[pl.ds(at, back_rows)],
                    back.at[pl.ds(pl.multiple_of(block * back_rows, 16), back_rows)],
                    sems.at[i, 0],
                )
            )
            for g in range(groups):
                copies.append(
                    pltpu.make_async_copy(
                        ref.at[pl.ds(at + back_rows, group_rows), pl.ds(g * vocab, vocab)],
                        head.at[pl.ds(pl.multiple_of(block * head_rows + g * group_rows, 16), group_rows)],
                        sems.at[i, 1 + g],
                    )
                )
        for copy in copies:
            copy.start()
        for copy in copies:
            copy.wait()

    @pl.when(meta[5 + slot] <= 0)
    def _():
        error_ref[...] = jnp.zeros_like(error_ref)

    @pl.when(meta[5 + slot] > 0)
    def _():
        part = 256
        lane = lax.broadcasted_iota(jnp.int32, (CHUNKS, LANES), 1)
        starts = range(0, frames, part)
        after = [
            jnp.dot(swished_ref[0, at : at + part, :], back[...], preferred_element_type=jnp.float32)
            for at in starts
        ]
        logits = []
        for at, values in zip(starts, after):
            values = values + stem_out_ref[0, at : at + part, :].astype(jnp.float32)
            normed = norm_rows(values, gain_ref[1:2, :])
            logits.append(jnp.dot(normed, head[...], preferred_element_type=jnp.float32))
        row = jnp.zeros((CHUNKS, LANES), jnp.float32)
        for at, scores in zip(starts, logits):
            top = jnp.max(scores, axis=-1, keepdims=True)
            grown = jnp.exp(scores - top)
            posterior = grown * (1.0 / jnp.sum(grown, axis=-1, keepdims=True))
            code = code_ref[0, at : at + part, :]
            onehot = (lax.broadcasted_iota(jnp.int32, (part, vocab), 1) == code).astype(jnp.float32)
            differ = posterior - onehot
            error = jnp.sqrt(jnp.sum(differ * differ, axis=-1, keepdims=True))
            error = jnp.where(code >= 0, error, 0.0)
            for m in range(part // CHUNKS):
                step = error[m * CHUNKS : (m + 1) * CHUNKS, :]
                row = row + jnp.where(lane == at // CHUNKS + m, step, 0.0)
        error_ref[0] = row


def call(kernel, grid, in_specs, out_specs, out_shape, scratch, flops, moved, operands, aliases={}):
    return pl.pallas_call(
        kernel,
        grid_spec=pltpu.PrefetchScalarGridSpec(
            num_scalar_prefetch=1,
            grid=grid,
            in_specs=in_specs,
            out_specs=out_specs,
            scratch_shapes=scratch,
        ),
        out_shape=out_shape,
        input_output_aliases=aliases,
        compiler_params=pltpu.CompilerParams(
            dimension_semantics=("arbitrary",), vmem_limit_bytes=VMEM_BYTES
        ),
        cost_estimate=pl.CostEstimate(flops=flops // 16, bytes_accessed=moved // 16, transcendentals=0),
    )(*operands)


def whole(shape):
    return pl.BlockSpec(shape, lambda i, meta: (0,) * len(shape))


def by_slot(shape, first=0):
    return pl.BlockSpec((1,) + shape, lambda i, meta: (i + first,) + (0,) * len(shape))


INWARD = [(0, 1), (3, 2)]
ACROSS = [(1, 2), (2, 1)]
BEYOND = [(0, 2), (3, 1)]
OUTWARD = [(1, 0), (2, 3)]
OUT_BEYOND = [(2, 0), (1, 3)]


def along(x, pairs):
    return lax.ppermute(x, "seq", pairs)


def to_mate(x):
    pairs = [(a * 4 + z, (1 - a) * 4 + z) for a in (0, 1) for z in (1, 2)]
    return lax.ppermute(x, ("fsdp", "seq"), pairs)


def seed_swap(x, bit):
    return lax.ppermute(x, "seed", [(i, i ^ bit) for i in range(4)])


def hub_body(
    mel_frames,
    lengths,
    targets,
    frame_mask,
    stem_weight,
    conv_in_weight,
    conv_out_weight,
    depth_weight,
    head_weight,
    norm_gain,
):
    chip = lax.axis_index("seq")
    side = lax.axis_index("fsdp")
    seed = lax.axis_index("seed")
    seeds = lax.axis_size("seed")
    rows = targets.shape[1]
    width = stem_weight.shape[2]
    channels = depth_weight.shape[2]
    vocab = head_weight.shape[2]
    step = mel_frames.shape[1] // rows
    tile = rows // 2
    low = chip == 1
    is_hub = jnp.logical_or(low, chip == 2)

    first = conv_in_weight[0]
    hub_first = along(first, ACROSS)
    share = rows // seeds
    quarter = lax.dynamic_slice_in_dim(mel_frames[0], seed * share * step, share * step, 0).reshape(share, -1)
    quarter_in = along(quarter, INWARD)
    margin = step * EDGE
    edge = along(jnp.where(low, mel_frames[0, -margin:], mel_frames[0, :margin]).reshape(EDGE, -1), ACROSS)
    first_held, _ = lax.optimization_barrier((first, quarter_in))
    near_first = along(first_held, INWARD)
    far_first = along(first_held, BEYOND)

    pair = seed_swap(quarter_in, 1)
    odd = seed % 2 == 1
    half = jnp.concatenate([jnp.where(odd, pair, quarter_in), jnp.where(odd, quarter_in, pair)], axis=0)
    other = seed_swap(half, 2)
    upper = seed // 2 == 1

    groups = width // vocab
    head_rows = head_weight.shape[1]
    second = jnp.concatenate(
        [
            conv_out_weight[0],
            jnp.concatenate(jnp.split(head_weight[0], groups, axis=0), axis=1),
        ],
        axis=0,
    )
    second_held, other, edge, hub_first = lax.optimization_barrier((second, other, edge, hub_first))
    near_second = along(second_held, INWARD)
    far_second = along(second_held, BEYOND)
    hub_second = along(second_held, ACROSS)
    outer = jnp.concatenate([jnp.where(upper, other, half), jnp.where(upper, half, other)], axis=0)

    blocks = mel_frames[0].reshape(rows, -1)
    none = jnp.zeros_like(edge)
    frames = jnp.concatenate(
        [
            jnp.where(low, none, edge),
            jnp.where(low, outer, blocks),
            jnp.where(low, blocks, outer),
            jnp.where(low, edge, none),
            none,
        ],
        axis=0,
    )
    slots = 4
    deep = tile + 2 * EDGE
    pairs = jnp.concatenate([frames[:-1], frames[1:]], axis=1)
    inner = pairs[EDGE : EDGE + slots * tile].reshape(slots, CHUNKS, tile // CHUNKS, -1)
    inner = inner.transpose(0, 2, 1, 3).reshape(slots, tile, -1)
    before = jnp.stack([pairs[k * tile : k * tile + EDGE] for k in range(slots)])
    after = jnp.stack([pairs[(k + 1) * tile + EDGE : (k + 1) * tile + 2 * EDGE] for k in range(slots)])
    pairs = jnp.concatenate([inner, before, after], axis=1)

    length = lengths[0]
    positions = chip * rows + jnp.arange(rows, dtype=jnp.int32)
    counted = jnp.logical_and(frame_mask[0] > 0, positions < length)
    code = jnp.where(counted, targets[0], -1)
    starts = (chip - 1) * 2 * rows + tile * jnp.arange(slots, dtype=jnp.int32)
    alive = jnp.logical_and(is_hub, starts < length).astype(jnp.int32)
    hub = jnp.clip(chip, 1, 2)
    meta = jnp.concatenate(
        [
            starts,
            lengths,
            alive,
            jnp.stack([hub, 3 * (hub - 1), 3 - hub, 3 * (2 - hub), side, jnp.max(alive)]),
        ]
    ).astype(jnp.int32)

    gains = norm_gain[0]
    stem_out, normed = call(
        stem_kernel,
        (slots,),
        [by_slot((deep, pairs.shape[2])), whole(stem_weight.shape[1:]), whole(gains.shape)],
        [by_slot((deep, width))] * 2,
        [jax.ShapeDtypeStruct((slots, deep, width), jnp.bfloat16)] * 2,
        [],
        2 * slots * deep * pairs.shape[2] * width,
        slots * deep * (pairs.shape[2] + 2 * width) * 2,
        (meta, pairs, stem_weight[0], gains),
    )

    near_first, far_first, normed = lax.optimization_barrier((near_first, far_first, normed))
    mine = [first, near_first, hub_first, far_first]
    first_pieces = (*mine, to_mate(jnp.concatenate(mine, axis=0)))
    code_held, _ = lax.optimization_barrier((code, first_pieces[-1]))
    outer_code = along(code_held, INWARD)
    codes = jnp.concatenate([jnp.where(low, outer_code, code), jnp.where(low, code, outer_code)])
    codes = codes.reshape(slots, CHUNKS, tile // CHUNKS).transpose(0, 2, 1).reshape(slots, tile, 1)

    taps = jnp.broadcast_to(
        depth_weight[0].astype(jnp.float32)[:, None, :], (depth_weight.shape[1], CHUNKS, channels)
    )
    apart = pl.BlockSpec(memory_space=pl.ANY)
    extent = tile // CHUNKS + depth_weight.shape[1] - 1
    def convolve(part, normed, pieces, *made):
        return call(
            functools.partial(conv_kernel, 2 * part),
            (2,),
            [by_slot((deep, width), 2 * part), whole(taps.shape)] + [apart] * (5 + len(made)),
            by_slot((tile, channels), 2 * part),
            jax.ShapeDtypeStruct((slots, tile, channels), jnp.bfloat16),
            [
                pltpu.VMEM((8 * first.shape[0], first.shape[1]), jnp.bfloat16),
                pltpu.VMEM((extent, CHUNKS, LANES), jnp.float32),
                pltpu.VMEM((extent, CHUNKS, LANES), jnp.float32),
                pltpu.VMEM((2 * EDGE, LANES), jnp.float32),
                pltpu.VMEM((deep, LANES), jnp.float32),
                pltpu.SemaphoreType.DMA((8,)),
            ],
            slots * deep * width * 2 * channels,
            slots * deep * width + 8 * first.size * 2,
            (meta, normed, taps, *pieces, *made),
            {8: 0} if made else {},
        )

    swished = convolve(0, normed, first_pieces)
    near_second, hub_second, far_second, swished = lax.optimization_barrier(
        (near_second, hub_second, far_second, swished)
    )
    mine = [second, near_second, hub_second, far_second]
    second_pieces = (*mine, to_mate(jnp.concatenate(mine, axis=0)))
    swished = convolve(1, normed, first_pieces, swished)
    errors = call(
        head_kernel,
        (slots,),
        [by_slot((tile, channels)), by_slot((deep, width)), by_slot((tile, 1)), whole(gains.shape)] + [apart] * 5,
        by_slot((CHUNKS, LANES)),
        jax.ShapeDtypeStruct((slots, CHUNKS, LANES), jnp.float32),
        [
            pltpu.VMEM((8 * conv_out_weight.shape[1], width), jnp.bfloat16),
            pltpu.VMEM((8 * head_rows, vocab), jnp.bfloat16),
            pltpu.SemaphoreType.DMA((8, 1 + groups)),
        ],
        2 * slots * tile * (channels + vocab) * width,
        slots * tile * (channels + width) * 2,
        (meta, swished, stem_out, codes, gains, *second_pieces),
    )

    one, two, three = [seed_swap(errors, bit) for bit in (1, 2, 3)]
    total = ((errors + one) + (two + three)) / jnp.float32(seeds)
    total = total[:, :, : tile // CHUNKS].reshape(2, rows)
    part = jnp.sum(total).reshape(1)
    outer_half = jnp.where(low, total[0], total[1])
    own_half = jnp.where(low, total[1], total[0])
    from_hub = along(jnp.concatenate([outer_half, part]), OUTWARD)
    parts = [part[0], along(part, ACROSS)[0], along(part, OUT_BEYOND)[0], from_hub[rows]]
    frame_error = jnp.where(is_hub, own_half, from_hub[:rows])
    utt_score = ((parts[0] + parts[3]) + (parts[1] + parts[2])) / length.astype(jnp.float32)
    return (frame_error[None, :], utt_score.reshape(1))


def from_behind(x, axis, by):
    count = lax.axis_size(axis)
    pairs = [(i, i + by) for i in range(count) if 0 <= i + by < count]
    return lax.ppermute(x, axis, pairs)


def extended(x, sides, width):
    for axis, dim in sides:
        count, length = (lax.axis_size(axis), x.shape[dim])
        up = [(i, (i + 1) % count) for i in range(count - 1)]
        down = [(j, i) for i, j in up]
        last = lax.slice_in_dim(x, length - width, length, axis=dim)
        first = lax.slice_in_dim(x, 0, width, axis=dim)
        before = lax.ppermute(last, axis, up)
        after = lax.ppermute(first, axis, down)
        x = jnp.concatenate([before, x, after], axis=dim)
    return x


def layer_norm(values, gain_row):
    row_mean = jnp.mean(values, axis=-1, keepdims=True)
    centred = values - row_mean
    row_var = jnp.mean(centred * centred, axis=-1, keepdims=True)
    return (centred * lax.rsqrt(row_var + 1e-05) * gain_row).astype(jnp.bfloat16)


def block_product(left_rows, right_matrix):
    return jnp.dot(left_rows, right_matrix, preferred_element_type=jnp.float32)


def row_product(activations, shard_piece):
    return block_product(activations, shard_piece[0])


def body(
    mel_frames,
    lengths,
    targets,
    frame_mask,
    stem_weight,
    conv_in_weight,
    conv_out_weight,
    depth_weight,
    head_weight,
    norm_gain,
):
    frame_rows = targets.shape[1]
    blocks = mel_frames[0].reshape(frame_rows, -1)
    next_block = from_behind(blocks[:1], "seq", -1)
    following = jnp.concatenate([blocks[1:], next_block], 0)
    half_width = blocks.shape[1]
    stem_matrix = stem_weight[0]
    stem_out = (
        jnp.dot(blocks, stem_matrix[:half_width], preferred_element_type=jnp.float32)
        + jnp.dot(following, stem_matrix[half_width:], preferred_element_type=jnp.float32)
    ).astype(jnp.bfloat16)
    offset = lax.axis_index("seq") * frame_rows
    length = lengths[0]
    positions = offset + jnp.arange(frame_rows, dtype=jnp.int32)
    frame_live = positions < length
    gain_rows = norm_gain[0]
    normed_one = layer_norm(stem_out.astype(jnp.float32), gain_rows[0])
    tap_count = depth_weight.shape[1]
    channels = depth_weight.shape[2]
    halo_width = tap_count // 2
    conv_input = extended(normed_one, (("seq", 0),), halo_width)
    mixed_rows = row_product(
        conv_input, lax.all_gather(conv_in_weight, ("fsdp", "seq"), axis=1, tiled=True)
    )
    input_positions = offset - halo_width + jnp.arange(conv_input.shape[0], dtype=jnp.int32)
    input_live = jnp.logical_and(input_positions >= 0, input_positions < length)
    gated_rows = (
        mixed_rows[:, :channels]
        * jax.nn.sigmoid(mixed_rows[:, channels:])
        * input_live[:, None].astype(jnp.float32)
    ).astype(jnp.bfloat16)
    depthwise = jnp.zeros((frame_rows, channels), jnp.float32)
    for tap_index in range(tap_count):
        depthwise = depthwise + gated_rows[tap_index : tap_index + frame_rows].astype(
            jnp.float32
        ) * depth_weight[0, tap_index].astype(jnp.float32)
    swished = jax.nn.silu(depthwise).astype(jnp.bfloat16)
    conv_proj = row_product(
        swished, lax.all_gather(conv_out_weight, ("fsdp", "seq"), axis=1, tiled=True)
    )
    after_conv = stem_out.astype(jnp.float32) + conv_proj
    normed_two = layer_norm(after_conv, gain_rows[1])
    logits = row_product(
        normed_two, lax.all_gather(head_weight, ("fsdp", "seq"), axis=1, tiled=True)
    )
    posterior = jax.nn.softmax(logits, axis=-1)
    vocab_size = logits.shape[1]
    onehot = (jnp.arange(vocab_size, dtype=jnp.int32)[None, :] == targets[0][:, None]).astype(
        jnp.float32
    )
    differ = posterior - onehot
    frame_err = (
        jnp.sqrt(jnp.sum(differ * differ, axis=-1))
        * frame_live.astype(jnp.float32)
        * frame_mask[0].astype(jnp.float32)
    )
    seed_count = lax.axis_size("seed")
    frame_error = lax.psum(frame_err, "seed") / jnp.float32(seed_count)
    numerator = lax.psum(jnp.sum(frame_error), "seq")
    utt_score = numerator / length.astype(jnp.float32)
    return (frame_error[None, :], utt_score.reshape(1))


def solution(mesh):
    in_specs = (
        P("fsdp", "seq", None),
        P("fsdp"),
        P("fsdp", "seq"),
        P("fsdp", "seq"),
        P("seed", None, None),
        P("seed", ("fsdp", "seq"), None),
        P("seed", ("fsdp", "seq"), None),
        P("seed", None, None),
        P("seed", ("fsdp", "seq"), None),
        P("seed", None, None),
    )
    out_specs = (P("fsdp", "seq"), P("fsdp"))
    hubs = mesh.shape["seq"] == 4 and mesh.shape["fsdp"] == 2
    return jax.shard_map(
        hub_body if hubs else body, mesh=mesh, in_specs=in_specs, out_specs=out_specs, check_vma=False
    )
```

```python
import functools

import jax
import jax.numpy as jnp
from jax import lax
from jax.experimental import pallas as pl
from jax.experimental.pallas import tpu as pltpu
from jax.sharding import PartitionSpec as P

LANES = 128
CHUNKS = 8
EDGE = 16
VMEM_BYTES = 24 * 1024 * 1024


def norm_rows(values, gain_row):
    row_mean = jnp.mean(values, axis=-1, keepdims=True)
    centred = values - row_mean
    row_var = jnp.mean(centred * centred, axis=-1, keepdims=True)
    return (centred * lax.rsqrt(row_var + 1e-05) * gain_row).astype(jnp.bfloat16)


def sigmoid(x):
    return 0.5 * jnp.tanh(0.5 * x) + 0.5


def stem_kernel(first_slot, meta, main_ref, margin_ref, stem_ref, gain_ref, *rest):
    stem_out_ref, normed_ref, acc_a, acc_b, acc_c = rest[-5:]
    slot = pl.program_id(0) + first_slot
    frames = main_ref.shape[1]
    part = acc_a.shape[0]
    group = 16

    def norm(acc, at, keep):
        for row in range(0, acc.shape[0], group):
            stem_out = acc[row : row + group, :].astype(jnp.bfloat16)
            if keep:
                stem_out_ref[0, at + row : at + row + group, :] = stem_out
            normed_ref[0, at + row : at + row + group, :] = norm_rows(stem_out.astype(jnp.float32), gain_ref[0:1, :])

    @pl.when(meta[5 + slot] > 0)
    def _():
        for acc, at in ((acc_a, 0), (acc_b, part)):
            acc[...] = jnp.dot(main_ref[0, at : at + part, :], stem_ref[...], preferred_element_type=jnp.float32)
        norm(acc_a, 0, True)
        acc_c[...] = jnp.dot(margin_ref[0], stem_ref[...], preferred_element_type=jnp.float32)
        norm(acc_b, part, True)
        norm(acc_c, frames, False)


def shards(meta, pieces):
    side = meta[13]
    length = pieces[0].shape[0]
    mine = [(pieces[i], 0, side * 4 + meta[9 + i]) for i in range(4)]
    return mine + [(pieces[4], i * length, (1 - side) * 4 + meta[9 + i]) for i in range(4)]


def conv_kernel(first_slot, meta, normed_ref, taps_ref, *rest):
    pieces = rest[:5]
    swished_ref, weight, mixed_a, mixed_b, gated, margin, mask, sems = rest[-8:]
    slot = pl.program_id(0) + first_slot
    rows = normed_ref.shape[1]
    frames = swished_ref.shape[1]
    channels = swished_ref.shape[2]
    tap_count = taps_ref.shape[0]
    reach = tap_count // 2
    piece = pieces[0].shape[0]
    run_length = frames // CHUNKS

    @pl.when(jnp.logical_and(pl.program_id(0) == 0, meta[14] > 0))
    def _():
        copies = [
            pltpu.make_async_copy(
                ref.at[pl.ds(at, piece)], weight.at[pl.ds(pl.multiple_of(block * piece, 16), piece)], sems.at[i]
            )
            for i, (ref, at, block) in enumerate(shards(meta, pieces))
        ]
        for copy in copies:
            copy.start()
        for copy in copies:
            copy.wait()

    @pl.when(meta[5 + slot] > 0)
    def _():
        row = lax.broadcasted_iota(jnp.int32, (rows, LANES), 0)
        inner = (row % CHUNKS) * run_length + row // CHUNKS
        outer = jnp.where(row < frames + EDGE, row - frames - EDGE, row - EDGE)
        at = meta[slot] + jnp.where(row < frames, inner, outer)
        mask[...] = jnp.logical_and(at >= 0, at < meta[4]).astype(jnp.float32)
        sublane = lax.broadcasted_iota(jnp.int32, (CHUNKS, LANES), 0)
        buffers = (mixed_a, mixed_b)

        def mix(block):
            low = block * LANES
            right = jnp.concatenate(
                [weight[:, low : low + LANES], weight[:, channels + low : channels + low + LANES]], axis=1
            )
            buffers[block % 2][...] = jnp.dot(normed_ref[0], right, preferred_element_type=jnp.float32)

        def gate(block):
            mixed = buffers[block % 2]
            group = 32
            for at in range(0, rows, group):
                here = slice(at, at + group)
                made = mixed[here, :LANES] * sigmoid(mixed[here, LANES:]) * mask[here, :]
                made = made.astype(jnp.bfloat16).astype(jnp.float32)
                if at < frames:
                    first = reach + at // CHUNKS
                    gated[first : first + group // CHUNKS] = made.reshape(group // CHUNKS, CHUNKS, LANES)
                else:
                    margin[...] = made
            for i in range(reach):
                before = pltpu.roll(gated[run_length + i], 1, 0)
                edge = margin[EDGE - reach + i : EDGE - reach + i + 1, :]
                gated[i] = jnp.where(sublane == 0, edge, before)
                after = pltpu.roll(gated[reach + i], CHUNKS - 1, 0)
                edge = margin[EDGE + i : EDGE + i + 1, :]
                gated[reach + run_length + i] = jnp.where(sublane == CHUNKS - 1, edge, after)

        def convolve(block):
            low = block * LANES
            run = 16
            for start in range(0, run_length, run):
                sums = [None] * run
                for at in range(start, start + run + tap_count - 1):
                    value = gated[at]
                    for m in range(max(start, at - tap_count + 1), min(start + run, at + 1)):
                        term = value * taps_ref[at - m, :, low : low + LANES]
                        k = m - start
                        sums[k] = term if sums[k] is None else sums[k] + term
                for k in range(0, run, 2):
                    total = jnp.concatenate(sums[k : k + 2], axis=0)
                    first = (start + k) * CHUNKS
                    swished_ref[0, first : first + 2 * CHUNKS, low : low + LANES] = (
                        total * sigmoid(total)
                    ).astype(jnp.bfloat16)

        blocks = channels // LANES
        mix(0)
        for block in range(blocks):
            if block + 1 < blocks:
                mix(block + 1)
            gate(block)
            convolve(block)


def head_kernel(meta, swished_ref, stem_out_ref, code_ref, gain_ref, *rest):
    pieces = rest[:5]
    error_ref, back, head, acc_a, acc_b, norm_a, norm_b, logit_a, logit_b, sems = rest[5:]
    slot = pl.program_id(0)
    frames = swished_ref.shape[1]
    vocab = head.shape[1]
    groups = back.shape[1] // vocab
    back_rows = back.shape[0] // 8
    head_rows = head.shape[0] // 8
    group_rows = head_rows // groups

    @pl.when(jnp.logical_and(pl.program_id(0) == 0, meta[14] > 0))
    def _():
        copies = []
        for i, (ref, at, block) in enumerate(shards(meta, pieces)):
            copies.append(
                pltpu.make_async_copy(
                    ref.at[pl.ds(at, back_rows)],
                    back.at[pl.ds(pl.multiple_of(block * back_rows, 16), back_rows)],
                    sems.at[i, 0],
                )
            )
            for g in range(groups):
                copies.append(
                    pltpu.make_async_copy(
                        ref.at[pl.ds(at + back_rows, group_rows), pl.ds(g * vocab, vocab)],
                        head.at[pl.ds(pl.multiple_of(block * head_rows + g * group_rows, 16), group_rows)],
                        sems.at[i, 1 + g],
                    )
                )
        for copy in copies:
            copy.start()
        for copy in copies:
            copy.wait()

    @pl.when(meta[5 + slot] <= 0)
    def _():
        error_ref[...] = jnp.zeros_like(error_ref)

    @pl.when(meta[5 + slot] > 0)
    def _():
        part = acc_a.shape[0]
        lane = lax.broadcasted_iota(jnp.int32, (CHUNKS, LANES), 1)
        halves = ((0, acc_a, norm_a, logit_a), (part, acc_b, norm_b, logit_b))

        def norm(at, acc, normed):
            group = 16
            for row in range(0, part, group):
                values = acc[row : row + group, :] + stem_out_ref[0, at + row : at + row + group, :].astype(jnp.float32)
                normed[row : row + group, :] = norm_rows(values, gain_ref[1:2, :])

        def errors(at, logits):
            group = 32
            token = lax.broadcasted_iota(jnp.int32, (group, vocab), 1)
            row = jnp.zeros((CHUNKS, LANES), jnp.float32)
            for first in range(0, part, group):
                scores = logits[first : first + group, :]
                grown = jnp.exp(scores - jnp.max(scores, axis=-1, keepdims=True))
                posterior = grown * (1.0 / jnp.sum(grown, axis=-1, keepdims=True))
                code = code_ref[0, at + first : at + first + group, :]
                differ = posterior - (token == code).astype(jnp.float32)
                error = jnp.sqrt(jnp.sum(differ * differ, axis=-1, keepdims=True))
                error = jnp.where(code >= 0, error, 0.0)
                for m in range(group // CHUNKS):
                    step = error[m * CHUNKS : (m + 1) * CHUNKS, :]
                    row = row + jnp.where(lane == (at + first) // CHUNKS + m, step, 0.0)
            return row

        for at, acc, _, _ in halves:
            acc[...] = jnp.dot(swished_ref[0, at : at + part, :], back[...], preferred_element_type=jnp.float32)
        for at, acc, normed, logits in halves:
            norm(at, acc, normed)
            logits[...] = jnp.dot(normed[...], head[...], preferred_element_type=jnp.float32)
        error_ref[0] = errors(0, logit_a) + errors(part, logit_b)


def call(kernel, grid, in_specs, out_specs, out_shape, scratch, flops, moved, operands, aliases={}):
    return pl.pallas_call(
        kernel,
        grid_spec=pltpu.PrefetchScalarGridSpec(
            num_scalar_prefetch=1,
            grid=grid,
            in_specs=in_specs,
            out_specs=out_specs,
            scratch_shapes=scratch,
        ),
        out_shape=out_shape,
        input_output_aliases=aliases,
        compiler_params=pltpu.CompilerParams(
            dimension_semantics=("arbitrary",), vmem_limit_bytes=VMEM_BYTES
        ),
        cost_estimate=pl.CostEstimate(flops=flops // 16, bytes_accessed=moved // 16, transcendentals=0),
    )(*operands)


def whole(shape):
    return pl.BlockSpec(shape, lambda i, meta: (0,) * len(shape))


def by_slot(shape, first=0):
    return pl.BlockSpec((1,) + shape, lambda i, meta: (i + first,) + (0,) * len(shape))


INWARD = [(0, 1), (3, 2)]
ACROSS = [(1, 2), (2, 1)]
BEYOND = [(0, 2), (3, 1)]
OUTWARD = [(1, 0), (2, 3)]
FORWARD = [(0, 1), (1, 2), (2, 3)]
BACKWARD = [(1, 0), (2, 1), (3, 2)]
OUT_BEYOND = [(2, 0), (1, 3)]


def along(x, pairs):
    return lax.ppermute(x, "seq", pairs)


def to_mate(x):
    pairs = [(a * 4 + z, (1 - a) * 4 + z) for a in (0, 1) for z in (1, 2)]
    return lax.ppermute(x, ("fsdp", "seq"), pairs)


def seed_swap(x, bit):
    return lax.ppermute(x, "seed", [(i, i ^ bit) for i in range(4)])


def hub_body(
    mel_frames,
    lengths,
    targets,
    frame_mask,
    stem_weight,
    conv_in_weight,
    conv_out_weight,
    depth_weight,
    head_weight,
    norm_gain,
):
    chip = lax.axis_index("seq")
    side = lax.axis_index("fsdp")
    seeds = lax.axis_size("seed")
    rows = targets.shape[1]
    width = stem_weight.shape[2]
    channels = depth_weight.shape[2]
    vocab = head_weight.shape[2]
    step = mel_frames.shape[1] // rows
    tile = rows // 2
    low = chip == 1
    is_hub = jnp.logical_or(low, chip == 2)

    first = conv_in_weight[0]
    near_first = along(first, INWARD)
    hub_first = along(first, ACROSS)
    margin = step * EDGE
    before = along(mel_frames[0, -margin:].reshape(EDGE, -1), FORWARD)
    after = along(mel_frames[0, :margin].reshape(EDGE, -1), BACKWARD)
    blocks = mel_frames[0].reshape(rows, -1)
    outer = along(blocks, INWARD)
    far_first = along(near_first, ACROSS)

    groups = width // vocab
    head_rows = head_weight.shape[1]
    second = jnp.concatenate(
        [
            conv_out_weight[0],
            jnp.concatenate(jnp.split(head_weight[0], groups, axis=0), axis=1),
        ],
        axis=0,
    )
    second_held, before, after, hub_first = lax.optimization_barrier((second, before, after, hub_first))
    near_second = along(second_held, INWARD)
    far_second = along(second_held, BEYOND)

    slots = 4
    deep = tile + 2 * EDGE

    def paired(before, block, after):
        frames = jnp.concatenate([before, block, after, after[:1]], axis=0)
        pairs = jnp.concatenate([frames[:-1], frames[1:]], axis=1)
        main = pairs[EDGE : EDGE + 2 * tile].reshape(2, CHUNKS, tile // CHUNKS, -1)
        main = main.transpose(0, 2, 1, 3).reshape(2, tile, -1)
        sides = [
            jnp.concatenate([pairs[k * tile : k * tile + EDGE], pairs[(k + 1) * tile + EDGE : (k + 1) * tile + 2 * EDGE]])
            for k in range(2)
        ]
        return main, jnp.stack(sides)

    length = lengths[0]
    positions = chip * rows + jnp.arange(rows, dtype=jnp.int32)
    counted = jnp.logical_and(frame_mask[0] > 0, positions < length)
    code = jnp.where(counted, targets[0], -1)
    lone = jnp.where(low, 0, 3)
    starts = jnp.stack([chip * rows, chip * rows + tile, lone * rows, lone * rows + tile]).astype(jnp.int32)
    alive = jnp.logical_and(is_hub, starts < length).astype(jnp.int32)
    hub = jnp.clip(chip, 1, 2)
    meta = jnp.concatenate(
        [
            starts,
            lengths,
            alive,
            jnp.stack([hub, 3 * (hub - 1), 3 - hub, 3 * (2 - hub), side, jnp.max(alive)]),
        ]
    ).astype(jnp.int32)

    gains = norm_gain[0]
    def stems(part, main, sides, *made):
        half = tile // 2
        return call(
            functools.partial(stem_kernel, 2 * part),
            (2,),
            [by_slot(main.shape[1:]), by_slot(sides.shape[1:]), whole(stem_weight.shape[1:]), whole(gains.shape)]
            + [apart] * len(made),
            [by_slot((tile, width), 2 * part), by_slot((deep, width))],
            [
                jax.ShapeDtypeStruct((slots, tile, width), jnp.bfloat16),
                jax.ShapeDtypeStruct((2, deep, width), jnp.bfloat16),
            ],
            [
                pltpu.VMEM((half, width), jnp.float32),
                pltpu.VMEM((half, width), jnp.float32),
                pltpu.VMEM((2 * EDGE, width), jnp.float32),
            ],
            slots * deep * main.shape[2] * width,
            slots * deep * (main.shape[2] + 2 * width),
            (meta, main, sides, stem_weight[0], gains, *made),
            {5: 0} if made else {},
        )

    apart = pl.BlockSpec(memory_space=pl.ANY)
    stem_out, own_normed = stems(0, *paired(before, blocks, after))

    near_first, far_first, outer, own_normed = lax.optimization_barrier((near_first, far_first, outer, own_normed))
    mine = [first, near_first, hub_first, far_first]
    first_pieces = (*mine, to_mate(jnp.concatenate(mine, axis=0)))
    second_late, _ = lax.optimization_barrier((second, outer))
    hub_second = along(second_late, ACROSS)

    none = jnp.zeros_like(before)
    outer_before = jnp.where(low, none, blocks[-EDGE:])
    outer_after = jnp.where(low, blocks[:EDGE], none)
    stem_out, outer_normed = stems(1, *paired(outer_before, outer, outer_after), stem_out)

    code_held, _ = lax.optimization_barrier((code, first_pieces[-1]))
    outer_code = along(code_held, INWARD)
    codes = jnp.concatenate([code, outer_code])
    codes = codes.reshape(slots, CHUNKS, tile // CHUNKS).transpose(0, 2, 1).reshape(slots, tile, 1)

    taps = jnp.broadcast_to(
        depth_weight[0].astype(jnp.float32)[:, None, :], (depth_weight.shape[1], CHUNKS, channels)
    )
    extent = tile // CHUNKS + depth_weight.shape[1] - 1
    def convolve(part, normed, pieces, *made):
        return call(
            functools.partial(conv_kernel, 2 * part),
            (2,),
            [by_slot((deep, width)), whole(taps.shape)] + [apart] * (5 + len(made)),
            by_slot((tile, channels), 2 * part),
            jax.ShapeDtypeStruct((slots, tile, channels), jnp.bfloat16),
            [
                pltpu.VMEM((8 * first.shape[0], first.shape[1]), jnp.bfloat16),
                pltpu.VMEM((deep, 2 * LANES), jnp.float32),
                pltpu.VMEM((deep, 2 * LANES), jnp.float32),
                pltpu.VMEM((extent, CHUNKS, LANES), jnp.float32),
                pltpu.VMEM((2 * EDGE, LANES), jnp.float32),
                pltpu.VMEM((deep, LANES), jnp.float32),
                pltpu.SemaphoreType.DMA((8,)),
            ],
            slots * deep * width * 2 * channels,
            slots * deep * width + 8 * first.size * 2,
            (meta, normed, taps, *pieces, *made),
            {8: 0} if made else {},
        )

    swished = convolve(0, own_normed, first_pieces)
    near_second, hub_second, far_second, swished, outer_normed = lax.optimization_barrier(
        (near_second, hub_second, far_second, swished, outer_normed)
    )
    mine = [second, near_second, hub_second, far_second]
    second_pieces = (*mine, to_mate(jnp.concatenate(mine, axis=0)))
    swished = convolve(1, outer_normed, first_pieces, swished)
    errors = call(
        head_kernel,
        (slots,),
        [by_slot((tile, channels)), by_slot((tile, width)), by_slot((tile, 1)), whole(gains.shape)] + [apart] * 5,
        by_slot((CHUNKS, LANES)),
        jax.ShapeDtypeStruct((slots, CHUNKS, LANES), jnp.float32),
        [
            pltpu.VMEM((8 * conv_out_weight.shape[1], width), jnp.bfloat16),
            pltpu.VMEM((8 * head_rows, vocab), jnp.bfloat16),
            pltpu.VMEM((tile // 2, width), jnp.float32),
            pltpu.VMEM((tile // 2, width), jnp.float32),
            pltpu.VMEM((tile // 2, width), jnp.bfloat16),
            pltpu.VMEM((tile // 2, width), jnp.bfloat16),
            pltpu.VMEM((tile // 2, vocab), jnp.float32),
            pltpu.VMEM((tile // 2, vocab), jnp.float32),
            pltpu.SemaphoreType.DMA((8, 1 + groups)),
        ],
        2 * slots * tile * (channels + vocab) * width,
        slots * tile * (channels + width) * 2,
        (meta, swished, stem_out, codes, gains, *second_pieces),
    )

    one, two, three = [seed_swap(errors, bit) for bit in (1, 2, 3)]
    total = ((errors + one) + (two + three)) / jnp.float32(seeds)
    total = total[:, :, : tile // CHUNKS].reshape(2, rows)
    part = jnp.sum(total).reshape(1)
    own_half, outer_half = total
    from_hub = along(jnp.concatenate([outer_half, part]), OUTWARD)
    parts = [part[0], along(part, ACROSS)[0], along(part, OUT_BEYOND)[0], from_hub[rows]]
    frame_error = jnp.where(is_hub, own_half, from_hub[:rows])
    utt_score = ((parts[0] + parts[3]) + (parts[1] + parts[2])) / length.astype(jnp.float32)
    return (frame_error[None, :], utt_score.reshape(1))


def from_behind(x, axis, by):
    count = lax.axis_size(axis)
    pairs = [(i, i + by) for i in range(count) if 0 <= i + by < count]
    return lax.ppermute(x, axis, pairs)


def extended(x, sides, width):
    for axis, dim in sides:
        count, length = (lax.axis_size(axis), x.shape[dim])
        up = [(i, (i + 1) % count) for i in range(count - 1)]
        down = [(j, i) for i, j in up]
        last = lax.slice_in_dim(x, length - width, length, axis=dim)
        first = lax.slice_in_dim(x, 0, width, axis=dim)
        before = lax.ppermute(last, axis, up)
        after = lax.ppermute(first, axis, down)
        x = jnp.concatenate([before, x, after], axis=dim)
    return x


def layer_norm(values, gain_row):
    row_mean = jnp.mean(values, axis=-1, keepdims=True)
    centred = values - row_mean
    row_var = jnp.mean(centred * centred, axis=-1, keepdims=True)
    return (centred * lax.rsqrt(row_var + 1e-05) * gain_row).astype(jnp.bfloat16)


def block_product(left_rows, right_matrix):
    return jnp.dot(left_rows, right_matrix, preferred_element_type=jnp.float32)


def row_product(activations, shard_piece):
    return block_product(activations, shard_piece[0])


def body(
    mel_frames,
    lengths,
    targets,
    frame_mask,
    stem_weight,
    conv_in_weight,
    conv_out_weight,
    depth_weight,
    head_weight,
    norm_gain,
):
    frame_rows = targets.shape[1]
    blocks = mel_frames[0].reshape(frame_rows, -1)
    next_block = from_behind(blocks[:1], "seq", -1)
    following = jnp.concatenate([blocks[1:], next_block], 0)
    half_width = blocks.shape[1]
    stem_matrix = stem_weight[0]
    stem_out = (
        jnp.dot(blocks, stem_matrix[:half_width], preferred_element_type=jnp.float32)
        + jnp.dot(following, stem_matrix[half_width:], preferred_element_type=jnp.float32)
    ).astype(jnp.bfloat16)
    offset = lax.axis_index("seq") * frame_rows
    length = lengths[0]
    positions = offset + jnp.arange(frame_rows, dtype=jnp.int32)
    frame_live = positions < length
    gain_rows = norm_gain[0]
    normed_one = layer_norm(stem_out.astype(jnp.float32), gain_rows[0])
    tap_count = depth_weight.shape[1]
    channels = depth_weight.shape[2]
    halo_width = tap_count // 2
    conv_input = extended(normed_one, (("seq", 0),), halo_width)
    mixed_rows = row_product(
        conv_input, lax.all_gather(conv_in_weight, ("fsdp", "seq"), axis=1, tiled=True)
    )
    input_positions = offset - halo_width + jnp.arange(conv_input.shape[0], dtype=jnp.int32)
    input_live = jnp.logical_and(input_positions >= 0, input_positions < length)
    gated_rows = (
        mixed_rows[:, :channels]
        * jax.nn.sigmoid(mixed_rows[:, channels:])
        * input_live[:, None].astype(jnp.float32)
    ).astype(jnp.bfloat16)
    depthwise = jnp.zeros((frame_rows, channels), jnp.float32)
    for tap_index in range(tap_count):
        depthwise = depthwise + gated_rows[tap_index : tap_index + frame_rows].astype(
            jnp.float32
        ) * depth_weight[0, tap_index].astype(jnp.float32)
    swished = jax.nn.silu(depthwise).astype(jnp.bfloat16)
    conv_proj = row_product(
        swished, lax.all_gather(conv_out_weight, ("fsdp", "seq"), axis=1, tiled=True)
    )
    after_conv = stem_out.astype(jnp.float32) + conv_proj
    normed_two = layer_norm(after_conv, gain_rows[1])
    logits = row_product(
        normed_two, lax.all_gather(head_weight, ("fsdp", "seq"), axis=1, tiled=True)
    )
    posterior = jax.nn.softmax(logits, axis=-1)
    vocab_size = logits.shape[1]
    onehot = (jnp.arange(vocab_size, dtype=jnp.int32)[None, :] == targets[0][:, None]).astype(
        jnp.float32
    )
    differ = posterior - onehot
    frame_err = (
        jnp.sqrt(jnp.sum(differ * differ, axis=-1))
        * frame_live.astype(jnp.float32)
        * frame_mask[0].astype(jnp.float32)
    )
    seed_count = lax.axis_size("seed")
    frame_error = lax.psum(frame_err, "seed") / jnp.float32(seed_count)
    numerator = lax.psum(jnp.sum(frame_error), "seq")
    utt_score = numerator / length.astype(jnp.float32)
    return (frame_error[None, :], utt_score.reshape(1))


def solution(mesh):
    in_specs = (
        P("fsdp", "seq", None),
        P("fsdp"),
        P("fsdp", "seq"),
        P("fsdp", "seq"),
        P("seed", None, None),
        P("seed", ("fsdp", "seq"), None),
        P("seed", ("fsdp", "seq"), None),
        P("seed", None, None),
        P("seed", ("fsdp", "seq"), None),
        P("seed", None, None),
    )
    out_specs = (P("fsdp", "seq"), P("fsdp"))
    hubs = mesh.shape["seq"] == 4 and mesh.shape["fsdp"] == 2
    return jax.shard_map(
        hub_body if hubs else body, mesh=mesh, in_specs=in_specs, out_specs=out_specs, check_vma=False
    )
```

```python
import functools

import jax
import jax.numpy as jnp
from jax import lax
from jax.experimental import pallas as pl
from jax.experimental.pallas import tpu as pltpu
from jax.sharding import PartitionSpec as P

LANES = 128
CHUNKS = 8
EDGE = 16
VMEM_BYTES = 24 * 1024 * 1024


def norm_rows(values, gain_row):
    row_mean = jnp.mean(values, axis=-1, keepdims=True)
    centred = values - row_mean
    row_var = jnp.mean(centred * centred, axis=-1, keepdims=True)
    return (centred * lax.rsqrt(row_var + 1e-05) * gain_row).astype(jnp.bfloat16)


def sigmoid(x):
    return 0.5 * jnp.tanh(0.5 * x) + 0.5


def weave(*tracks):
    steps = [((i + 0.5) / len(track), k, step) for k, track in enumerate(tracks) for i, step in enumerate(track)]
    for _, _, step in sorted(steps, key=lambda entry: entry[:2]):
        step()


def column_steps(left, right, into, block):
    def step(at):
        into[:, at : at + block] = jnp.dot(left(), right[:, at : at + block], preferred_element_type=jnp.float32)

    return [functools.partial(step, at) for at in range(0, right.shape[1], block)]


def stem_kernel(first_slot, meta, main_ref, margin_ref, stem_ref, gain_ref, *rest):
    stem_out_ref, normed_ref, acc_a, acc_b, acc_c = rest[-5:]
    slot = pl.program_id(0) + first_slot
    frames = main_ref.shape[1]
    part = acc_a.shape[0]
    group = 16

    def norm_step(acc, at, keep, row):
        stem_out = acc[row : row + group, :].astype(jnp.bfloat16)
        if keep:
            stem_out_ref[0, at + row : at + row + group, :] = stem_out
        normed_ref[0, at + row : at + row + group, :] = norm_rows(stem_out.astype(jnp.float32), gain_ref[0:1, :])

    def norm(acc, at, keep):
        return [functools.partial(norm_step, acc, at, keep, row) for row in range(0, acc.shape[0], group)]

    @pl.when(meta[5 + slot] > 0)
    def _():
        block = 2 * LANES
        weave(column_steps(lambda: main_ref[0, :part, :], stem_ref, acc_a, block))
        weave(column_steps(lambda: main_ref[0, part:, :], stem_ref, acc_b, block), norm(acc_a, 0, True))
        weave(column_steps(lambda: margin_ref[0], stem_ref, acc_c, block), norm(acc_b, part, True))
        weave(norm(acc_c, frames, False))


def shards(meta, pieces):
    side = meta[13]
    return [(pieces[i], (side if i < 4 else 1 - side) * 4 + meta[9 + i % 4]) for i in range(8)]


def conv_kernel(first_slot, meta, normed_ref, taps_ref, *rest):
    pieces = rest[:8]
    swished_ref, weight, mixed_a, mixed_b, gated, margin, mask, sems = rest[-8:]
    slot = pl.program_id(0) + first_slot
    rows = normed_ref.shape[1]
    frames = swished_ref.shape[1]
    channels = swished_ref.shape[2]
    tap_count = taps_ref.shape[0]
    reach = tap_count // 2
    piece = pieces[0].shape[0]
    run_length = frames // CHUNKS

    @pl.when(jnp.logical_and(pl.program_id(0) == 0, meta[14] > 0))
    def _():
        copies = [
            pltpu.make_async_copy(
                ref, weight.at[pl.ds(pl.multiple_of(block * piece, 16), piece)], sems.at[i]
            )
            for i, (ref, block) in enumerate(shards(meta, pieces))
        ]
        for copy in copies:
            copy.start()
        for copy in copies:
            copy.wait()

    @pl.when(meta[5 + slot] > 0)
    def _():
        row = lax.broadcasted_iota(jnp.int32, (rows, LANES), 0)
        inner = (row % CHUNKS) * run_length + row // CHUNKS
        outer = jnp.where(row < frames + EDGE, row - frames - EDGE, row - EDGE)
        at = meta[slot] + jnp.where(row < frames, inner, outer)
        mask[...] = jnp.logical_and(at >= 0, at < meta[4]).astype(jnp.float32)
        sublane = lax.broadcasted_iota(jnp.int32, (CHUNKS, LANES), 0)
        buffers = (mixed_a, mixed_b)

        def mix(block):
            low = block * LANES
            half = rows // 2

            def step(at):
                right = jnp.concatenate(
                    [weight[:, low : low + LANES], weight[:, channels + low : channels + low + LANES]], axis=1
                )
                buffers[block % 2][at : at + half, :] = jnp.dot(
                    normed_ref[0, at : at + half, :], right, preferred_element_type=jnp.float32
                )

            return [functools.partial(step, at) for at in (0, half)]

        def gate(block):
            mixed = buffers[block % 2]
            group = 32

            def step(at):
                here = slice(at, at + group)
                made = mixed[here, :LANES] * sigmoid(mixed[here, LANES:]) * mask[here, :]
                made = made.astype(jnp.bfloat16).astype(jnp.float32)
                if at < frames:
                    first = reach + at // CHUNKS
                    gated[first : first + group // CHUNKS] = made.reshape(group // CHUNKS, CHUNKS, LANES)
                else:
                    margin[...] = made

            def sides(i):
                before = pltpu.roll(gated[run_length + i], 1, 0)
                edge = margin[EDGE - reach + i : EDGE - reach + i + 1, :]
                gated[i] = jnp.where(sublane == 0, edge, before)
                after = pltpu.roll(gated[reach + i], CHUNKS - 1, 0)
                edge = margin[EDGE + i : EDGE + i + 1, :]
                gated[reach + run_length + i] = jnp.where(sublane == CHUNKS - 1, edge, after)

            return [functools.partial(step, at) for at in range(0, rows, group)] + [
                functools.partial(sides, i) for i in range(reach)
            ]

        def convolve(block):
            low = block * LANES
            run = 16

            def step(start):
                sums = [None] * run
                for at in range(start, start + run + tap_count - 1):
                    value = gated[at]
                    for m in range(max(start, at - tap_count + 1), min(start + run, at + 1)):
                        term = value * taps_ref[at - m, :, low : low + LANES]
                        k = m - start
                        sums[k] = term if sums[k] is None else sums[k] + term
                for k in range(0, run, 2):
                    total = jnp.concatenate(sums[k : k + 2], axis=0)
                    first = (start + k) * CHUNKS
                    swished_ref[0, first : first + 2 * CHUNKS, low : low + LANES] = (
                        total * sigmoid(total)
                    ).astype(jnp.bfloat16)

            return [functools.partial(step, start) for start in range(0, run_length, run)]

        blocks = channels // LANES
        weave(mix(0))
        for block in range(blocks):
            weave(gate(block) + convolve(block), mix(block + 1) if block + 1 < blocks else [])


def head_kernel(meta, swished_ref, stem_out_ref, code_ref, gain_ref, *rest):
    pieces = rest[:8]
    error_ref, back, head, acc_a, acc_b, norm_a, norm_b, logit_a, logit_b, sems = rest[8:]
    slot = pl.program_id(0)
    frames = swished_ref.shape[1]
    vocab = head.shape[1]
    groups = back.shape[1] // vocab
    back_rows = back.shape[0] // 8
    head_rows = head.shape[0] // 8
    group_rows = head_rows // groups

    @pl.when(jnp.logical_and(pl.program_id(0) == 0, meta[14] > 0))
    def _():
        copies = []
        for i, (ref, block) in enumerate(shards(meta, pieces)):
            copies.append(
                pltpu.make_async_copy(
                    ref.at[pl.ds(0, back_rows)],
                    back.at[pl.ds(pl.multiple_of(block * back_rows, 16), back_rows)],
                    sems.at[i, 0],
                )
            )
            for g in range(groups):
                copies.append(
                    pltpu.make_async_copy(
                        ref.at[pl.ds(back_rows, group_rows), pl.ds(g * vocab, vocab)],
                        head.at[pl.ds(pl.multiple_of(block * head_rows + g * group_rows, 16), group_rows)],
                        sems.at[i, 1 + g],
                    )
                )
        for copy in copies:
            copy.start()
        for copy in copies:
            copy.wait()

    @pl.when(meta[5 + slot] <= 0)
    def _():
        error_ref[...] = jnp.zeros_like(error_ref)

    @pl.when(meta[5 + slot] > 0)
    def _():
        part = acc_a.shape[0]
        lane = lax.broadcasted_iota(jnp.int32, (CHUNKS, LANES), 1)
        error_ref[...] = jnp.zeros_like(error_ref)

        def norm(at, acc, normed):
            group = 16

            def step(row):
                values = acc[row : row + group, :] + stem_out_ref[0, at + row : at + row + group, :].astype(jnp.float32)
                normed[row : row + group, :] = norm_rows(values, gain_ref[1:2, :])

            return [functools.partial(step, row) for row in range(0, part, group)]

        def errors(at, logits):
            group = 32
            token = lax.broadcasted_iota(jnp.int32, (group, vocab), 1)

            def step(first):
                scores = logits[first : first + group, :]
                grown = jnp.exp(scores - jnp.max(scores, axis=-1, keepdims=True))
                posterior = grown * (1.0 / jnp.sum(grown, axis=-1, keepdims=True))
                steps = range((at + first) // CHUNKS, (at + first + group) // CHUNKS)
                code = jnp.concatenate([code_ref[0, :, m : m + 1] for m in steps], axis=0)
                differ = posterior - (token == code).astype(jnp.float32)
                error = jnp.sqrt(jnp.sum(differ * differ, axis=-1, keepdims=True))
                error = jnp.where(code >= 0, error, 0.0)
                row = error_ref[0]
                for k, m in enumerate(steps):
                    row = jnp.where(lane == m, error[k * CHUNKS : (k + 1) * CHUNKS, :], row)
                error_ref[0] = row

            return [functools.partial(step, first) for first in range(0, part, group)]

        block = 2 * LANES
        weave(column_steps(lambda: swished_ref[0, :part, :], back, acc_a, block))
        weave(column_steps(lambda: swished_ref[0, part:, :], back, acc_b, block), norm(0, acc_a, norm_a))
        weave(column_steps(lambda: norm_a[...], head, logit_a, block), norm(part, acc_b, norm_b))
        weave(column_steps(lambda: norm_b[...], head, logit_b, block), errors(0, logit_a))
        weave(errors(part, logit_b))


def call(kernel, grid, in_specs, out_specs, out_shape, scratch, flops, moved, operands, aliases={}):
    return pl.pallas_call(
        kernel,
        grid_spec=pltpu.PrefetchScalarGridSpec(
            num_scalar_prefetch=1,
            grid=grid,
            in_specs=in_specs,
            out_specs=out_specs,
            scratch_shapes=scratch,
        ),
        out_shape=out_shape,
        input_output_aliases=aliases,
        compiler_params=pltpu.CompilerParams(
            dimension_semantics=("arbitrary",), vmem_limit_bytes=VMEM_BYTES
        ),
        cost_estimate=pl.CostEstimate(flops=flops // 16, bytes_accessed=moved // 16, transcendentals=0),
    )(*operands)


def whole(shape):
    return pl.BlockSpec(shape, lambda i, meta: (0,) * len(shape))


def by_slot(shape, first=0):
    return pl.BlockSpec((1,) + shape, lambda i, meta: (i + first,) + (0,) * len(shape))


INWARD = [(0, 1), (3, 2)]
ACROSS = [(1, 2), (2, 1)]
BEYOND = [(0, 2), (3, 1)]
OUTWARD = [(1, 0), (2, 3)]
FORWARD = [(0, 1), (1, 2), (2, 3)]
BACKWARD = [(1, 0), (2, 1), (3, 2)]
OUT_BEYOND = [(2, 0), (1, 3)]


def along(x, pairs):
    return lax.ppermute(x, "seq", pairs)


def to_mate(x):
    pairs = [(a * 4 + z, (1 - a) * 4 + z) for a in (0, 1) for z in (1, 2)]
    return lax.ppermute(x, ("fsdp", "seq"), pairs)


def seed_swap(x, bit):
    return lax.ppermute(x, "seed", [(i, i ^ bit) for i in range(4)])


def hub_body(
    mel_frames,
    lengths,
    targets,
    frame_mask,
    stem_weight,
    conv_in_weight,
    conv_out_weight,
    depth_weight,
    head_weight,
    norm_gain,
):
    chip = lax.axis_index("seq")
    side = lax.axis_index("fsdp")
    seeds = lax.axis_size("seed")
    rows = targets.shape[1]
    width = stem_weight.shape[2]
    channels = depth_weight.shape[2]
    vocab = head_weight.shape[2]
    step = mel_frames.shape[1] // rows
    tile = rows // 2
    low = chip == 1
    is_hub = jnp.logical_or(low, chip == 2)

    first = conv_in_weight[0]
    near_first = along(first, INWARD)
    hub_first = along(first, ACROSS)
    margin = step * EDGE
    before = along(mel_frames[0, -margin:].reshape(EDGE, -1), FORWARD)
    after = along(mel_frames[0, :margin].reshape(EDGE, -1), BACKWARD)
    blocks = mel_frames[0].reshape(rows, -1)
    outer = along(blocks, INWARD)
    far_first = along(near_first, ACROSS)

    groups = width // vocab
    head_rows = head_weight.shape[1]
    second = jnp.concatenate(
        [
            conv_out_weight[0],
            jnp.concatenate(jnp.split(head_weight[0], groups, axis=0), axis=1),
        ],
        axis=0,
    )
    mates = [to_mate(x) for x in (first, near_first, hub_first)]

    slots = 4
    deep = tile + 2 * EDGE

    def paired(before, block, after):
        frames = jnp.concatenate([before, block, after, after[:1]], axis=0)
        pairs = jnp.concatenate([frames[:-1], frames[1:]], axis=1)
        main = pairs[EDGE : EDGE + 2 * tile].reshape(2, CHUNKS, tile // CHUNKS, -1)
        main = main.transpose(0, 2, 1, 3).reshape(2, tile, -1)
        sides = [
            jnp.concatenate([pairs[k * tile : k * tile + EDGE], pairs[(k + 1) * tile + EDGE : (k + 1) * tile + 2 * EDGE]])
            for k in range(2)
        ]
        return main, jnp.stack(sides)

    length = lengths[0]
    positions = chip * rows + jnp.arange(rows, dtype=jnp.int32)
    counted = jnp.logical_and(frame_mask[0] > 0, positions < length)
    code = jnp.where(counted, targets[0], -1)
    lone = jnp.where(low, 0, 3)
    starts = jnp.stack([chip * rows, chip * rows + tile, lone * rows, lone * rows + tile]).astype(jnp.int32)
    alive = jnp.logical_and(is_hub, starts < length).astype(jnp.int32)
    hub = jnp.clip(chip, 1, 2)
    meta = jnp.concatenate(
        [
            starts,
            lengths,
            alive,
            jnp.stack([hub, 3 * (hub - 1), 3 - hub, 3 * (2 - hub), side, jnp.max(alive)]),
        ]
    ).astype(jnp.int32)

    gains = norm_gain[0]
    def stems(part, main, sides, *made):
        half = tile // 2
        return call(
            functools.partial(stem_kernel, 2 * part),
            (2,),
            [by_slot(main.shape[1:]), by_slot(sides.shape[1:]), whole(stem_weight.shape[1:]), whole(gains.shape)]
            + [apart] * len(made),
            [by_slot((tile, width), 2 * part), by_slot((deep, width))],
            [
                jax.ShapeDtypeStruct((slots, tile, width), jnp.bfloat16),
                jax.ShapeDtypeStruct((2, deep, width), jnp.bfloat16),
            ],
            [
                pltpu.VMEM((half, width), jnp.float32),
                pltpu.VMEM((half, width), jnp.float32),
                pltpu.VMEM((2 * EDGE, width), jnp.float32),
            ],
            slots * deep * main.shape[2] * width,
            slots * deep * (main.shape[2] + 2 * width),
            (meta, main, sides, stem_weight[0], gains, *made),
            {5: 0} if made else {},
        )

    apart = pl.BlockSpec(memory_space=pl.ANY)
    pinned = pl.BlockSpec(memory_space=pltpu.HBM)
    own_pairs, mates = lax.optimization_barrier((paired(before, blocks, after), mates))
    stem_out, own_normed = stems(0, *own_pairs)

    far_first, outer, own_normed = lax.optimization_barrier((far_first, outer, own_normed))
    first_pieces = (first, near_first, hub_first, far_first, *mates, to_mate(far_first))
    none = jnp.zeros_like(before)
    outer_before = jnp.where(low, none, blocks[-EDGE:])
    outer_after = jnp.where(low, blocks[:EDGE], none)
    outer_pairs = paired(outer_before, outer, outer_after)
    second_held, outer_pairs = lax.optimization_barrier((second, outer_pairs))
    near_second, hub_second, far_second = [along(second_held, pairs) for pairs in (INWARD, ACROSS, BEYOND)]
    second_mate = to_mate(second_held)
    stem_out, outer_normed = stems(1, *outer_pairs, stem_out)

    code_held, _ = lax.optimization_barrier((code, first_pieces[-1]))
    codes = jnp.concatenate([code, along(code_held, INWARD)]).reshape(slots, CHUNKS, tile // CHUNKS)

    taps = jnp.broadcast_to(
        depth_weight[0].astype(jnp.float32)[:, None, :], (depth_weight.shape[1], CHUNKS, channels)
    )
    extent = tile // CHUNKS + depth_weight.shape[1] - 1
    def convolve(part, normed, pieces, *made):
        return call(
            functools.partial(conv_kernel, 2 * part),
            (2,),
            [by_slot((deep, width)), whole(taps.shape)] + [pinned] * 8 + [apart] * len(made),
            by_slot((tile, channels), 2 * part),
            jax.ShapeDtypeStruct((slots, tile, channels), jnp.bfloat16),
            [
                pltpu.VMEM((8 * first.shape[0], first.shape[1]), jnp.bfloat16),
                pltpu.VMEM((deep, 2 * LANES), jnp.float32),
                pltpu.VMEM((deep, 2 * LANES), jnp.float32),
                pltpu.VMEM((extent, CHUNKS, LANES), jnp.float32),
                pltpu.VMEM((2 * EDGE, LANES), jnp.float32),
                pltpu.VMEM((deep, LANES), jnp.float32),
                pltpu.SemaphoreType.DMA((8,)),
            ],
            slots * deep * width * 2 * channels,
            slots * deep * width + 8 * first.size * 2,
            (meta, normed, taps, *pieces, *made),
            {11: 0} if made else {},
        )

    swished = convolve(0, own_normed, first_pieces)
    near_second, hub_second, far_second, swished, outer_normed = lax.optimization_barrier(
        (near_second, hub_second, far_second, swished, outer_normed)
    )
    second_rest = [near_second, hub_second, far_second]
    second_pieces = (second, *second_rest, second_mate, *[to_mate(x) for x in second_rest])
    swished = convolve(1, outer_normed, first_pieces, swished)
    errors = call(
        head_kernel,
        (slots,),
        [by_slot((tile, channels)), by_slot((tile, width)), by_slot(codes.shape[1:]), whole(gains.shape)] + [pinned] * 8,
        by_slot((CHUNKS, LANES)),
        jax.ShapeDtypeStruct((slots, CHUNKS, LANES), jnp.float32),
        [
            pltpu.VMEM((8 * conv_out_weight.shape[1], width), jnp.bfloat16),
            pltpu.VMEM((8 * head_rows, vocab), jnp.bfloat16),
            pltpu.VMEM((tile // 2, width), jnp.float32),
            pltpu.VMEM((tile // 2, width), jnp.float32),
            pltpu.VMEM((tile // 2, width), jnp.bfloat16),
            pltpu.VMEM((tile // 2, width), jnp.bfloat16),
            pltpu.VMEM((tile // 2, vocab), jnp.float32),
            pltpu.VMEM((tile // 2, vocab), jnp.float32),
            pltpu.SemaphoreType.DMA((8, 1 + groups)),
        ],
        2 * slots * tile * (channels + vocab) * width,
        slots * tile * (channels + width) * 2,
        (meta, swished, stem_out, codes, gains, *second_pieces),
    )

    one, two, three = [seed_swap(errors, bit) for bit in (1, 2, 3)]
    total = ((errors + one) + (two + three)) / jnp.float32(seeds)
    total = total[:, :, : tile // CHUNKS].reshape(2, rows)
    part = jnp.sum(total).reshape(1)
    own_half, outer_half = total
    from_hub = along(jnp.concatenate([outer_half, part]), OUTWARD)
    parts = [part[0], along(part, ACROSS)[0], along(part, OUT_BEYOND)[0], from_hub[rows]]
    frame_error = jnp.where(is_hub, own_half, from_hub[:rows])
    utt_score = ((parts[0] + parts[3]) + (parts[1] + parts[2])) / length.astype(jnp.float32)
    return (frame_error[None, :], utt_score.reshape(1))


def from_behind(x, axis, by):
    count = lax.axis_size(axis)
    pairs = [(i, i + by) for i in range(count) if 0 <= i + by < count]
    return lax.ppermute(x, axis, pairs)


def extended(x, sides, width):
    for axis, dim in sides:
        count, length = (lax.axis_size(axis), x.shape[dim])
        up = [(i, (i + 1) % count) for i in range(count - 1)]
        down = [(j, i) for i, j in up]
        last = lax.slice_in_dim(x, length - width, length, axis=dim)
        first = lax.slice_in_dim(x, 0, width, axis=dim)
        before = lax.ppermute(last, axis, up)
        after = lax.ppermute(first, axis, down)
        x = jnp.concatenate([before, x, after], axis=dim)
    return x


def layer_norm(values, gain_row):
    row_mean = jnp.mean(values, axis=-1, keepdims=True)
    centred = values - row_mean
    row_var = jnp.mean(centred * centred, axis=-1, keepdims=True)
    return (centred * lax.rsqrt(row_var + 1e-05) * gain_row).astype(jnp.bfloat16)


def block_product(left_rows, right_matrix):
    return jnp.dot(left_rows, right_matrix, preferred_element_type=jnp.float32)


def row_product(activations, shard_piece):
    return block_product(activations, shard_piece[0])


def body(
    mel_frames,
    lengths,
    targets,
    frame_mask,
    stem_weight,
    conv_in_weight,
    conv_out_weight,
    depth_weight,
    head_weight,
    norm_gain,
):
    frame_rows = targets.shape[1]
    blocks = mel_frames[0].reshape(frame_rows, -1)
    next_block = from_behind(blocks[:1], "seq", -1)
    following = jnp.concatenate([blocks[1:], next_block], 0)
    half_width = blocks.shape[1]
    stem_matrix = stem_weight[0]
    stem_out = (
        jnp.dot(blocks, stem_matrix[:half_width], preferred_element_type=jnp.float32)
        + jnp.dot(following, stem_matrix[half_width:], preferred_element_type=jnp.float32)
    ).astype(jnp.bfloat16)
    offset = lax.axis_index("seq") * frame_rows
    length = lengths[0]
    positions = offset + jnp.arange(frame_rows, dtype=jnp.int32)
    frame_live = positions < length
    gain_rows = norm_gain[0]
    normed_one = layer_norm(stem_out.astype(jnp.float32), gain_rows[0])
    tap_count = depth_weight.shape[1]
    channels = depth_weight.shape[2]
    halo_width = tap_count // 2
    conv_input = extended(normed_one, (("seq", 0),), halo_width)
    mixed_rows = row_product(
        conv_input, lax.all_gather(conv_in_weight, ("fsdp", "seq"), axis=1, tiled=True)
    )
    input_positions = offset - halo_width + jnp.arange(conv_input.shape[0], dtype=jnp.int32)
    input_live = jnp.logical_and(input_positions >= 0, input_positions < length)
    gated_rows = (
        mixed_rows[:, :channels]
        * jax.nn.sigmoid(mixed_rows[:, channels:])
        * input_live[:, None].astype(jnp.float32)
    ).astype(jnp.bfloat16)
    depthwise = jnp.zeros((frame_rows, channels), jnp.float32)
    for tap_index in range(tap_count):
        depthwise = depthwise + gated_rows[tap_index : tap_index + frame_rows].astype(
            jnp.float32
        ) * depth_weight[0, tap_index].astype(jnp.float32)
    swished = jax.nn.silu(depthwise).astype(jnp.bfloat16)
    conv_proj = row_product(
        swished, lax.all_gather(conv_out_weight, ("fsdp", "seq"), axis=1, tiled=True)
    )
    after_conv = stem_out.astype(jnp.float32) + conv_proj
    normed_two = layer_norm(after_conv, gain_rows[1])
    logits = row_product(
        normed_two, lax.all_gather(head_weight, ("fsdp", "seq"), axis=1, tiled=True)
    )
    posterior = jax.nn.softmax(logits, axis=-1)
    vocab_size = logits.shape[1]
    onehot = (jnp.arange(vocab_size, dtype=jnp.int32)[None, :] == targets[0][:, None]).astype(
        jnp.float32
    )
    differ = posterior - onehot
    frame_err = (
        jnp.sqrt(jnp.sum(differ * differ, axis=-1))
        * frame_live.astype(jnp.float32)
        * frame_mask[0].astype(jnp.float32)
    )
    seed_count = lax.axis_size("seed")
    frame_error = lax.psum(frame_err, "seed") / jnp.float32(seed_count)
    numerator = lax.psum(jnp.sum(frame_error), "seq")
    utt_score = numerator / length.astype(jnp.float32)
    return (frame_error[None, :], utt_score.reshape(1))


def solution(mesh):
    in_specs = (
        P("fsdp", "seq", None),
        P("fsdp"),
        P("fsdp", "seq"),
        P("fsdp", "seq"),
        P("seed", None, None),
        P("seed", ("fsdp", "seq"), None),
        P("seed", ("fsdp", "seq"), None),
        P("seed", None, None),
        P("seed", ("fsdp", "seq"), None),
        P("seed", None, None),
    )
    out_specs = (P("fsdp", "seq"), P("fsdp"))
    hubs = mesh.shape["seq"] == 4 and mesh.shape["fsdp"] == 2
    return jax.shard_map(
        hub_body if hubs else body, mesh=mesh, in_specs=in_specs, out_specs=out_specs, check_vma=False
    )
```

```python
import functools

import jax
import jax.numpy as jnp
from jax import lax
from jax.experimental import pallas as pl
from jax.experimental.pallas import tpu as pltpu
from jax.sharding import PartitionSpec as P

LANES = 128
CHUNKS = 8
EDGE = 16
VMEM_BYTES = 24 * 1024 * 1024


def norm_rows(values, gain_row):
    row_mean = jnp.mean(values, axis=-1, keepdims=True)
    centred = values - row_mean
    row_var = jnp.mean(centred * centred, axis=-1, keepdims=True)
    return (centred * lax.rsqrt(row_var + 1e-05) * gain_row).astype(jnp.bfloat16)


def sigmoid(x):
    return 0.5 * jnp.tanh(0.5 * x) + 0.5


def weave(*tracks):
    steps = [((i + 0.5) / len(track), k, step) for k, track in enumerate(tracks) for i, step in enumerate(track)]
    for _, _, step in sorted(steps, key=lambda entry: entry[:2]):
        step()


def column_steps(left, right, into, block):
    def step(at):
        into[:, at : at + block] = jnp.dot(left(), right[:, at : at + block], preferred_element_type=jnp.float32)

    return [functools.partial(step, at) for at in range(0, right.shape[1], block)]


def stem_kernel(
    first_slot, meta, main_ref, margin_ref, stem_ref, gain_ref, stem_out_ref, normed_ref, acc_a, acc_b, acc_c
):
    slot = pl.program_id(0) + first_slot
    frames = main_ref.shape[1]
    part = acc_a.shape[0]
    group = 16

    def norm_step(acc, at, keep, row):
        stem_out = acc[row : row + group, :].astype(jnp.bfloat16)
        if keep:
            stem_out_ref[0, at + row : at + row + group, :] = stem_out
        normed_ref[0, at + row : at + row + group, :] = norm_rows(stem_out.astype(jnp.float32), gain_ref[0:1, :])

    def norm(acc, at, keep):
        return [functools.partial(norm_step, acc, at, keep, row) for row in range(0, acc.shape[0], group)]

    @pl.when(meta[5 + slot] > 0)
    def _():
        block = 2 * LANES
        weave(column_steps(lambda: main_ref[0, :part, :], stem_ref, acc_a, block))
        weave(column_steps(lambda: main_ref[0, part:, :], stem_ref, acc_b, block), norm(acc_a, 0, True))
        weave(column_steps(lambda: margin_ref[0], stem_ref, acc_c, block), norm(acc_b, part, True))
        weave(norm(acc_c, frames, False))


def shards(meta, pieces):
    side = meta[13]
    return [(pieces[i], (side if i < 4 else 1 - side) * 4 + meta[9 + i % 4]) for i in range(8)]


def conv_kernel(first_slot, meta, normed_ref, taps_ref, *rest):
    pieces = rest[:8]
    swished_ref, weight, mixed_a, mixed_b, gated, margin, mask, sems = rest[8:]
    slot = pl.program_id(0) + first_slot
    rows = normed_ref.shape[1]
    frames = swished_ref.shape[1]
    channels = swished_ref.shape[2]
    tap_count = taps_ref.shape[0]
    reach = tap_count // 2
    piece = pieces[0].shape[0]
    run_length = frames // CHUNKS

    @pl.when(jnp.logical_and(pl.program_id(0) == 0, meta[14] > 0))
    def _():
        copies = [
            pltpu.make_async_copy(
                ref, weight.at[pl.ds(pl.multiple_of(block * piece, 16), piece)], sems.at[i]
            )
            for i, (ref, block) in enumerate(shards(meta, pieces))
        ]
        for copy in copies:
            copy.start()
        for copy in copies:
            copy.wait()

    @pl.when(meta[5 + slot] > 0)
    def _():
        row = lax.broadcasted_iota(jnp.int32, (rows, LANES), 0)
        inner = (row % CHUNKS) * run_length + row // CHUNKS
        outer = jnp.where(row < frames + EDGE, row - frames - EDGE, row - EDGE)
        at = meta[slot] + jnp.where(row < frames, inner, outer)
        mask[...] = jnp.logical_and(at >= 0, at < meta[4]).astype(jnp.float32)
        sublane = lax.broadcasted_iota(jnp.int32, (CHUNKS, LANES), 0)
        buffers = (mixed_a, mixed_b)

        def mix(block):
            low = block * LANES
            half = rows // 2

            def step(at):
                right = jnp.concatenate(
                    [weight[:, low : low + LANES], weight[:, channels + low : channels + low + LANES]], axis=1
                )
                buffers[block % 2][at : at + half, :] = jnp.dot(
                    normed_ref[0, at : at + half, :], right, preferred_element_type=jnp.float32
                )

            return [functools.partial(step, at) for at in (0, half)]

        def gate(block):
            mixed = buffers[block % 2]
            group = 32

            def step(at):
                here = slice(at, at + group)
                made = mixed[here, :LANES] * sigmoid(mixed[here, LANES:]) * mask[here, :]
                made = made.astype(jnp.bfloat16).astype(jnp.float32)
                if at < frames:
                    first = reach + at // CHUNKS
                    gated[first : first + group // CHUNKS] = made.reshape(group // CHUNKS, CHUNKS, LANES)
                else:
                    margin[...] = made

            def sides(i):
                before = pltpu.roll(gated[run_length + i], 1, 0)
                edge = margin[EDGE - reach + i : EDGE - reach + i + 1, :]
                gated[i] = jnp.where(sublane == 0, edge, before)
                after = pltpu.roll(gated[reach + i], CHUNKS - 1, 0)
                edge = margin[EDGE + i : EDGE + i + 1, :]
                gated[reach + run_length + i] = jnp.where(sublane == CHUNKS - 1, edge, after)

            return [functools.partial(step, at) for at in range(0, rows, group)] + [
                functools.partial(sides, i) for i in range(reach)
            ]

        def convolve(block):
            low = block * LANES
            run, held = 32, 8

            def step(start):
                sums = [None] * run
                for tap in range(0, tap_count, held):
                    taps = [taps_ref[j, :, low : low + LANES] for j in range(tap, min(tap + held, tap_count))]
                    for at in range(start + tap, start + tap + run + len(taps) - 1):
                        value = gated[at]
                        for j, weight_row in enumerate(taps):
                            k = at - tap - j - start
                            if 0 <= k < run:
                                term = value * weight_row
                                sums[k] = term if sums[k] is None else sums[k] + term
                for k in range(0, run, 2):
                    total = jnp.concatenate(sums[k : k + 2], axis=0)
                    first = (start + k) * CHUNKS
                    swished_ref[0, first : first + 2 * CHUNKS, low : low + LANES] = (
                        total * sigmoid(total)
                    ).astype(jnp.bfloat16)

            return [functools.partial(step, start) for start in range(0, run_length, run)]

        blocks = channels // LANES
        weave(mix(0))
        for block in range(blocks):
            weave(gate(block) + convolve(block), mix(block + 1) if block + 1 < blocks else [])


def head_kernel(first_slot, meta, swished_ref, stem_out_ref, code_ref, gain_ref, *rest):
    pieces = rest[:8]
    error_ref, back, head, acc_a, acc_b, norm_a, norm_b, logit_a, logit_b, sems = rest[8:]
    slot = pl.program_id(0) + first_slot
    frames = swished_ref.shape[1]
    vocab = head.shape[1]
    groups = back.shape[1] // vocab
    back_rows = back.shape[0] // 8
    head_rows = head.shape[0] // 8
    group_rows = head_rows // groups

    @pl.when(jnp.logical_and(pl.program_id(0) == 0, meta[14] > 0))
    def _():
        copies = []
        for i, (ref, block) in enumerate(shards(meta, pieces)):
            copies.append(
                pltpu.make_async_copy(
                    ref.at[pl.ds(0, back_rows)],
                    back.at[pl.ds(pl.multiple_of(block * back_rows, 16), back_rows)],
                    sems.at[i, 0],
                )
            )
            for g in range(groups):
                copies.append(
                    pltpu.make_async_copy(
                        ref.at[pl.ds(back_rows, group_rows), pl.ds(g * vocab, vocab)],
                        head.at[pl.ds(pl.multiple_of(block * head_rows + g * group_rows, 16), group_rows)],
                        sems.at[i, 1 + g],
                    )
                )
        for copy in copies:
            copy.start()
        for copy in copies:
            copy.wait()

    @pl.when(meta[5 + slot] <= 0)
    def _():
        error_ref[...] = jnp.zeros_like(error_ref)

    @pl.when(meta[5 + slot] > 0)
    def _():
        part = acc_a.shape[0]
        lane = lax.broadcasted_iota(jnp.int32, (CHUNKS, LANES), 1)
        error_ref[...] = jnp.zeros_like(error_ref)

        def norm(at, acc, normed):
            group = 16

            def step(row):
                values = acc[row : row + group, :] + stem_out_ref[0, at + row : at + row + group, :].astype(jnp.float32)
                normed[row : row + group, :] = norm_rows(values, gain_ref[1:2, :])

            return [functools.partial(step, row) for row in range(0, part, group)]

        def errors(at, logits):
            group = 32
            token = lax.broadcasted_iota(jnp.int32, (group, vocab), 1)

            def step(first):
                scores = logits[first : first + group, :]
                grown = jnp.exp(scores - jnp.max(scores, axis=-1, keepdims=True))
                posterior = grown * (1.0 / jnp.sum(grown, axis=-1, keepdims=True))
                steps = range((at + first) // CHUNKS, (at + first + group) // CHUNKS)
                code = jnp.concatenate([code_ref[0, :, m : m + 1] for m in steps], axis=0)
                differ = posterior - (token == code).astype(jnp.float32)
                error = jnp.sqrt(jnp.sum(differ * differ, axis=-1, keepdims=True))
                error = jnp.where(code >= 0, error, 0.0)
                row = error_ref[0]
                for k, m in enumerate(steps):
                    row = jnp.where(lane == m, error[k * CHUNKS : (k + 1) * CHUNKS, :], row)
                error_ref[0] = row

            return [functools.partial(step, first) for first in range(0, part, group)]

        block = 2 * LANES
        weave(column_steps(lambda: swished_ref[0, :part, :], back, acc_a, block))
        weave(column_steps(lambda: swished_ref[0, part:, :], back, acc_b, block), norm(0, acc_a, norm_a))
        weave(column_steps(lambda: norm_a[...], head, logit_a, block), norm(part, acc_b, norm_b))
        weave(column_steps(lambda: norm_b[...], head, logit_b, block), errors(0, logit_a))
        weave(errors(part, logit_b))


def call(kernel, grid, in_specs, out_specs, out_shape, scratch, flops, moved, operands):
    return pl.pallas_call(
        kernel,
        grid_spec=pltpu.PrefetchScalarGridSpec(
            num_scalar_prefetch=1,
            grid=grid,
            in_specs=in_specs,
            out_specs=out_specs,
            scratch_shapes=scratch,
        ),
        out_shape=out_shape,
        compiler_params=pltpu.CompilerParams(
            dimension_semantics=("arbitrary",), vmem_limit_bytes=VMEM_BYTES
        ),
        cost_estimate=pl.CostEstimate(flops=flops // 16, bytes_accessed=moved // 16, transcendentals=0),
    )(*operands)


def whole(shape):
    return pl.BlockSpec(shape, lambda i, meta: (0,) * len(shape))


def by_slot(shape):
    return pl.BlockSpec((1,) + shape, lambda i, meta: (i,) + (0,) * len(shape))


INWARD = [(0, 1), (3, 2)]
ACROSS = [(1, 2), (2, 1)]
BEYOND = [(0, 2), (3, 1)]
OUTWARD = [(1, 0), (2, 3)]
FORWARD = [(0, 1), (1, 2), (2, 3)]
BACKWARD = [(1, 0), (2, 1), (3, 2)]
OUT_BEYOND = [(2, 0), (1, 3)]


def along(x, pairs):
    return lax.ppermute(x, "seq", pairs)


def to_mate(x):
    pairs = [(a * 4 + z, (1 - a) * 4 + z) for a in (0, 1) for z in (1, 2)]
    return lax.ppermute(x, ("fsdp", "seq"), pairs)


def seed_swap(x, bit):
    return lax.ppermute(x, "seed", [(i, i ^ bit) for i in range(4)])


def hub_body(
    mel_frames,
    lengths,
    targets,
    frame_mask,
    stem_weight,
    conv_in_weight,
    conv_out_weight,
    depth_weight,
    head_weight,
    norm_gain,
):
    chip = lax.axis_index("seq")
    side = lax.axis_index("fsdp")
    seeds = lax.axis_size("seed")
    rows = targets.shape[1]
    width = stem_weight.shape[2]
    channels = depth_weight.shape[2]
    vocab = head_weight.shape[2]
    step = mel_frames.shape[1] // rows
    tile = rows // 2
    low = chip == 1
    is_hub = jnp.logical_or(low, chip == 2)

    first = conv_in_weight[0]
    near_first, hub_first, far_first = [along(first, pairs) for pairs in (INWARD, ACROSS, BEYOND)]
    margin = step * EDGE
    before = along(mel_frames[0, -margin:].reshape(EDGE, -1), FORWARD)
    after = along(mel_frames[0, :margin].reshape(EDGE, -1), BACKWARD)
    blocks = mel_frames[0].reshape(rows, -1)
    outer = along(blocks, INWARD)

    groups = width // vocab
    head_rows = head_weight.shape[1]
    second = jnp.concatenate(
        [
            conv_out_weight[0],
            jnp.concatenate(jnp.split(head_weight[0], groups, axis=0), axis=1),
        ],
        axis=0,
    )
    mates = [to_mate(x) for x in (first, near_first, hub_first)]

    slots = 4
    deep = tile + 2 * EDGE

    def paired(before, block, after):
        frames = jnp.concatenate([before, block, after, after[:1]], axis=0)
        pairs = jnp.concatenate([frames[:-1], frames[1:]], axis=1)
        main = pairs[EDGE : EDGE + 2 * tile].reshape(2, CHUNKS, tile // CHUNKS, -1)
        main = main.transpose(0, 2, 1, 3).reshape(2, tile, -1)
        sides = [
            jnp.concatenate([pairs[k * tile : k * tile + EDGE], pairs[(k + 1) * tile + EDGE : (k + 1) * tile + 2 * EDGE]])
            for k in range(2)
        ]
        return main, jnp.stack(sides)

    length = lengths[0]
    positions = chip * rows + jnp.arange(rows, dtype=jnp.int32)
    counted = jnp.logical_and(frame_mask[0] > 0, positions < length)
    code = jnp.where(counted, targets[0], -1)
    lone = jnp.where(low, 0, 3)
    starts = jnp.stack([chip * rows, chip * rows + tile, lone * rows, lone * rows + tile]).astype(jnp.int32)
    alive = jnp.logical_and(is_hub, starts < length).astype(jnp.int32)
    hub = jnp.clip(chip, 1, 2)
    meta = jnp.concatenate(
        [
            starts,
            lengths,
            alive,
            jnp.stack([hub, 3 * (hub - 1), 3 - hub, 3 * (2 - hub), side, jnp.max(alive)]),
        ]
    ).astype(jnp.int32)

    gains = norm_gain[0]
    def stems(part, main, sides):
        half = tile // 2
        return call(
            functools.partial(stem_kernel, 2 * part),
            (2,),
            [by_slot(main.shape[1:]), by_slot(sides.shape[1:]), whole(stem_weight.shape[1:]), whole(gains.shape)],
            [by_slot((tile, width)), by_slot((deep, width))],
            [
                jax.ShapeDtypeStruct((2, tile, width), jnp.bfloat16),
                jax.ShapeDtypeStruct((2, deep, width), jnp.bfloat16),
            ],
            [
                pltpu.VMEM((half, width), jnp.float32),
                pltpu.VMEM((half, width), jnp.float32),
                pltpu.VMEM((2 * EDGE, width), jnp.float32),
            ],
            slots * deep * main.shape[2] * width,
            slots * deep * (main.shape[2] + 2 * width),
            (meta, main, sides, stem_weight[0], gains),
        )

    pinned = pl.BlockSpec(memory_space=pltpu.HBM)
    own_pairs, mates, far_first = lax.optimization_barrier((paired(before, blocks, after), mates, far_first))
    own_stem, own_normed = stems(0, *own_pairs)
    first_pieces = (first, near_first, hub_first, far_first, *mates, to_mate(far_first))
    second_held, own_normed = lax.optimization_barrier((second, own_normed))
    near_second, hub_second, far_second = [along(second_held, pairs) for pairs in (INWARD, ACROSS, BEYOND)]
    second_mate = to_mate(second_held)
    none = jnp.zeros_like(before)
    outer_before = jnp.where(low, none, blocks[-EDGE:])
    outer_after = jnp.where(low, blocks[:EDGE], none)
    code_held, _ = lax.optimization_barrier((code, first_pieces[-1]))
    codes = jnp.concatenate([code, along(code_held, INWARD)]).reshape(slots, CHUNKS, tile // CHUNKS)

    taps = jnp.broadcast_to(
        depth_weight[0].astype(jnp.float32)[:, None, :], (depth_weight.shape[1], CHUNKS, channels)
    )
    extent = tile // CHUNKS + depth_weight.shape[1] - 1
    def convolve(part, normed, pieces):
        return call(
            functools.partial(conv_kernel, 2 * part),
            (2,),
            [by_slot((deep, width)), whole(taps.shape)] + [pinned] * 8,
            by_slot((tile, channels)),
            jax.ShapeDtypeStruct((2, tile, channels), jnp.bfloat16),
            [
                pltpu.VMEM((8 * first.shape[0], first.shape[1]), jnp.bfloat16),
                pltpu.VMEM((deep, 2 * LANES), jnp.float32),
                pltpu.VMEM((deep, 2 * LANES), jnp.float32),
                pltpu.VMEM((extent, CHUNKS, LANES), jnp.float32),
                pltpu.VMEM((2 * EDGE, LANES), jnp.float32),
                pltpu.VMEM((deep, LANES), jnp.float32),
                pltpu.SemaphoreType.DMA((8,)),
            ],
            slots * deep * width * 2 * channels,
            slots * deep * width + 8 * first.size * 2,
            (meta, normed, taps, *pieces),
        )

    own_swished = convolve(0, own_normed, first_pieces)
    outer, own_swished = lax.optimization_barrier((outer, own_swished))
    outer_stem, outer_normed = stems(1, *paired(outer_before, outer, outer_after))

    near_second, hub_second, far_second, outer_normed = lax.optimization_barrier(
        (near_second, hub_second, far_second, outer_normed)
    )
    second_rest = [near_second, hub_second, far_second]
    second_pieces = (second, *second_rest, second_mate, *[to_mate(x) for x in second_rest])
    outer_swished = convolve(1, outer_normed, first_pieces)

    def heads(part, swished, stem_out, code):
        return call(
            functools.partial(head_kernel, 2 * part),
            (2,),
            [by_slot((tile, channels)), by_slot((tile, width)), by_slot(code.shape[1:]), whole(gains.shape)]
            + [pinned] * 8,
            by_slot((CHUNKS, LANES)),
            jax.ShapeDtypeStruct((2, CHUNKS, LANES), jnp.float32),
            [
                pltpu.VMEM((8 * conv_out_weight.shape[1], width), jnp.bfloat16),
                pltpu.VMEM((8 * head_rows, vocab), jnp.bfloat16),
                pltpu.VMEM((tile // 2, width), jnp.float32),
                pltpu.VMEM((tile // 2, width), jnp.float32),
                pltpu.VMEM((tile // 2, width), jnp.bfloat16),
                pltpu.VMEM((tile // 2, width), jnp.bfloat16),
                pltpu.VMEM((tile // 2, vocab), jnp.float32),
                pltpu.VMEM((tile // 2, vocab), jnp.float32),
                pltpu.SemaphoreType.DMA((8, 1 + groups)),
            ],
            slots * tile * (channels + vocab) * width,
            slots * tile * (channels + width),
            (meta, swished, stem_out, code, gains, *second_pieces),
        )

    codes = codes.reshape(2, 2, CHUNKS, tile // CHUNKS)
    errors = jnp.concatenate(
        [heads(0, own_swished, own_stem, codes[0]), heads(1, outer_swished, outer_stem, codes[1])], axis=0
    )

    one, two, three = [seed_swap(errors, bit) for bit in (1, 2, 3)]
    total = ((errors + one) + (two + three)) / jnp.float32(seeds)
    total = total[:, :, : tile // CHUNKS].reshape(2, rows)
    part = jnp.sum(total).reshape(1)
    own_half, outer_half = total
    from_hub = along(jnp.concatenate([outer_half, part]), OUTWARD)
    parts = [part[0], along(part, ACROSS)[0], along(part, OUT_BEYOND)[0], from_hub[rows]]
    frame_error = jnp.where(is_hub, own_half, from_hub[:rows])
    utt_score = ((parts[0] + parts[3]) + (parts[1] + parts[2])) / length.astype(jnp.float32)
    return (frame_error[None, :], utt_score.reshape(1))


def from_behind(x, axis, by):
    count = lax.axis_size(axis)
    pairs = [(i, i + by) for i in range(count) if 0 <= i + by < count]
    return lax.ppermute(x, axis, pairs)


def extended(x, sides, width):
    for axis, dim in sides:
        count, length = (lax.axis_size(axis), x.shape[dim])
        up = [(i, (i + 1) % count) for i in range(count - 1)]
        down = [(j, i) for i, j in up]
        last = lax.slice_in_dim(x, length - width, length, axis=dim)
        first = lax.slice_in_dim(x, 0, width, axis=dim)
        before = lax.ppermute(last, axis, up)
        after = lax.ppermute(first, axis, down)
        x = jnp.concatenate([before, x, after], axis=dim)
    return x


def layer_norm(values, gain_row):
    row_mean = jnp.mean(values, axis=-1, keepdims=True)
    centred = values - row_mean
    row_var = jnp.mean(centred * centred, axis=-1, keepdims=True)
    return (centred * lax.rsqrt(row_var + 1e-05) * gain_row).astype(jnp.bfloat16)


def block_product(left_rows, right_matrix):
    return jnp.dot(left_rows, right_matrix, preferred_element_type=jnp.float32)


def row_product(activations, shard_piece):
    return block_product(activations, shard_piece[0])


def body(
    mel_frames,
    lengths,
    targets,
    frame_mask,
    stem_weight,
    conv_in_weight,
    conv_out_weight,
    depth_weight,
    head_weight,
    norm_gain,
):
    frame_rows = targets.shape[1]
    blocks = mel_frames[0].reshape(frame_rows, -1)
    next_block = from_behind(blocks[:1], "seq", -1)
    following = jnp.concatenate([blocks[1:], next_block], 0)
    half_width = blocks.shape[1]
    stem_matrix = stem_weight[0]
    stem_out = (
        jnp.dot(blocks, stem_matrix[:half_width], preferred_element_type=jnp.float32)
        + jnp.dot(following, stem_matrix[half_width:], preferred_element_type=jnp.float32)
    ).astype(jnp.bfloat16)
    offset = lax.axis_index("seq") * frame_rows
    length = lengths[0]
    positions = offset + jnp.arange(frame_rows, dtype=jnp.int32)
    frame_live = positions < length
    gain_rows = norm_gain[0]
    normed_one = layer_norm(stem_out.astype(jnp.float32), gain_rows[0])
    tap_count = depth_weight.shape[1]
    channels = depth_weight.shape[2]
    halo_width = tap_count // 2
    conv_input = extended(normed_one, (("seq", 0),), halo_width)
    mixed_rows = row_product(
        conv_input, lax.all_gather(conv_in_weight, ("fsdp", "seq"), axis=1, tiled=True)
    )
    input_positions = offset - halo_width + jnp.arange(conv_input.shape[0], dtype=jnp.int32)
    input_live = jnp.logical_and(input_positions >= 0, input_positions < length)
    gated_rows = (
        mixed_rows[:, :channels]
        * jax.nn.sigmoid(mixed_rows[:, channels:])
        * input_live[:, None].astype(jnp.float32)
    ).astype(jnp.bfloat16)
    depthwise = jnp.zeros((frame_rows, channels), jnp.float32)
    for tap_index in range(tap_count):
        depthwise = depthwise + gated_rows[tap_index : tap_index + frame_rows].astype(
            jnp.float32
        ) * depth_weight[0, tap_index].astype(jnp.float32)
    swished = jax.nn.silu(depthwise).astype(jnp.bfloat16)
    conv_proj = row_product(
        swished, lax.all_gather(conv_out_weight, ("fsdp", "seq"), axis=1, tiled=True)
    )
    after_conv = stem_out.astype(jnp.float32) + conv_proj
    normed_two = layer_norm(after_conv, gain_rows[1])
    logits = row_product(
        normed_two, lax.all_gather(head_weight, ("fsdp", "seq"), axis=1, tiled=True)
    )
    posterior = jax.nn.softmax(logits, axis=-1)
    vocab_size = logits.shape[1]
    onehot = (jnp.arange(vocab_size, dtype=jnp.int32)[None, :] == targets[0][:, None]).astype(
        jnp.float32
    )
    differ = posterior - onehot
    frame_err = (
        jnp.sqrt(jnp.sum(differ * differ, axis=-1))
        * frame_live.astype(jnp.float32)
        * frame_mask[0].astype(jnp.float32)
    )
    seed_count = lax.axis_size("seed")
    frame_error = lax.psum(frame_err, "seed") / jnp.float32(seed_count)
    numerator = lax.psum(jnp.sum(frame_error), "seq")
    utt_score = numerator / length.astype(jnp.float32)
    return (frame_error[None, :], utt_score.reshape(1))


def solution(mesh):
    in_specs = (
        P("fsdp", "seq", None),
        P("fsdp"),
        P("fsdp", "seq"),
        P("fsdp", "seq"),
        P("seed", None, None),
        P("seed", ("fsdp", "seq"), None),
        P("seed", ("fsdp", "seq"), None),
        P("seed", None, None),
        P("seed", ("fsdp", "seq"), None),
        P("seed", None, None),
    )
    out_specs = (P("fsdp", "seq"), P("fsdp"))
    hubs = mesh.shape["seq"] == 4 and mesh.shape["fsdp"] == 2
    return jax.shard_map(
        hub_body if hubs else body, mesh=mesh, in_specs=in_specs, out_specs=out_specs, check_vma=False
    )
```

```python
import jax
import jax.numpy as jnp
from jax import lax
from jax.experimental import pallas as pl
from jax.experimental.pallas import tpu as pltpu
from jax.sharding import PartitionSpec as P

LANES = 128
CHUNKS = 8
EDGE = 16
VMEM_BYTES = 56 * 1024 * 1024


def norm_rows(values, gain_row):
    row_mean = jnp.mean(values, axis=-1, keepdims=True)
    centred = values - row_mean
    row_var = jnp.mean(centred * centred, axis=-1, keepdims=True)
    return (centred * lax.rsqrt(row_var + 1e-05) * gain_row).astype(jnp.bfloat16)


def sigmoid(x):
    return 0.5 * jnp.tanh(0.5 * x) + 0.5


def stem_kernel(
    meta, main_ref, margin_ref, stem_ref, gain_ref, stem_out_ref, normed_ref, acc_a, acc_b, acc_c
):
    slot = pl.program_id(0)
    frames = main_ref.shape[1]
    part = acc_a.shape[0]
    group = 16

    def norm(acc, at, keep):
        for row in range(0, acc.shape[0], group):
            stem_out = acc[row : row + group, :].astype(jnp.bfloat16)
            if keep:
                stem_out_ref[0, at + row : at + row + group, :] = stem_out
            normed_ref[0, at + row : at + row + group, :] = norm_rows(stem_out.astype(jnp.float32), gain_ref[0:1, :])

    @pl.when(meta[5 + slot] > 0)
    def _():
        for acc, left in ((acc_a, main_ref[0, :part, :]), (acc_b, main_ref[0, part:, :]), (acc_c, margin_ref[0])):
            acc[...] = jnp.dot(left, stem_ref[...], preferred_element_type=jnp.float32)
        norm(acc_a, 0, True)
        norm(acc_b, part, True)
        norm(acc_c, frames, False)


def shards(meta, pieces):
    side = meta[13]
    return [(pieces[i], (side if i < 4 else 1 - side) * 4 + meta[9 + i % 4]) for i in range(8)]


def conv_kernel(meta, normed_ref, taps_ref, *rest):
    pieces = rest[:8]
    swished_ref, weight, mixed, gated_a, gated_b, margin, mask, sems = rest[8:]
    slot = pl.program_id(0)
    rows = normed_ref.shape[1]
    frames = swished_ref.shape[1]
    channels = swished_ref.shape[2]
    tap_count = taps_ref.shape[0]
    reach = tap_count // 2
    piece = weight.shape[0] // 8
    run_length = frames // CHUNKS

    @pl.when(jnp.logical_and(pl.program_id(0) == 0, meta[14] > 0))
    def _():
        copies = [
            pltpu.make_async_copy(
                ref.at[pl.ds(0, piece)], weight.at[pl.ds(pl.multiple_of(block * piece, 16), piece)], sems.at[i]
            )
            for i, (ref, block) in enumerate(shards(meta, pieces))
        ]
        for copy in copies:
            copy.start()
        for copy in copies:
            copy.wait()

    @pl.when(meta[5 + slot] > 0)
    def _():
        row = lax.broadcasted_iota(jnp.int32, (rows, LANES), 0)
        inner = (row % CHUNKS) * run_length + row // CHUNKS
        outer = jnp.where(row < frames + EDGE, row - frames - EDGE, row - EDGE)
        at = meta[slot] + jnp.where(row < frames, inner, outer)
        mask[...] = jnp.logical_and(at >= 0, at < meta[4]).astype(jnp.float32)
        sublane = lax.broadcasted_iota(jnp.int32, (CHUNKS, LANES), 0)
        half = rows // 2
        for first in (0, half):
            mixed[first : first + half, :] = jnp.dot(
                normed_ref[0, first : first + half, :], weight[...], preferred_element_type=jnp.float32
            )

        def gate(block):
            low = block * LANES
            gated = (gated_a, gated_b)[block % 2]
            group = 32
            for at in range(0, rows, group):
                here = slice(at, at + group)
                made = mixed[here, low : low + LANES] * mask[here, :]
                made = made * sigmoid(mixed[here, channels + low : channels + low + LANES])
                made = made.astype(jnp.bfloat16).astype(jnp.float32)
                if at < frames:
                    first = reach + at // CHUNKS
                    gated[first : first + group // CHUNKS] = made.reshape(group // CHUNKS, CHUNKS, LANES)
                else:
                    margin[...] = made
            for i in range(reach):
                before = pltpu.roll(gated[run_length + i], 1, 0)
                edge = margin[EDGE - reach + i : EDGE - reach + i + 1, :]
                gated[i] = jnp.where(sublane == 0, edge, before)
                after = pltpu.roll(gated[reach + i], CHUNKS - 1, 0)
                edge = margin[EDGE + i : EDGE + i + 1, :]
                gated[reach + run_length + i] = jnp.where(sublane == CHUNKS - 1, edge, after)

        def convolve(block):
            low = block * LANES
            run, held = 32, 8
            gated = (gated_a, gated_b)[block % 2]
            for start in range(0, run_length, run):
                sums = [None] * run
                for tap in range(0, tap_count, held):
                    taps = [taps_ref[j, :, low : low + LANES] for j in range(tap, min(tap + held, tap_count))]
                    for at in range(start + tap, start + tap + run + len(taps) - 1):
                        value = gated[at]
                        for j, weight_row in enumerate(taps):
                            k = at - tap - j - start
                            if 0 <= k < run:
                                term = value * weight_row
                                sums[k] = term if sums[k] is None else sums[k] + term
                for k in range(0, run, 2):
                    total = jnp.concatenate(sums[k : k + 2], axis=0)
                    first = (start + k) * CHUNKS
                    swished_ref[0, first : first + 2 * CHUNKS, low : low + LANES] = (
                        total * sigmoid(total)
                    ).astype(jnp.bfloat16)

        blocks = channels // LANES
        for block in range(blocks):
            gate(block)
            convolve(block)


def head_kernel(meta, swished_ref, stem_out_ref, code_ref, gain_ref, *rest):
    pieces = rest[:8]
    error_ref, back, head, acc_a, acc_b, norm_a, norm_b, logit_a, logit_b, sems = rest[8:]
    slot = pl.program_id(0)
    frames = swished_ref.shape[1]
    vocab = head.shape[1]
    groups = back.shape[1] // vocab
    back_rows = back.shape[0] // 8
    head_rows = head.shape[0] // 8
    group_rows = head_rows // groups

    @pl.when(jnp.logical_and(pl.program_id(0) == 0, meta[14] > 0))
    def _():
        copies = []
        for i, (ref, block) in enumerate(shards(meta, pieces)):
            copies.append(
                pltpu.make_async_copy(
                    ref.at[pl.ds(0, back_rows)],
                    back.at[pl.ds(pl.multiple_of(block * back_rows, 16), back_rows)],
                    sems.at[i, 0],
                )
            )
            for g in range(groups):
                copies.append(
                    pltpu.make_async_copy(
                        ref.at[pl.ds(back_rows, group_rows), pl.ds(g * vocab, vocab)],
                        head.at[pl.ds(pl.multiple_of(block * head_rows + g * group_rows, 16), group_rows)],
                        sems.at[i, 1 + g],
                    )
                )
        for copy in copies:
            copy.start()
        for copy in copies:
            copy.wait()

    @pl.when(meta[5 + slot] <= 0)
    def _():
        error_ref[...] = jnp.zeros_like(error_ref)

    @pl.when(meta[5 + slot] > 0)
    def _():
        part = acc_a.shape[0]
        lane = lax.broadcasted_iota(jnp.int32, (CHUNKS, LANES), 1)
        def norm(at, acc, normed):
            group = 16
            for row in range(0, part, group):
                values = acc[row : row + group, :] + stem_out_ref[0, at + row : at + row + group, :].astype(jnp.float32)
                normed[row : row + group, :] = norm_rows(values, gain_ref[1:2, :])

        def errors(at, logits, row):
            group = 32
            token = lax.broadcasted_iota(jnp.int32, (group, vocab), 1)
            for first in range(0, part, group):
                scores = logits[first : first + group, :]
                grown = jnp.exp(scores - jnp.max(scores, axis=-1, keepdims=True))
                posterior = grown * (1.0 / jnp.sum(grown, axis=-1, keepdims=True))
                steps = range((at + first) // CHUNKS, (at + first + group) // CHUNKS)
                code = jnp.concatenate([code_ref[0, :, m : m + 1] for m in steps], axis=0)
                differ = posterior - (token == code).astype(jnp.float32)
                error = jnp.sqrt(jnp.sum(differ * differ, axis=-1, keepdims=True))
                error = jnp.where(code >= 0, error, 0.0)
                for k, m in enumerate(steps):
                    row = jnp.where(lane == m, error[k * CHUNKS : (k + 1) * CHUNKS, :], row)
            return row

        halves = ((0, acc_a, norm_a, logit_a), (part, acc_b, norm_b, logit_b))
        for at, acc, _, _ in halves:
            acc[...] = jnp.dot(swished_ref[0, at : at + part, :], back[...], preferred_element_type=jnp.float32)
        for at, acc, normed, logits in halves:
            norm(at, acc, normed)
            logits[...] = jnp.dot(normed[...], head[...], preferred_element_type=jnp.float32)
        row = jnp.zeros((CHUNKS, LANES), jnp.float32)
        for at, _, _, logits in halves:
            row = errors(at, logits, row)
        error_ref[0] = row


def call(kernel, grid, in_specs, out_specs, out_shape, scratch, flops, moved, operands):
    return pl.pallas_call(
        kernel,
        grid_spec=pltpu.PrefetchScalarGridSpec(
            num_scalar_prefetch=1,
            grid=grid,
            in_specs=in_specs,
            out_specs=out_specs,
            scratch_shapes=scratch,
        ),
        out_shape=out_shape,
        compiler_params=pltpu.CompilerParams(
            dimension_semantics=("arbitrary",), vmem_limit_bytes=VMEM_BYTES
        ),
        cost_estimate=pl.CostEstimate(flops=flops // 16, bytes_accessed=moved // 16, transcendentals=0),
    )(*operands)


def whole(shape):
    return pl.BlockSpec(shape, lambda i, meta: (0,) * len(shape))


def by_slot(shape):
    return pl.BlockSpec((1,) + shape, lambda i, meta: (i,) + (0,) * len(shape))


INWARD = [(0, 1), (3, 2)]
ACROSS = [(1, 2), (2, 1)]
BEYOND = [(0, 2), (3, 1)]
OUTWARD = [(1, 0), (2, 3)]
OUT_BEYOND = [(2, 0), (1, 3)]


def along(x, pairs):
    return lax.ppermute(x, "seq", pairs)


def to_mate(x):
    pairs = [(a * 4 + z, (1 - a) * 4 + z) for a in (0, 1) for z in (1, 2)]
    return lax.ppermute(x, ("fsdp", "seq"), pairs)


def seed_swap(x, bit):
    return lax.ppermute(x, "seed", [(i, i ^ bit) for i in range(4)])


def hub_body(
    mel_frames,
    lengths,
    targets,
    frame_mask,
    stem_weight,
    conv_in_weight,
    conv_out_weight,
    depth_weight,
    head_weight,
    norm_gain,
):
    chip = lax.axis_index("seq")
    side = lax.axis_index("fsdp")
    seeds = lax.axis_size("seed")
    rows = targets.shape[1]
    width = stem_weight.shape[2]
    channels = depth_weight.shape[2]
    vocab = head_weight.shape[2]
    step = mel_frames.shape[1] // rows
    tile = rows // 2
    seed = lax.axis_index("seed")
    low = chip == 1
    is_hub = jnp.logical_or(low, chip == 2)

    first = conv_in_weight[0]
    blocks = mel_frames[0].reshape(rows, -1)
    deep_in = blocks.shape[1]
    share = rows // seeds
    stack = width // (-(-deep_in // LANES) * LANES)

    def widened(x, count):
        side = width // stack
        parts = jnp.pad(x, ((0, 0), (0, side - deep_in))).reshape(count, -1, side)
        return jnp.pad(jnp.concatenate(list(parts), axis=1), ((0, 0), (0, (stack - count) * side)))

    quarter = lax.dynamic_slice_in_dim(mel_frames[0], seed * share * step, share * step, 0).reshape(share, -1)
    margin = step * EDGE
    edge_out = jnp.where(low, mel_frames[0, -margin:], mel_frames[0, :margin]).reshape(EDGE, -1)
    far_first = along(first, BEYOND)
    near_first = along(jnp.concatenate([first, widened(quarter, stack)], axis=0), INWARD)
    hub_first = along(jnp.concatenate([first, widened(edge_out, 1)], axis=0), ACROSS)
    held = first.shape[0]
    edge = hub_first[held:, :deep_in]
    quarter_in = near_first[held:].reshape(share // stack, stack, -1).transpose(1, 0, 2).reshape(share, -1)
    quarter_in = quarter_in[:, :deep_in]

    pair = seed_swap(quarter_in, 1)
    odd = seed % 2 == 1
    pairs = jnp.concatenate([jnp.where(odd, pair, quarter_in), jnp.where(odd, quarter_in, pair)], axis=0)
    other = seed_swap(pairs, 2)
    upper = seed // 2 == 1
    outer = jnp.concatenate([jnp.where(upper, other, pairs), jnp.where(upper, pairs, other)], axis=0)

    groups = width // vocab
    head_rows = head_weight.shape[1]
    second = jnp.concatenate(
        [
            conv_out_weight[0],
            jnp.concatenate(jnp.split(head_weight[0], groups, axis=0), axis=1),
        ],
        axis=0,
    )
    slots = 4
    deep = tile + 2 * EDGE
    none = jnp.zeros_like(edge)
    frames = jnp.concatenate(
        [
            jnp.where(low, none, edge),
            jnp.where(low, outer, blocks),
            jnp.where(low, blocks, outer),
            jnp.where(low, edge, none),
            none[:1],
        ],
        axis=0,
    )
    pairs = jnp.concatenate([frames[:-1], frames[1:]], axis=1)
    main = pairs[EDGE : EDGE + slots * tile].reshape(slots, CHUNKS, tile // CHUNKS, -1)
    main = main.transpose(0, 2, 1, 3).reshape(slots, tile, -1)
    margins = jnp.stack(
        [
            jnp.concatenate([pairs[k * tile : k * tile + EDGE], pairs[(k + 1) * tile + EDGE : (k + 1) * tile + 2 * EDGE]])
            for k in range(slots)
        ]
    )

    length = lengths[0]
    positions = chip * rows + jnp.arange(rows, dtype=jnp.int32)
    counted = jnp.logical_and(frame_mask[0] > 0, positions < length)
    code = jnp.where(counted, targets[0], -1)
    starts = (chip - 1) * 2 * rows + tile * jnp.arange(slots, dtype=jnp.int32)
    alive = jnp.logical_and(is_hub, starts < length).astype(jnp.int32)
    hub = jnp.clip(chip, 1, 2)
    meta = jnp.concatenate(
        [
            starts,
            lengths,
            alive,
            jnp.stack([hub, 3 * (hub - 1), 3 - hub, 3 * (2 - hub), side, jnp.max(alive)]),
        ]
    ).astype(jnp.int32)

    gains = norm_gain[0]
    half = tile // 2
    stem_out, normed = call(
        stem_kernel,
        (slots,),
        [by_slot(main.shape[1:]), by_slot(margins.shape[1:]), whole(stem_weight.shape[1:]), whole(gains.shape)],
        [by_slot((tile, width)), by_slot((deep, width))],
        [
            jax.ShapeDtypeStruct((slots, tile, width), jnp.bfloat16),
            jax.ShapeDtypeStruct((slots, deep, width), jnp.bfloat16),
        ],
        [
            pltpu.VMEM((half, width), jnp.float32),
            pltpu.VMEM((half, width), jnp.float32),
            pltpu.VMEM((2 * EDGE, width), jnp.float32),
        ],
        2 * slots * deep * main.shape[2] * width,
        2 * slots * deep * (main.shape[2] + 2 * width),
        (meta, main, margins, stem_weight[0], gains),
    )
    pinned = pl.BlockSpec(memory_space=pltpu.HBM)

    outer_code = along(code, INWARD)
    codes = jnp.concatenate([jnp.where(low, outer_code, code), jnp.where(low, code, outer_code)])
    codes = codes.reshape(slots, CHUNKS, tile // CHUNKS)
    far_first, normed, codes = lax.optimization_barrier((far_first, normed, codes))
    mine = [first, near_first, hub_first, far_first]
    first_pieces = (*mine, *[to_mate(x) for x in mine])
    near_second, hub_second, far_second = [along(second, pairs_) for pairs_ in (INWARD, ACROSS, BEYOND)]
    taps = jnp.broadcast_to(
        depth_weight[0].astype(jnp.float32)[:, None, :], (depth_weight.shape[1], CHUNKS, channels)
    )
    extent = tile // CHUNKS + depth_weight.shape[1] - 1
    swished = call(
        conv_kernel,
        (slots,),
        [by_slot((deep, width)), whole(taps.shape)] + [pinned] * 8,
        by_slot((tile, channels)),
        jax.ShapeDtypeStruct((slots, tile, channels), jnp.bfloat16),
        [
            pltpu.VMEM((8 * held, width), jnp.bfloat16),
            pltpu.VMEM((deep, 2 * channels), jnp.float32),
            pltpu.VMEM((extent, CHUNKS, LANES), jnp.float32),
            pltpu.VMEM((extent, CHUNKS, LANES), jnp.float32),
            pltpu.VMEM((2 * EDGE, LANES), jnp.float32),
            pltpu.VMEM((deep, LANES), jnp.float32),
            pltpu.SemaphoreType.DMA((8,)),
        ],
        2 * slots * deep * width * 2 * channels,
        2 * slots * deep * width + 8 * first.size * 2,
        (meta, normed, taps, *first_pieces),
    )

    near_second, hub_second, far_second, swished = lax.optimization_barrier(
        (near_second, hub_second, far_second, swished)
    )
    mine = [second, near_second, hub_second, far_second]
    second_pieces = (*mine, to_mate(second), *[to_mate(x) for x in mine[1:]])
    errors = call(
        head_kernel,
        (slots,),
        [by_slot((tile, channels)), by_slot((tile, width)), by_slot(codes.shape[1:]), whole(gains.shape)]
        + [pinned] * 8,
        by_slot((CHUNKS, LANES)),
        jax.ShapeDtypeStruct((slots, CHUNKS, LANES), jnp.float32),
        [
            pltpu.VMEM((8 * conv_out_weight.shape[1], width), jnp.bfloat16),
            pltpu.VMEM((8 * head_rows, vocab), jnp.bfloat16),
            pltpu.VMEM((half, width), jnp.float32),
            pltpu.VMEM((half, width), jnp.float32),
            pltpu.VMEM((half, width), jnp.bfloat16),
            pltpu.VMEM((half, width), jnp.bfloat16),
            pltpu.VMEM((half, vocab), jnp.float32),
            pltpu.VMEM((half, vocab), jnp.float32),
            pltpu.SemaphoreType.DMA((8, 1 + groups)),
        ],
        2 * slots * tile * (channels + vocab) * width,
        2 * slots * tile * (channels + width),
        (meta, swished, stem_out, codes, gains, *second_pieces),
    )

    one, two, three = [seed_swap(errors, bit) for bit in (1, 2, 3)]
    total = ((errors + one) + (two + three)) / jnp.float32(seeds)
    total = total[:, :, : tile // CHUNKS].reshape(2, rows)
    part = jnp.sum(total).reshape(1)
    outer_half = jnp.where(low, total[0], total[1])
    own_half = jnp.where(low, total[1], total[0])
    from_hub = along(jnp.concatenate([outer_half, part]), OUTWARD)
    parts = [part[0], along(part, ACROSS)[0], along(part, OUT_BEYOND)[0], from_hub[rows]]
    frame_error = jnp.where(is_hub, own_half, from_hub[:rows])
    utt_score = ((parts[0] + parts[3]) + (parts[1] + parts[2])) / length.astype(jnp.float32)
    return (frame_error[None, :], utt_score.reshape(1))


def from_behind(x, axis, by):
    count = lax.axis_size(axis)
    pairs = [(i, i + by) for i in range(count) if 0 <= i + by < count]
    return lax.ppermute(x, axis, pairs)


def extended(x, sides, width):
    for axis, dim in sides:
        count, length = (lax.axis_size(axis), x.shape[dim])
        up = [(i, (i + 1) % count) for i in range(count - 1)]
        down = [(j, i) for i, j in up]
        last = lax.slice_in_dim(x, length - width, length, axis=dim)
        first = lax.slice_in_dim(x, 0, width, axis=dim)
        before = lax.ppermute(last, axis, up)
        after = lax.ppermute(first, axis, down)
        x = jnp.concatenate([before, x, after], axis=dim)
    return x


def layer_norm(values, gain_row):
    row_mean = jnp.mean(values, axis=-1, keepdims=True)
    centred = values - row_mean
    row_var = jnp.mean(centred * centred, axis=-1, keepdims=True)
    return (centred * lax.rsqrt(row_var + 1e-05) * gain_row).astype(jnp.bfloat16)


def block_product(left_rows, right_matrix):
    return jnp.dot(left_rows, right_matrix, preferred_element_type=jnp.float32)


def row_product(activations, shard_piece):
    return block_product(activations, shard_piece[0])


def body(
    mel_frames,
    lengths,
    targets,
    frame_mask,
    stem_weight,
    conv_in_weight,
    conv_out_weight,
    depth_weight,
    head_weight,
    norm_gain,
):
    frame_rows = targets.shape[1]
    blocks = mel_frames[0].reshape(frame_rows, -1)
    next_block = from_behind(blocks[:1], "seq", -1)
    following = jnp.concatenate([blocks[1:], next_block], 0)
    half_width = blocks.shape[1]
    stem_matrix = stem_weight[0]
    stem_out = (
        jnp.dot(blocks, stem_matrix[:half_width], preferred_element_type=jnp.float32)
        + jnp.dot(following, stem_matrix[half_width:], preferred_element_type=jnp.float32)
    ).astype(jnp.bfloat16)
    offset = lax.axis_index("seq") * frame_rows
    length = lengths[0]
    positions = offset + jnp.arange(frame_rows, dtype=jnp.int32)
    frame_live = positions < length
    gain_rows = norm_gain[0]
    normed_one = layer_norm(stem_out.astype(jnp.float32), gain_rows[0])
    tap_count = depth_weight.shape[1]
    channels = depth_weight.shape[2]
    halo_width = tap_count // 2
    conv_input = extended(normed_one, (("seq", 0),), halo_width)
    mixed_rows = row_product(
        conv_input, lax.all_gather(conv_in_weight, ("fsdp", "seq"), axis=1, tiled=True)
    )
    input_positions = offset - halo_width + jnp.arange(conv_input.shape[0], dtype=jnp.int32)
    input_live = jnp.logical_and(input_positions >= 0, input_positions < length)
    gated_rows = (
        mixed_rows[:, :channels]
        * jax.nn.sigmoid(mixed_rows[:, channels:])
        * input_live[:, None].astype(jnp.float32)
    ).astype(jnp.bfloat16)
    depthwise = jnp.zeros((frame_rows, channels), jnp.float32)
    for tap_index in range(tap_count):
        depthwise = depthwise + gated_rows[tap_index : tap_index + frame_rows].astype(
            jnp.float32
        ) * depth_weight[0, tap_index].astype(jnp.float32)
    swished = jax.nn.silu(depthwise).astype(jnp.bfloat16)
    conv_proj = row_product(
        swished, lax.all_gather(conv_out_weight, ("fsdp", "seq"), axis=1, tiled=True)
    )
    after_conv = stem_out.astype(jnp.float32) + conv_proj
    normed_two = layer_norm(after_conv, gain_rows[1])
    logits = row_product(
        normed_two, lax.all_gather(head_weight, ("fsdp", "seq"), axis=1, tiled=True)
    )
    posterior = jax.nn.softmax(logits, axis=-1)
    vocab_size = logits.shape[1]
    onehot = (jnp.arange(vocab_size, dtype=jnp.int32)[None, :] == targets[0][:, None]).astype(
        jnp.float32
    )
    differ = posterior - onehot
    frame_err = (
        jnp.sqrt(jnp.sum(differ * differ, axis=-1))
        * frame_live.astype(jnp.float32)
        * frame_mask[0].astype(jnp.float32)
    )
    seed_count = lax.axis_size("seed")
    frame_error = lax.psum(frame_err, "seed") / jnp.float32(seed_count)
    numerator = lax.psum(jnp.sum(frame_error), "seq")
    utt_score = numerator / length.astype(jnp.float32)
    return (frame_error[None, :], utt_score.reshape(1))


def solution(mesh):
    in_specs = (
        P("fsdp", "seq", None),
        P("fsdp"),
        P("fsdp", "seq"),
        P("fsdp", "seq"),
        P("seed", None, None),
        P("seed", ("fsdp", "seq"), None),
        P("seed", ("fsdp", "seq"), None),
        P("seed", None, None),
        P("seed", ("fsdp", "seq"), None),
        P("seed", None, None),
    )
    out_specs = (P("fsdp", "seq"), P("fsdp"))
    hubs = mesh.shape["seq"] == 4 and mesh.shape["fsdp"] == 2
    return jax.shard_map(
        hub_body if hubs else body, mesh=mesh, in_specs=in_specs, out_specs=out_specs, check_vma=False
    )
```

```python
import jax
import jax.numpy as jnp
from jax import lax
from jax.experimental import pallas as pl
from jax.experimental.pallas import tpu as pltpu
from jax.sharding import PartitionSpec as P

LANES = 128
CHUNKS = 8
EDGE = 16
VMEM_BYTES = 24 * 1024 * 1024


def norm_rows(values, gain_row):
    row_mean = jnp.mean(values, axis=-1, keepdims=True)
    centred = values - row_mean
    row_var = jnp.mean(centred * centred, axis=-1, keepdims=True)
    return (centred * lax.rsqrt(row_var + 1e-05) * gain_row).astype(jnp.bfloat16)


def sigmoid(x):
    return 0.5 * jnp.tanh(0.5 * x) + 0.5


def stem_kernel(
    meta, main_ref, margin_ref, stem_ref, gain_ref, stem_out_ref, normed_ref, acc_a, acc_b, acc_c
):
    slot = pl.program_id(0)
    frames = main_ref.shape[1]
    part = acc_a.shape[0]
    group = 16

    def norm(acc, at, keep):
        for row in range(0, acc.shape[0], group):
            stem_out = acc[row : row + group, :].astype(jnp.bfloat16)
            if keep:
                stem_out_ref[0, at + row : at + row + group, :] = stem_out
            normed_ref[0, at + row : at + row + group, :] = norm_rows(stem_out.astype(jnp.float32), gain_ref[0:1, :])

    @pl.when(meta[5 + slot] > 0)
    def _():
        for acc, left in ((acc_a, main_ref[0, :part, :]), (acc_b, main_ref[0, part:, :]), (acc_c, margin_ref[0])):
            acc[...] = jnp.dot(left, stem_ref[...], preferred_element_type=jnp.float32)
        norm(acc_a, 0, True)
        norm(acc_b, part, True)
        norm(acc_c, frames, False)


def shards(meta, pieces):
    side = meta[13]
    length = pieces[0].shape[0]
    places = [(pieces[i], 0) for i in range(5)] + [(pieces[5], i * length) for i in range(3)]
    return [(*place, (side if i < 4 else 1 - side) * 4 + meta[9 + i % 4]) for i, place in enumerate(places)]


def conv_kernel(meta, normed_ref, taps_ref, *rest):
    pieces = rest[:6]
    swished_ref, weight, mixed_a, mixed_b, gated, margin, mask, sems = rest[6:]
    slot = pl.program_id(0)
    rows = normed_ref.shape[1]
    frames = swished_ref.shape[1]
    channels = swished_ref.shape[2]
    tap_count = taps_ref.shape[0]
    reach = tap_count // 2
    piece = weight.shape[0] // 8
    run_length = frames // CHUNKS

    @pl.when(jnp.logical_and(pl.program_id(0) == 0, meta[14] > 0))
    def _():
        copies = [
            pltpu.make_async_copy(
                ref.at[pl.ds(at, piece)], weight.at[pl.ds(pl.multiple_of(block * piece, 16), piece)], sems.at[i]
            )
            for i, (ref, at, block) in enumerate(shards(meta, pieces))
        ]
        for copy in copies:
            copy.start()
        for copy in copies:
            copy.wait()

    @pl.when(meta[5 + slot] > 0)
    def _():
        row = lax.broadcasted_iota(jnp.int32, (rows, LANES), 0)
        inner = (row % CHUNKS) * run_length + row // CHUNKS
        outer = jnp.where(row < frames + EDGE, row - frames - EDGE, row - EDGE)
        at = meta[slot] + jnp.where(row < frames, inner, outer)
        mask[...] = jnp.logical_and(at >= 0, at < meta[4]).astype(jnp.float32)
        sublane = lax.broadcasted_iota(jnp.int32, (CHUNKS, LANES), 0)
        buffers = (mixed_a, mixed_b)

        def mix(block):
            low = block * LANES
            right = jnp.concatenate(
                [weight[:, low : low + LANES], weight[:, channels + low : channels + low + LANES]], axis=1
            )
            buffers[block % 2][...] = jnp.dot(normed_ref[0], right, preferred_element_type=jnp.float32)

        def gate(block):
            mixed = buffers[block % 2]
            group = 32
            for at in range(0, rows, group):
                here = slice(at, at + group)
                made = mixed[here, :LANES] * sigmoid(mixed[here, LANES:]) * mask[here, :]
                made = made.astype(jnp.bfloat16).astype(jnp.float32)
                if at < frames:
                    first = reach + at // CHUNKS
                    gated[first : first + group // CHUNKS] = made.reshape(group // CHUNKS, CHUNKS, LANES)
                else:
                    margin[...] = made
            for i in range(reach):
                before = pltpu.roll(gated[run_length + i], 1, 0)
                edge = margin[EDGE - reach + i : EDGE - reach + i + 1, :]
                gated[i] = jnp.where(sublane == 0, edge, before)
                after = pltpu.roll(gated[reach + i], CHUNKS - 1, 0)
                edge = margin[EDGE + i : EDGE + i + 1, :]
                gated[reach + run_length + i] = jnp.where(sublane == CHUNKS - 1, edge, after)

        def convolve(block):
            low = block * LANES
            run = 16
            for start in range(0, run_length, run):
                sums = [None] * run
                for at in range(start, start + run + tap_count - 1):
                    value = gated[at]
                    for m in range(max(start, at - tap_count + 1), min(start + run, at + 1)):
                        term = value * taps_ref[at - m, :, low : low + LANES]
                        k = m - start
                        sums[k] = term if sums[k] is None else sums[k] + term
                for k in range(0, run, 2):
                    total = jnp.concatenate(sums[k : k + 2], axis=0)
                    first = (start + k) * CHUNKS
                    swished_ref[0, first : first + 2 * CHUNKS, low : low + LANES] = (
                        total * sigmoid(total)
                    ).astype(jnp.bfloat16)

        blocks = channels // LANES
        mix(0)
        for block in range(blocks):
            if block + 1 < blocks:
                mix(block + 1)
            gate(block)
            convolve(block)


def head_kernel(meta, swished_ref, stem_out_ref, code_ref, gain_ref, *rest):
    pieces = rest[:6]
    error_ref, back, head, acc_a, acc_b, norm_a, norm_b, logit_a, logit_b, sems = rest[6:]
    slot = pl.program_id(0)
    frames = swished_ref.shape[1]
    vocab = head.shape[1]
    groups = back.shape[1] // vocab
    back_rows = back.shape[0] // 8
    head_rows = head.shape[0] // 8
    group_rows = head_rows // groups

    @pl.when(jnp.logical_and(pl.program_id(0) == 0, meta[14] > 0))
    def _():
        copies = []
        for i, (ref, at, block) in enumerate(shards(meta, pieces)):
            copies.append(
                pltpu.make_async_copy(
                    ref.at[pl.ds(at, back_rows)],
                    back.at[pl.ds(pl.multiple_of(block * back_rows, 16), back_rows)],
                    sems.at[i, 0],
                )
            )
            for g in range(groups):
                copies.append(
                    pltpu.make_async_copy(
                        ref.at[pl.ds(at + back_rows, group_rows), pl.ds(g * vocab, vocab)],
                        head.at[pl.ds(pl.multiple_of(block * head_rows + g * group_rows, 16), group_rows)],
                        sems.at[i, 1 + g],
                    )
                )
        for copy in copies:
            copy.start()
        for copy in copies:
            copy.wait()

    @pl.when(meta[5 + slot] <= 0)
    def _():
        error_ref[...] = jnp.zeros_like(error_ref)

    @pl.when(meta[5 + slot] > 0)
    def _():
        part = acc_a.shape[0]
        lane = lax.broadcasted_iota(jnp.int32, (CHUNKS, LANES), 1)
        def norm(at, acc, normed):
            group = 16
            for row in range(0, part, group):
                values = acc[row : row + group, :] + stem_out_ref[0, at + row : at + row + group, :].astype(jnp.float32)
                normed[row : row + group, :] = norm_rows(values, gain_ref[1:2, :])

        def errors(at, logits, row):
            group = 32
            token = lax.broadcasted_iota(jnp.int32, (group, vocab), 1)
            for first in range(0, part, group):
                scores = logits[first : first + group, :]
                grown = jnp.exp(scores - jnp.max(scores, axis=-1, keepdims=True))
                posterior = grown * (1.0 / jnp.sum(grown, axis=-1, keepdims=True))
                steps = range((at + first) // CHUNKS, (at + first + group) // CHUNKS)
                code = jnp.concatenate([code_ref[0, :, m : m + 1] for m in steps], axis=0)
                differ = posterior - (token == code).astype(jnp.float32)
                error = jnp.sqrt(jnp.sum(differ * differ, axis=-1, keepdims=True))
                error = jnp.where(code >= 0, error, 0.0)
                for k, m in enumerate(steps):
                    row = jnp.where(lane == m, error[k * CHUNKS : (k + 1) * CHUNKS, :], row)
            return row

        halves = ((0, acc_a, norm_a, logit_a), (part, acc_b, norm_b, logit_b))
        for at, acc, _, _ in halves:
            acc[...] = jnp.dot(swished_ref[0, at : at + part, :], back[...], preferred_element_type=jnp.float32)
        for at, acc, normed, logits in halves:
            norm(at, acc, normed)
            logits[...] = jnp.dot(normed[...], head[...], preferred_element_type=jnp.float32)
        row = jnp.zeros((CHUNKS, LANES), jnp.float32)
        for at, _, _, logits in halves:
            row = errors(at, logits, row)
        error_ref[0] = row


def call(kernel, grid, in_specs, out_specs, out_shape, scratch, flops, moved, operands):
    return pl.pallas_call(
        kernel,
        grid_spec=pltpu.PrefetchScalarGridSpec(
            num_scalar_prefetch=1,
            grid=grid,
            in_specs=in_specs,
            out_specs=out_specs,
            scratch_shapes=scratch,
        ),
        out_shape=out_shape,
        compiler_params=pltpu.CompilerParams(
            dimension_semantics=("arbitrary",), vmem_limit_bytes=VMEM_BYTES
        ),
        cost_estimate=pl.CostEstimate(flops=flops // 16, bytes_accessed=moved // 16, transcendentals=0),
    )(*operands)


def whole(shape):
    return pl.BlockSpec(shape, lambda i, meta: (0,) * len(shape))


def by_slot(shape):
    return pl.BlockSpec((1,) + shape, lambda i, meta: (i,) + (0,) * len(shape))


INWARD = [(0, 1), (3, 2)]
ACROSS = [(1, 2), (2, 1)]
BEYOND = [(0, 2), (3, 1)]
OUTWARD = [(1, 0), (2, 3)]
OUT_BEYOND = [(2, 0), (1, 3)]


def along(x, pairs):
    return lax.ppermute(x, "seq", pairs)


def to_mate(x):
    pairs = [(a * 4 + z, (1 - a) * 4 + z) for a in (0, 1) for z in (1, 2)]
    return lax.ppermute(x, ("fsdp", "seq"), pairs)


def seed_swap(x, bit):
    return lax.ppermute(x, "seed", [(i, i ^ bit) for i in range(4)])


def hub_body(
    mel_frames,
    lengths,
    targets,
    frame_mask,
    stem_weight,
    conv_in_weight,
    conv_out_weight,
    depth_weight,
    head_weight,
    norm_gain,
):
    chip = lax.axis_index("seq")
    side = lax.axis_index("fsdp")
    seeds = lax.axis_size("seed")
    rows = targets.shape[1]
    width = stem_weight.shape[2]
    channels = depth_weight.shape[2]
    vocab = head_weight.shape[2]
    step = mel_frames.shape[1] // rows
    tile = rows // 2
    seed = lax.axis_index("seed")
    low = chip == 1
    is_hub = jnp.logical_or(low, chip == 2)

    length = lengths[0]
    positions = chip * rows + jnp.arange(rows, dtype=jnp.int32)
    counted = jnp.logical_and(frame_mask[0] > 0, positions < length)
    code = jnp.where(counted, targets[0], -1)
    first = conv_in_weight[0]
    blocks = mel_frames[0].reshape(rows, -1)
    share = rows // seeds
    margin = step * EDGE
    quarter = lax.dynamic_slice_in_dim(mel_frames[0], seed * share * step, share * step, 0).reshape(share, -1)
    edge_out = jnp.where(low, mel_frames[0, -margin:], mel_frames[0, :margin]).reshape(EDGE, -1)
    quarter_in = along(quarter, INWARD)
    edge = along(edge_out, ACROSS)
    outer_code = along(code, INWARD)
    first_held, quarter_in, edge, outer_code = lax.optimization_barrier((first, quarter_in, edge, outer_code))
    near_first, hub_first, far_first = [along(first_held, pairs_) for pairs_ in (INWARD, ACROSS, BEYOND)]
    held = first.shape[0]

    pair = seed_swap(quarter_in, 1)
    odd = seed % 2 == 1
    pairs = jnp.concatenate([jnp.where(odd, pair, quarter_in), jnp.where(odd, quarter_in, pair)], axis=0)
    other = seed_swap(pairs, 2)
    upper = seed // 2 == 1
    outer = jnp.concatenate([jnp.where(upper, other, pairs), jnp.where(upper, pairs, other)], axis=0)

    groups = width // vocab
    head_rows = head_weight.shape[1]
    second = jnp.concatenate(
        [
            conv_out_weight[0],
            jnp.concatenate(jnp.split(head_weight[0], groups, axis=0), axis=1),
        ],
        axis=0,
    )
    slots = 4
    deep = tile + 2 * EDGE
    none = jnp.zeros_like(edge)
    frames = jnp.concatenate(
        [
            jnp.where(low, none, edge),
            jnp.where(low, outer, blocks),
            jnp.where(low, blocks, outer),
            jnp.where(low, edge, none),
            none,
        ],
        axis=0,
    )
    pairs = jnp.concatenate([frames[:-1], frames[1:]], axis=1)
    main = pairs[EDGE : EDGE + slots * tile].reshape(slots, CHUNKS, tile // CHUNKS, -1)
    main = main.transpose(0, 2, 1, 3).reshape(slots, tile, -1)
    margins = jnp.stack(
        [
            jnp.concatenate([pairs[k * tile : k * tile + EDGE], pairs[(k + 1) * tile + EDGE : (k + 1) * tile + 2 * EDGE]])
            for k in range(slots)
        ]
    )

    starts = (chip - 1) * 2 * rows + tile * jnp.arange(slots, dtype=jnp.int32)
    alive = jnp.logical_and(is_hub, starts < length).astype(jnp.int32)
    hub = jnp.clip(chip, 1, 2)
    meta = jnp.concatenate(
        [
            starts,
            lengths,
            alive,
            jnp.stack([hub, 3 * (hub - 1), 3 - hub, 3 * (2 - hub), side, jnp.max(alive)]),
        ]
    ).astype(jnp.int32)

    gains = norm_gain[0]
    half = tile // 2
    stem_out, normed = call(
        stem_kernel,
        (slots,),
        [by_slot(main.shape[1:]), by_slot(margins.shape[1:]), whole(stem_weight.shape[1:]), whole(gains.shape)],
        [by_slot((tile, width)), by_slot((deep, width))],
        [
            jax.ShapeDtypeStruct((slots, tile, width), jnp.bfloat16),
            jax.ShapeDtypeStruct((slots, deep, width), jnp.bfloat16),
        ],
        [
            pltpu.VMEM((half, width), jnp.float32),
            pltpu.VMEM((half, width), jnp.float32),
            pltpu.VMEM((2 * EDGE, width), jnp.float32),
        ],
        2 * slots * deep * main.shape[2] * width,
        2 * slots * deep * (main.shape[2] + 2 * width),
        (meta, main, margins, stem_weight[0], gains),
    )
    pinned = pl.BlockSpec(memory_space=pltpu.HBM)

    codes = jnp.concatenate([jnp.where(low, outer_code, code), jnp.where(low, code, outer_code)])
    codes = codes.reshape(slots, CHUNKS, tile // CHUNKS)
    far_first, normed, codes = lax.optimization_barrier((far_first, normed, codes))
    mine = [first, near_first, hub_first, far_first]
    first_pieces = (*mine, to_mate(first), to_mate(jnp.concatenate(mine[1:], axis=0)))
    near_second, hub_second, far_second = [along(second, pairs_) for pairs_ in (INWARD, ACROSS, BEYOND)]
    taps = jnp.broadcast_to(
        depth_weight[0].astype(jnp.float32)[:, None, :], (depth_weight.shape[1], CHUNKS, channels)
    )
    extent = tile // CHUNKS + depth_weight.shape[1] - 1
    swished = call(
        conv_kernel,
        (slots,),
        [by_slot((deep, width)), whole(taps.shape)] + [pinned] * 6,
        by_slot((tile, channels)),
        jax.ShapeDtypeStruct((slots, tile, channels), jnp.bfloat16),
        [
            pltpu.VMEM((8 * held, width), jnp.bfloat16),
            pltpu.VMEM((deep, 2 * LANES), jnp.float32),
            pltpu.VMEM((deep, 2 * LANES), jnp.float32),
            pltpu.VMEM((extent, CHUNKS, LANES), jnp.float32),
            pltpu.VMEM((2 * EDGE, LANES), jnp.float32),
            pltpu.VMEM((deep, LANES), jnp.float32),
            pltpu.SemaphoreType.DMA((8,)),
        ],
        2 * slots * deep * width * 2 * channels,
        2 * slots * deep * width + 8 * first.size * 2,
        (meta, normed, taps, *first_pieces),
    )

    near_second, hub_second, far_second, swished = lax.optimization_barrier(
        (near_second, hub_second, far_second, swished)
    )
    mine = [second, near_second, hub_second, far_second]
    second_pieces = (*mine, to_mate(second), to_mate(jnp.concatenate(mine[1:], axis=0)))
    errors = call(
        head_kernel,
        (slots,),
        [by_slot((tile, channels)), by_slot((tile, width)), by_slot(codes.shape[1:]), whole(gains.shape)]
        + [pinned] * 6,
        by_slot((CHUNKS, LANES)),
        jax.ShapeDtypeStruct((slots, CHUNKS, LANES), jnp.float32),
        [
            pltpu.VMEM((8 * conv_out_weight.shape[1], width), jnp.bfloat16),
            pltpu.VMEM((8 * head_rows, vocab), jnp.bfloat16),
            pltpu.VMEM((half, width), jnp.float32),
            pltpu.VMEM((half, width), jnp.float32),
            pltpu.VMEM((half, width), jnp.bfloat16),
            pltpu.VMEM((half, width), jnp.bfloat16),
            pltpu.VMEM((half, vocab), jnp.float32),
            pltpu.VMEM((half, vocab), jnp.float32),
            pltpu.SemaphoreType.DMA((8, 1 + groups)),
        ],
        2 * slots * tile * (channels + vocab) * width,
        2 * slots * tile * (channels + width),
        (meta, swished, stem_out, codes, gains, *second_pieces),
    )

    one, two, three = [seed_swap(errors, bit) for bit in (1, 2, 3)]
    total = ((errors + one) + (two + three)) / jnp.float32(seeds)
    total = total[:, :, : tile // CHUNKS].reshape(2, rows)
    part = jnp.sum(total).reshape(1)
    outer_half = jnp.where(low, total[0], total[1])
    own_half = jnp.where(low, total[1], total[0])
    from_hub = along(jnp.concatenate([outer_half, part]), OUTWARD)
    parts = [part[0], along(part, ACROSS)[0], along(part, OUT_BEYOND)[0], from_hub[rows]]
    frame_error = jnp.where(is_hub, own_half, from_hub[:rows])
    utt_score = ((parts[0] + parts[3]) + (parts[1] + parts[2])) / length.astype(jnp.float32)
    return (frame_error[None, :], utt_score.reshape(1))


def from_behind(x, axis, by):
    count = lax.axis_size(axis)
    pairs = [(i, i + by) for i in range(count) if 0 <= i + by < count]
    return lax.ppermute(x, axis, pairs)


def extended(x, sides, width):
    for axis, dim in sides:
        count, length = (lax.axis_size(axis), x.shape[dim])
        up = [(i, (i + 1) % count) for i in range(count - 1)]
        down = [(j, i) for i, j in up]
        last = lax.slice_in_dim(x, length - width, length, axis=dim)
        first = lax.slice_in_dim(x, 0, width, axis=dim)
        before = lax.ppermute(last, axis, up)
        after = lax.ppermute(first, axis, down)
        x = jnp.concatenate([before, x, after], axis=dim)
    return x


def layer_norm(values, gain_row):
    row_mean = jnp.mean(values, axis=-1, keepdims=True)
    centred = values - row_mean
    row_var = jnp.mean(centred * centred, axis=-1, keepdims=True)
    return (centred * lax.rsqrt(row_var + 1e-05) * gain_row).astype(jnp.bfloat16)


def block_product(left_rows, right_matrix):
    return jnp.dot(left_rows, right_matrix, preferred_element_type=jnp.float32)


def row_product(activations, shard_piece):
    return block_product(activations, shard_piece[0])


def body(
    mel_frames,
    lengths,
    targets,
    frame_mask,
    stem_weight,
    conv_in_weight,
    conv_out_weight,
    depth_weight,
    head_weight,
    norm_gain,
):
    frame_rows = targets.shape[1]
    blocks = mel_frames[0].reshape(frame_rows, -1)
    next_block = from_behind(blocks[:1], "seq", -1)
    following = jnp.concatenate([blocks[1:], next_block], 0)
    half_width = blocks.shape[1]
    stem_matrix = stem_weight[0]
    stem_out = (
        jnp.dot(blocks, stem_matrix[:half_width], preferred_element_type=jnp.float32)
        + jnp.dot(following, stem_matrix[half_width:], preferred_element_type=jnp.float32)
    ).astype(jnp.bfloat16)
    offset = lax.axis_index("seq") * frame_rows
    length = lengths[0]
    positions = offset + jnp.arange(frame_rows, dtype=jnp.int32)
    frame_live = positions < length
    gain_rows = norm_gain[0]
    normed_one = layer_norm(stem_out.astype(jnp.float32), gain_rows[0])
    tap_count = depth_weight.shape[1]
    channels = depth_weight.shape[2]
    halo_width = tap_count // 2
    conv_input = extended(normed_one, (("seq", 0),), halo_width)
    mixed_rows = row_product(
        conv_input, lax.all_gather(conv_in_weight, ("fsdp", "seq"), axis=1, tiled=True)
    )
    input_positions = offset - halo_width + jnp.arange(conv_input.shape[0], dtype=jnp.int32)
    input_live = jnp.logical_and(input_positions >= 0, input_positions < length)
    gated_rows = (
        mixed_rows[:, :channels]
        * jax.nn.sigmoid(mixed_rows[:, channels:])
        * input_live[:, None].astype(jnp.float32)
    ).astype(jnp.bfloat16)
    depthwise = jnp.zeros((frame_rows, channels), jnp.float32)
    for tap_index in range(tap_count):
        depthwise = depthwise + gated_rows[tap_index : tap_index + frame_rows].astype(
            jnp.float32
        ) * depth_weight[0, tap_index].astype(jnp.float32)
    swished = jax.nn.silu(depthwise).astype(jnp.bfloat16)
    conv_proj = row_product(
        swished, lax.all_gather(conv_out_weight, ("fsdp", "seq"), axis=1, tiled=True)
    )
    after_conv = stem_out.astype(jnp.float32) + conv_proj
    normed_two = layer_norm(after_conv, gain_rows[1])
    logits = row_product(
        normed_two, lax.all_gather(head_weight, ("fsdp", "seq"), axis=1, tiled=True)
    )
    posterior = jax.nn.softmax(logits, axis=-1)
    vocab_size = logits.shape[1]
    onehot = (jnp.arange(vocab_size, dtype=jnp.int32)[None, :] == targets[0][:, None]).astype(
        jnp.float32
    )
    differ = posterior - onehot
    frame_err = (
        jnp.sqrt(jnp.sum(differ * differ, axis=-1))
        * frame_live.astype(jnp.float32)
        * frame_mask[0].astype(jnp.float32)
    )
    seed_count = lax.axis_size("seed")
    frame_error = lax.psum(frame_err, "seed") / jnp.float32(seed_count)
    numerator = lax.psum(jnp.sum(frame_error), "seq")
    utt_score = numerator / length.astype(jnp.float32)
    return (frame_error[None, :], utt_score.reshape(1))


def solution(mesh):
    in_specs = (
        P("fsdp", "seq", None),
        P("fsdp"),
        P("fsdp", "seq"),
        P("fsdp", "seq"),
        P("seed", None, None),
        P("seed", ("fsdp", "seq"), None),
        P("seed", ("fsdp", "seq"), None),
        P("seed", None, None),
        P("seed", ("fsdp", "seq"), None),
        P("seed", None, None),
    )
    out_specs = (P("fsdp", "seq"), P("fsdp"))
    hubs = mesh.shape["seq"] == 4 and mesh.shape["fsdp"] == 2
    return jax.shard_map(
        hub_body if hubs else body, mesh=mesh, in_specs=in_specs, out_specs=out_specs, check_vma=False
    )
```

```python
import functools

import jax
import jax.numpy as jnp
from jax import lax
from jax.experimental import pallas as pl
from jax.experimental.pallas import tpu as pltpu
from jax.sharding import PartitionSpec as P

LANES = 128
CHUNKS = 8
EDGE = 16
VMEM_BYTES = 24 * 1024 * 1024


def norm_rows(values, gain_row):
    row_mean = jnp.mean(values, axis=-1, keepdims=True)
    centred = values - row_mean
    row_var = jnp.mean(centred * centred, axis=-1, keepdims=True)
    return (centred * lax.rsqrt(row_var + 1e-05) * gain_row).astype(jnp.bfloat16)


def sigmoid(x):
    return 0.5 * jnp.tanh(0.5 * x) + 0.5


def stem_kernel(
    first_slot, meta, main_ref, margin_ref, stem_ref, gain_ref, stem_out_ref, normed_ref, acc_a, acc_b, acc_c
):
    slot = pl.program_id(0) + first_slot
    frames = main_ref.shape[1]
    part = acc_a.shape[0]
    group = 16

    def norm(acc, at, keep):
        for row in range(0, acc.shape[0], group):
            stem_out = acc[row : row + group, :].astype(jnp.bfloat16)
            if keep:
                stem_out_ref[0, at + row : at + row + group, :] = stem_out
            normed_ref[0, at + row : at + row + group, :] = norm_rows(stem_out.astype(jnp.float32), gain_ref[0:1, :])

    @pl.when(meta[5 + slot] > 0)
    def _():
        for acc, left in ((acc_a, main_ref[0, :part, :]), (acc_b, main_ref[0, part:, :]), (acc_c, margin_ref[0])):
            acc[...] = jnp.dot(left, stem_ref[...], preferred_element_type=jnp.float32)
        norm(acc_a, 0, True)
        norm(acc_b, part, True)
        norm(acc_c, frames, False)


def shards(meta, pieces):
    side = meta[13]
    length = pieces[0].shape[0]
    places = [(piece, 0) for piece in pieces[:-1]]
    places += [(pieces[-1], i * length) for i in range(8 - len(places))]
    return [(*place, (side if i < 4 else 1 - side) * 4 + meta[9 + i % 4]) for i, place in enumerate(places)]


def conv_kernel(meta, own_ref, outer_ref, taps_ref, *rest):
    pieces = rest[:6]
    swished_ref, weight, mixed_a, mixed_b, gated, margin, mask, sems = rest[6:]
    slot = pl.program_id(0)
    rows = own_ref.shape[1]
    frames = swished_ref.shape[1]
    channels = swished_ref.shape[2]
    tap_count = taps_ref.shape[0]
    reach = tap_count // 2
    piece = weight.shape[0] // 8
    run_length = frames // CHUNKS

    @pl.when(jnp.logical_and(pl.program_id(0) == 0, meta[14] > 0))
    def _():
        copies = [
            pltpu.make_async_copy(
                ref.at[pl.ds(at, piece)], weight.at[pl.ds(pl.multiple_of(block * piece, 16), piece)], sems.at[i]
            )
            for i, (ref, at, block) in enumerate(shards(meta, pieces))
        ]
        for copy in copies:
            copy.start()
        for copy in copies:
            copy.wait()

    def run_tile(normed_ref):
        row = lax.broadcasted_iota(jnp.int32, (rows, LANES), 0)
        inner = (row % CHUNKS) * run_length + row // CHUNKS
        outer = jnp.where(row < frames + EDGE, row - frames - EDGE, row - EDGE)
        at = meta[slot] + jnp.where(row < frames, inner, outer)
        mask[...] = jnp.logical_and(at >= 0, at < meta[4]).astype(jnp.float32)
        sublane = lax.broadcasted_iota(jnp.int32, (CHUNKS, LANES), 0)
        buffers = (mixed_a, mixed_b)

        def mix(block):
            low = block * LANES
            right = jnp.concatenate(
                [weight[:, low : low + LANES], weight[:, channels + low : channels + low + LANES]], axis=1
            )
            buffers[block % 2][...] = jnp.dot(normed_ref[0], right, preferred_element_type=jnp.float32)

        def gate(block):
            mixed = buffers[block % 2]
            group = 32
            for at in range(0, rows, group):
                here = slice(at, at + group)
                made = mixed[here, :LANES] * sigmoid(mixed[here, LANES:]) * mask[here, :]
                made = made.astype(jnp.bfloat16).astype(jnp.float32)
                if at < frames:
                    first = reach + at // CHUNKS
                    gated[first : first + group // CHUNKS] = made.reshape(group // CHUNKS, CHUNKS, LANES)
                else:
                    margin[...] = made
            for i in range(reach):
                before = pltpu.roll(gated[run_length + i], 1, 0)
                edge = margin[EDGE - reach + i : EDGE - reach + i + 1, :]
                gated[i] = jnp.where(sublane == 0, edge, before)
                after = pltpu.roll(gated[reach + i], CHUNKS - 1, 0)
                edge = margin[EDGE + i : EDGE + i + 1, :]
                gated[reach + run_length + i] = jnp.where(sublane == CHUNKS - 1, edge, after)

        def convolve(block):
            low = block * LANES
            run = 16
            for start in range(0, run_length, run):
                sums = [None] * run
                for at in range(start, start + run + tap_count - 1):
                    value = gated[at]
                    for m in range(max(start, at - tap_count + 1), min(start + run, at + 1)):
                        term = value * taps_ref[at - m, :, low : low + LANES]
                        k = m - start
                        sums[k] = term if sums[k] is None else sums[k] + term
                for k in range(0, run, 2):
                    total = jnp.concatenate(sums[k : k + 2], axis=0)
                    first = (start + k) * CHUNKS
                    swished_ref[0, first : first + 2 * CHUNKS, low : low + LANES] = (
                        total * sigmoid(total)
                    ).astype(jnp.bfloat16)

        blocks = channels // LANES
        mix(0)
        for block in range(blocks):
            if block + 1 < blocks:
                mix(block + 1)
            gate(block)
            convolve(block)

    for is_own, normed_ref in ((True, own_ref), (False, outer_ref)):

        @pl.when(jnp.logical_and(meta[5 + slot] > 0, (slot < 2) == is_own))
        def _(normed_ref=normed_ref):
            run_tile(normed_ref)


def head_kernel(meta, swished_ref, own_stem, outer_stem, own_code, outer_code, gain_ref, *rest):
    pieces = rest[:5]
    error_ref, back, head, acc_a, acc_b, norm_a, norm_b, logit_a, logit_b, sems = rest[5:]
    slot = pl.program_id(0)
    frames = swished_ref.shape[1]
    vocab = head.shape[1]
    groups = back.shape[1] // vocab
    back_rows = back.shape[0] // 8
    head_rows = head.shape[0] // 8
    group_rows = head_rows // groups

    @pl.when(jnp.logical_and(pl.program_id(0) == 0, meta[14] > 0))
    def _():
        copies = []
        for i, (ref, at, block) in enumerate(shards(meta, pieces)):
            copies.append(
                pltpu.make_async_copy(
                    ref.at[pl.ds(at, back_rows)],
                    back.at[pl.ds(pl.multiple_of(block * back_rows, 16), back_rows)],
                    sems.at[i, 0],
                )
            )
            for g in range(groups):
                copies.append(
                    pltpu.make_async_copy(
                        ref.at[pl.ds(at + back_rows, group_rows), pl.ds(g * vocab, vocab)],
                        head.at[pl.ds(pl.multiple_of(block * head_rows + g * group_rows, 16), group_rows)],
                        sems.at[i, 1 + g],
                    )
                )
        for copy in copies:
            copy.start()
        for copy in copies:
            copy.wait()

    @pl.when(meta[5 + slot] <= 0)
    def _():
        error_ref[...] = jnp.zeros_like(error_ref)

    @pl.when(meta[5 + slot] > 0)
    def _():
        part = acc_a.shape[0]
        lane = lax.broadcasted_iota(jnp.int32, (CHUNKS, LANES), 1)
        is_own = slot < 2
        codes = jnp.where(is_own, own_code[0], outer_code[0])
        def norm(at, acc, normed):
            group = 16
            for row in range(0, part, group):
                here = slice(at + row, at + row + group)
                stem_out = [ref[0, here, :].astype(jnp.float32) for ref in (own_stem, outer_stem)]
                values = acc[row : row + group, :] + jnp.where(is_own, *stem_out)
                normed[row : row + group, :] = norm_rows(values, gain_ref[1:2, :])

        def errors(at, logits, row):
            group = 32
            token = lax.broadcasted_iota(jnp.int32, (group, vocab), 1)
            for first in range(0, part, group):
                scores = logits[first : first + group, :]
                grown = jnp.exp(scores - jnp.max(scores, axis=-1, keepdims=True))
                posterior = grown * (1.0 / jnp.sum(grown, axis=-1, keepdims=True))
                steps = range((at + first) // CHUNKS, (at + first + group) // CHUNKS)
                code = jnp.concatenate([codes[:, m : m + 1] for m in steps], axis=0)
                differ = posterior - (token == code).astype(jnp.float32)
                error = jnp.sqrt(jnp.sum(differ * differ, axis=-1, keepdims=True))
                error = jnp.where(code >= 0, error, 0.0)
                for k, m in enumerate(steps):
                    row = jnp.where(lane == m, error[k * CHUNKS : (k + 1) * CHUNKS, :], row)
            return row

        halves = ((0, acc_a, norm_a, logit_a), (part, acc_b, norm_b, logit_b))
        for at, acc, _, _ in halves:
            acc[...] = jnp.dot(swished_ref[0, at : at + part, :], back[...], preferred_element_type=jnp.float32)
        for at, acc, normed, logits in halves:
            norm(at, acc, normed)
            logits[...] = jnp.dot(normed[...], head[...], preferred_element_type=jnp.float32)
        row = jnp.zeros((CHUNKS, LANES), jnp.float32)
        for at, _, _, logits in halves:
            row = errors(at, logits, row)
        error_ref[0] = row


def call(kernel, grid, in_specs, out_specs, out_shape, scratch, flops, moved, operands):
    return pl.pallas_call(
        kernel,
        grid_spec=pltpu.PrefetchScalarGridSpec(
            num_scalar_prefetch=1,
            grid=grid,
            in_specs=in_specs,
            out_specs=out_specs,
            scratch_shapes=scratch,
        ),
        out_shape=out_shape,
        compiler_params=pltpu.CompilerParams(
            dimension_semantics=("arbitrary",), vmem_limit_bytes=VMEM_BYTES
        ),
        cost_estimate=pl.CostEstimate(flops=flops // 16, bytes_accessed=moved // 16, transcendentals=0),
    )(*operands)


def whole(shape):
    return pl.BlockSpec(shape, lambda i, meta: (0,) * len(shape))


def by_slot(shape):
    return pl.BlockSpec((1,) + shape, lambda i, meta: (i,) + (0,) * len(shape))


def own_slots(shape):
    return pl.BlockSpec((1,) + shape, lambda i, meta: (jnp.minimum(i, 1),) + (0,) * len(shape))


def outer_slots(shape):
    return pl.BlockSpec((1,) + shape, lambda i, meta: (jnp.maximum(i - 2, 0),) + (0,) * len(shape))


INWARD = [(0, 1), (3, 2)]
ACROSS = [(1, 2), (2, 1)]
BEYOND = [(0, 2), (3, 1)]
OUTWARD = [(1, 0), (2, 3)]
FORWARD = [(0, 1), (1, 2), (2, 3)]
BACKWARD = [(1, 0), (2, 1), (3, 2)]
OUT_BEYOND = [(2, 0), (1, 3)]


def along(x, pairs):
    return lax.ppermute(x, "seq", pairs)


def to_mate(x):
    pairs = [(a * 4 + z, (1 - a) * 4 + z) for a in (0, 1) for z in (1, 2)]
    return lax.ppermute(x, ("fsdp", "seq"), pairs)


def seed_swap(x, bit):
    return lax.ppermute(x, "seed", [(i, i ^ bit) for i in range(4)])


def hub_body(
    mel_frames,
    lengths,
    targets,
    frame_mask,
    stem_weight,
    conv_in_weight,
    conv_out_weight,
    depth_weight,
    head_weight,
    norm_gain,
):
    chip = lax.axis_index("seq")
    side = lax.axis_index("fsdp")
    seeds = lax.axis_size("seed")
    rows = targets.shape[1]
    width = stem_weight.shape[2]
    channels = depth_weight.shape[2]
    vocab = head_weight.shape[2]
    step = mel_frames.shape[1] // rows
    tile = rows // 2
    seed = lax.axis_index("seed")
    low = chip == 1
    is_hub = jnp.logical_or(low, chip == 2)

    length = lengths[0]
    positions = chip * rows + jnp.arange(rows, dtype=jnp.int32)
    counted = jnp.logical_and(frame_mask[0] > 0, positions < length)
    code = jnp.where(counted, targets[0], -1)
    first = conv_in_weight[0]
    blocks = mel_frames[0].reshape(rows, -1)
    share = rows // seeds
    margin = step * EDGE
    quarter = lax.dynamic_slice_in_dim(mel_frames[0], seed * share * step, share * step, 0).reshape(share, -1)
    quarter_in = along(quarter, INWARD)
    before = along(mel_frames[0, -margin:].reshape(EDGE, -1), FORWARD)
    after = along(mel_frames[0, :margin].reshape(EDGE, -1), BACKWARD)
    first_held, quarter_in, before, after = lax.optimization_barrier((first, quarter_in, before, after))
    near_first, hub_first, far_first = [along(first_held, pairs_) for pairs_ in (INWARD, ACROSS, BEYOND)]
    held = first.shape[0]
    code = code.reshape(2, CHUNKS, tile // CHUNKS)
    code_held, quarter_in = lax.optimization_barrier((code, quarter_in))
    outer_code = along(code_held, INWARD)

    pair = seed_swap(quarter_in, 1)
    odd = seed % 2 == 1
    pairs = jnp.concatenate([jnp.where(odd, pair, quarter_in), jnp.where(odd, quarter_in, pair)], axis=0)
    other = seed_swap(pairs, 2)
    upper = seed // 2 == 1
    outer = jnp.concatenate([jnp.where(upper, other, pairs), jnp.where(upper, pairs, other)], axis=0)

    groups = width // vocab
    head_rows = head_weight.shape[1]
    second = jnp.concatenate(
        [
            conv_out_weight[0],
            jnp.concatenate(jnp.split(head_weight[0], groups, axis=0), axis=1),
        ],
        axis=0,
    )
    slots = 4
    deep = tile + 2 * EDGE

    def paired(before, block, after):
        frames = jnp.concatenate([before, block, after, after], axis=0)
        pairs = jnp.concatenate([frames[:-1], frames[1:]], axis=1)
        main = pairs[EDGE : EDGE + 2 * tile].reshape(2, CHUNKS, tile // CHUNKS, -1)
        main = main.transpose(0, 2, 1, 3).reshape(2, tile, -1)
        sides = [
            jnp.concatenate([pairs[k * tile : k * tile + EDGE], pairs[(k + 1) * tile + EDGE : (k + 1) * tile + 2 * EDGE]])
            for k in range(2)
        ]
        return main, jnp.stack(sides)

    lone = jnp.where(low, 0, 3)
    starts = jnp.stack([chip * rows, chip * rows + tile, lone * rows, lone * rows + tile]).astype(jnp.int32)
    alive = jnp.logical_and(is_hub, starts < length).astype(jnp.int32)
    hub = jnp.clip(chip, 1, 2)
    meta = jnp.concatenate(
        [
            starts,
            lengths,
            alive,
            jnp.stack([hub, 3 * (hub - 1), 3 - hub, 3 * (2 - hub), side, jnp.max(alive)]),
        ]
    ).astype(jnp.int32)

    gains = norm_gain[0]
    half = tile // 2

    def stems(first_slot, main, sides):
        return call(
            functools.partial(stem_kernel, first_slot),
            (2,),
            [by_slot(main.shape[1:]), by_slot(sides.shape[1:]), whole(stem_weight.shape[1:]), whole(gains.shape)],
            [by_slot((tile, width)), by_slot((deep, width))],
            [
                jax.ShapeDtypeStruct((2, tile, width), jnp.bfloat16),
                jax.ShapeDtypeStruct((2, deep, width), jnp.bfloat16),
            ],
            [
                pltpu.VMEM((half, width), jnp.float32),
                pltpu.VMEM((half, width), jnp.float32),
                pltpu.VMEM((2 * EDGE, width), jnp.float32),
            ],
            slots * deep * main.shape[2] * width,
            slots * deep * (main.shape[2] + 2 * width),
            (meta, main, sides, stem_weight[0], gains),
        )

    own_stem, own_normed = stems(0, *paired(before, blocks, after))
    none = jnp.zeros_like(before)
    outer_pairs = paired(jnp.where(low, none, blocks[-EDGE:]), outer, jnp.where(low, blocks[:EDGE], none))
    first_mate = to_mate(first)
    outer_pairs, first_mate, own_normed = lax.optimization_barrier((outer_pairs, first_mate, own_normed))
    outer_stem, outer_normed = stems(2, *outer_pairs)
    pinned = pl.BlockSpec(memory_space=pltpu.HBM)

    far_first, outer_normed = lax.optimization_barrier((far_first, outer_normed))
    mine = [first, near_first, hub_first, far_first]
    first_pieces = (*mine, first_mate, to_mate(jnp.concatenate(mine[1:], axis=0)))
    near_second, hub_second, far_second = [along(second, pairs_) for pairs_ in (INWARD, ACROSS, BEYOND)]
    taps = jnp.broadcast_to(
        depth_weight[0].astype(jnp.float32)[:, None, :], (depth_weight.shape[1], CHUNKS, channels)
    )
    extent = tile // CHUNKS + depth_weight.shape[1] - 1
    swished = call(
        conv_kernel,
        (slots,),
        [own_slots((deep, width)), outer_slots((deep, width)), whole(taps.shape)] + [pinned] * 6,
        by_slot((tile, channels)),
        jax.ShapeDtypeStruct((slots, tile, channels), jnp.bfloat16),
        [
            pltpu.VMEM((8 * held, width), jnp.bfloat16),
            pltpu.VMEM((deep, 2 * LANES), jnp.float32),
            pltpu.VMEM((deep, 2 * LANES), jnp.float32),
            pltpu.VMEM((extent, CHUNKS, LANES), jnp.float32),
            pltpu.VMEM((2 * EDGE, LANES), jnp.float32),
            pltpu.VMEM((deep, LANES), jnp.float32),
            pltpu.SemaphoreType.DMA((8,)),
        ],
        2 * slots * deep * width * 2 * channels,
        2 * slots * deep * width + 8 * first.size * 2,
        (meta, own_normed, outer_normed, taps, *first_pieces),
    )

    near_second, hub_second, far_second, swished = lax.optimization_barrier(
        (near_second, hub_second, far_second, swished)
    )
    mine = [second, near_second, hub_second, far_second]
    second_pieces = (*mine, to_mate(jnp.concatenate(mine, axis=0)))
    errors = call(
        head_kernel,
        (slots,),
        [by_slot((tile, channels)), own_slots((tile, width)), outer_slots((tile, width))]
        + [own_slots(code.shape[1:]), outer_slots(code.shape[1:]), whole(gains.shape)]
        + [pinned] * 5,
        by_slot((CHUNKS, LANES)),
        jax.ShapeDtypeStruct((slots, CHUNKS, LANES), jnp.float32),
        [
            pltpu.VMEM((8 * conv_out_weight.shape[1], width), jnp.bfloat16),
            pltpu.VMEM((8 * head_rows, vocab), jnp.bfloat16),
            pltpu.VMEM((half, width), jnp.float32),
            pltpu.VMEM((half, width), jnp.float32),
            pltpu.VMEM((half, width), jnp.bfloat16),
            pltpu.VMEM((half, width), jnp.bfloat16),
            pltpu.VMEM((half, vocab), jnp.float32),
            pltpu.VMEM((half, vocab), jnp.float32),
            pltpu.SemaphoreType.DMA((8, 1 + groups)),
        ],
        2 * slots * tile * (channels + vocab) * width,
        2 * slots * tile * (channels + width),
        (meta, swished, own_stem, outer_stem, code, outer_code, gains, *second_pieces),
    )

    one, two, three = [seed_swap(errors, bit) for bit in (1, 2, 3)]
    total = ((errors + one) + (two + three)) / jnp.float32(seeds)
    total = total[:, :, : tile // CHUNKS].reshape(2, rows)
    part = jnp.sum(total).reshape(1)
    own_half, outer_half = total
    from_hub = along(jnp.concatenate([outer_half, part]), OUTWARD)
    parts = [part[0], along(part, ACROSS)[0], along(part, OUT_BEYOND)[0], from_hub[rows]]
    frame_error = jnp.where(is_hub, own_half, from_hub[:rows])
    utt_score = ((parts[0] + parts[3]) + (parts[1] + parts[2])) / length.astype(jnp.float32)
    return (frame_error[None, :], utt_score.reshape(1))


def from_behind(x, axis, by):
    count = lax.axis_size(axis)
    pairs = [(i, i + by) for i in range(count) if 0 <= i + by < count]
    return lax.ppermute(x, axis, pairs)


def extended(x, sides, width):
    for axis, dim in sides:
        count, length = (lax.axis_size(axis), x.shape[dim])
        up = [(i, (i + 1) % count) for i in range(count - 1)]
        down = [(j, i) for i, j in up]
        last = lax.slice_in_dim(x, length - width, length, axis=dim)
        first = lax.slice_in_dim(x, 0, width, axis=dim)
        before = lax.ppermute(last, axis, up)
        after = lax.ppermute(first, axis, down)
        x = jnp.concatenate([before, x, after], axis=dim)
    return x


def layer_norm(values, gain_row):
    row_mean = jnp.mean(values, axis=-1, keepdims=True)
    centred = values - row_mean
    row_var = jnp.mean(centred * centred, axis=-1, keepdims=True)
    return (centred * lax.rsqrt(row_var + 1e-05) * gain_row).astype(jnp.bfloat16)


def block_product(left_rows, right_matrix):
    return jnp.dot(left_rows, right_matrix, preferred_element_type=jnp.float32)


def row_product(activations, shard_piece):
    return block_product(activations, shard_piece[0])


def body(
    mel_frames,
    lengths,
    targets,
    frame_mask,
    stem_weight,
    conv_in_weight,
    conv_out_weight,
    depth_weight,
    head_weight,
    norm_gain,
):
    frame_rows = targets.shape[1]
    blocks = mel_frames[0].reshape(frame_rows, -1)
    next_block = from_behind(blocks[:1], "seq", -1)
    following = jnp.concatenate([blocks[1:], next_block], 0)
    half_width = blocks.shape[1]
    stem_matrix = stem_weight[0]
    stem_out = (
        jnp.dot(blocks, stem_matrix[:half_width], preferred_element_type=jnp.float32)
        + jnp.dot(following, stem_matrix[half_width:], preferred_element_type=jnp.float32)
    ).astype(jnp.bfloat16)
    offset = lax.axis_index("seq") * frame_rows
    length = lengths[0]
    positions = offset + jnp.arange(frame_rows, dtype=jnp.int32)
    frame_live = positions < length
    gain_rows = norm_gain[0]
    normed_one = layer_norm(stem_out.astype(jnp.float32), gain_rows[0])
    tap_count = depth_weight.shape[1]
    channels = depth_weight.shape[2]
    halo_width = tap_count // 2
    conv_input = extended(normed_one, (("seq", 0),), halo_width)
    mixed_rows = row_product(
        conv_input, lax.all_gather(conv_in_weight, ("fsdp", "seq"), axis=1, tiled=True)
    )
    input_positions = offset - halo_width + jnp.arange(conv_input.shape[0], dtype=jnp.int32)
    input_live = jnp.logical_and(input_positions >= 0, input_positions < length)
    gated_rows = (
        mixed_rows[:, :channels]
        * jax.nn.sigmoid(mixed_rows[:, channels:])
        * input_live[:, None].astype(jnp.float32)
    ).astype(jnp.bfloat16)
    depthwise = jnp.zeros((frame_rows, channels), jnp.float32)
    for tap_index in range(tap_count):
        depthwise = depthwise + gated_rows[tap_index : tap_index + frame_rows].astype(
            jnp.float32
        ) * depth_weight[0, tap_index].astype(jnp.float32)
    swished = jax.nn.silu(depthwise).astype(jnp.bfloat16)
    conv_proj = row_product(
        swished, lax.all_gather(conv_out_weight, ("fsdp", "seq"), axis=1, tiled=True)
    )
    after_conv = stem_out.astype(jnp.float32) + conv_proj
    normed_two = layer_norm(after_conv, gain_rows[1])
    logits = row_product(
        normed_two, lax.all_gather(head_weight, ("fsdp", "seq"), axis=1, tiled=True)
    )
    posterior = jax.nn.softmax(logits, axis=-1)
    vocab_size = logits.shape[1]
    onehot = (jnp.arange(vocab_size, dtype=jnp.int32)[None, :] == targets[0][:, None]).astype(
        jnp.float32
    )
    differ = posterior - onehot
    frame_err = (
        jnp.sqrt(jnp.sum(differ * differ, axis=-1))
        * frame_live.astype(jnp.float32)
        * frame_mask[0].astype(jnp.float32)
    )
    seed_count = lax.axis_size("seed")
    frame_error = lax.psum(frame_err, "seed") / jnp.float32(seed_count)
    numerator = lax.psum(jnp.sum(frame_error), "seq")
    utt_score = numerator / length.astype(jnp.float32)
    return (frame_error[None, :], utt_score.reshape(1))


def solution(mesh):
    in_specs = (
        P("fsdp", "seq", None),
        P("fsdp"),
        P("fsdp", "seq"),
        P("fsdp", "seq"),
        P("seed", None, None),
        P("seed", ("fsdp", "seq"), None),
        P("seed", ("fsdp", "seq"), None),
        P("seed", None, None),
        P("seed", ("fsdp", "seq"), None),
        P("seed", None, None),
    )
    out_specs = (P("fsdp", "seq"), P("fsdp"))
    hubs = mesh.shape["seq"] == 4 and mesh.shape["fsdp"] == 2
    return jax.shard_map(
        hub_body if hubs else body, mesh=mesh, in_specs=in_specs, out_specs=out_specs, check_vma=False
    )
```

```python
import jax
import jax.numpy as jnp
from jax import lax
from jax.experimental import pallas as pl
from jax.experimental.pallas import tpu as pltpu
from jax.sharding import PartitionSpec as P

LANES = 128
CHUNKS = 8
EDGE = 16
VMEM_BYTES = 24 * 1024 * 1024


def norm_rows(values, gain_row):
    row_mean = jnp.mean(values, axis=-1, keepdims=True)
    centred = values - row_mean
    row_var = jnp.mean(centred * centred, axis=-1, keepdims=True)
    return (centred * lax.rsqrt(row_var + 1e-05) * gain_row).astype(jnp.bfloat16)


def sigmoid(x):
    return 0.5 * jnp.tanh(0.5 * x) + 0.5


def stem_kernel(
    meta, main_ref, margin_ref, stem_ref, gain_ref, stem_out_ref, normed_ref, acc_a, acc_b, acc_c
):
    slot = pl.program_id(0)
    frames = main_ref.shape[1]
    part = acc_a.shape[0]
    group = 16

    def norm(acc, at, keep):
        for row in range(0, acc.shape[0], group):
            stem_out = acc[row : row + group, :].astype(jnp.bfloat16)
            if keep:
                stem_out_ref[0, at + row : at + row + group, :] = stem_out
            normed_ref[0, at + row : at + row + group, :] = norm_rows(stem_out.astype(jnp.float32), gain_ref[0:1, :])

    @pl.when(meta[5 + slot] > 0)
    def _():
        for acc, left in ((acc_a, main_ref[0, :part, :]), (acc_b, main_ref[0, part:, :]), (acc_c, margin_ref[0])):
            acc[...] = jnp.dot(left, stem_ref[...], preferred_element_type=jnp.float32)
        norm(acc_a, 0, True)
        norm(acc_b, part, True)
        norm(acc_c, frames, False)


def shards(meta, pieces):
    side = meta[13]
    length = pieces[0].shape[0]
    places = [(piece, 0) for piece in pieces[:-1]]
    places += [(pieces[-1], i * length) for i in range(8 - len(places))]
    return [(*place, (side if i < 4 else 1 - side) * 4 + meta[9 + i % 4]) for i, place in enumerate(places)]


def conv_kernel(meta, normed_ref, taps_ref, *rest):
    pieces = rest[:5]
    swished_ref, weight, mixed_a, mixed_b, gated, margin, mask, sems = rest[5:]
    slot = pl.program_id(0)
    rows = normed_ref.shape[1]
    frames = swished_ref.shape[1]
    channels = swished_ref.shape[2]
    tap_count = taps_ref.shape[0]
    reach = tap_count // 2
    piece = weight.shape[0] // 8
    run_length = frames // CHUNKS

    @pl.when(jnp.logical_and(pl.program_id(0) == 0, meta[14] > 0))
    def _():
        copies = [
            pltpu.make_async_copy(
                ref.at[pl.ds(at, piece)], weight.at[pl.ds(pl.multiple_of(block * piece, 16), piece)], sems.at[i]
            )
            for i, (ref, at, block) in enumerate(shards(meta, pieces))
        ]
        for copy in copies:
            copy.start()
        for copy in copies:
            copy.wait()

    @pl.when(meta[5 + slot] > 0)
    def _():
        row = lax.broadcasted_iota(jnp.int32, (rows, LANES), 0)
        inner = (row % CHUNKS) * run_length + row // CHUNKS
        outer = jnp.where(row < frames + EDGE, row - frames - EDGE, row - EDGE)
        at = meta[slot] + jnp.where(row < frames, inner, outer)
        mask[...] = jnp.logical_and(at >= 0, at < meta[4]).astype(jnp.float32)
        sublane = lax.broadcasted_iota(jnp.int32, (CHUNKS, LANES), 0)
        buffers = (mixed_a, mixed_b)

        def mix(block):
            low = block * LANES
            right = jnp.concatenate(
                [weight[:, low : low + LANES], weight[:, channels + low : channels + low + LANES]], axis=1
            )
            buffers[block % 2][...] = jnp.dot(normed_ref[0], right, preferred_element_type=jnp.float32)

        def gate(block):
            mixed = buffers[block % 2]
            group = 32
            for at in range(0, rows, group):
                here = slice(at, at + group)
                made = mixed[here, :LANES] * sigmoid(mixed[here, LANES:]) * mask[here, :]
                made = made.astype(jnp.bfloat16).astype(jnp.float32)
                if at < frames:
                    first = reach + at // CHUNKS
                    gated[first : first + group // CHUNKS] = made.reshape(group // CHUNKS, CHUNKS, LANES)
                else:
                    margin[...] = made
            for i in range(reach):
                before = pltpu.roll(gated[run_length + i], 1, 0)
                edge = margin[EDGE - reach + i : EDGE - reach + i + 1, :]
                gated[i] = jnp.where(sublane == 0, edge, before)
                after = pltpu.roll(gated[reach + i], CHUNKS - 1, 0)
                edge = margin[EDGE + i : EDGE + i + 1, :]
                gated[reach + run_length + i] = jnp.where(sublane == CHUNKS - 1, edge, after)

        def convolve(block):
            low = block * LANES
            run = 16
            for start in range(0, run_length, run):
                sums = [None] * run
                for at in range(start, start + run + tap_count - 1):
                    value = gated[at]
                    for m in range(max(start, at - tap_count + 1), min(start + run, at + 1)):
                        term = value * taps_ref[at - m, :, low : low + LANES]
                        k = m - start
                        sums[k] = term if sums[k] is None else sums[k] + term
                for k in range(0, run, 2):
                    total = jnp.concatenate(sums[k : k + 2], axis=0)
                    first = (start + k) * CHUNKS
                    swished_ref[0, first : first + 2 * CHUNKS, low : low + LANES] = (
                        total * sigmoid(total)
                    ).astype(jnp.bfloat16)

        blocks = channels // LANES
        mix(0)
        for block in range(blocks):
            if block + 1 < blocks:
                mix(block + 1)
            gate(block)
            convolve(block)


def head_kernel(meta, swished_ref, stem_out_ref, code_ref, gain_ref, *rest):
    pieces = rest[:6]
    error_ref, back, head, acc_a, acc_b, norm_a, norm_b, logit_a, logit_b, sems = rest[6:]
    slot = pl.program_id(0)
    frames = swished_ref.shape[1]
    vocab = head.shape[1]
    groups = back.shape[1] // vocab
    back_rows = back.shape[0] // 8
    head_rows = head.shape[0] // 8
    group_rows = head_rows // groups

    @pl.when(jnp.logical_and(pl.program_id(0) == 0, meta[14] > 0))
    def _():
        copies = []
        for i, (ref, at, block) in enumerate(shards(meta, pieces)):
            copies.append(
                pltpu.make_async_copy(
                    ref.at[pl.ds(at, back_rows)],
                    back.at[pl.ds(pl.multiple_of(block * back_rows, 16), back_rows)],
                    sems.at[i, 0],
                )
            )
            for g in range(groups):
                copies.append(
                    pltpu.make_async_copy(
                        ref.at[pl.ds(at + back_rows, group_rows), pl.ds(g * vocab, vocab)],
                        head.at[pl.ds(pl.multiple_of(block * head_rows + g * group_rows, 16), group_rows)],
                        sems.at[i, 1 + g],
                    )
                )
        for copy in copies:
            copy.start()
        for copy in copies:
            copy.wait()

    @pl.when(meta[5 + slot] <= 0)
    def _():
        error_ref[...] = jnp.zeros_like(error_ref)

    @pl.when(meta[5 + slot] > 0)
    def _():
        part = acc_a.shape[0]
        lane = lax.broadcasted_iota(jnp.int32, (CHUNKS, LANES), 1)
        def norm(at, acc, normed):
            group = 16
            for row in range(0, part, group):
                values = acc[row : row + group, :] + stem_out_ref[0, at + row : at + row + group, :].astype(jnp.float32)
                normed[row : row + group, :] = norm_rows(values, gain_ref[1:2, :])

        def errors(at, logits, row):
            group = 32
            token = lax.broadcasted_iota(jnp.int32, (group, vocab), 1)
            for first in range(0, part, group):
                scores = logits[first : first + group, :]
                grown = jnp.exp(scores - jnp.max(scores, axis=-1, keepdims=True))
                posterior = grown * (1.0 / jnp.sum(grown, axis=-1, keepdims=True))
                steps = range((at + first) // CHUNKS, (at + first + group) // CHUNKS)
                code = jnp.concatenate([code_ref[0, :, m : m + 1] for m in steps], axis=0)
                differ = posterior - (token == code).astype(jnp.float32)
                error = jnp.sqrt(jnp.sum(differ * differ, axis=-1, keepdims=True))
                error = jnp.where(code >= 0, error, 0.0)
                for k, m in enumerate(steps):
                    row = jnp.where(lane == m, error[k * CHUNKS : (k + 1) * CHUNKS, :], row)
            return row

        halves = ((0, acc_a, norm_a, logit_a), (part, acc_b, norm_b, logit_b))
        for at, acc, _, _ in halves:
            acc[...] = jnp.dot(swished_ref[0, at : at + part, :], back[...], preferred_element_type=jnp.float32)
        for at, acc, normed, logits in halves:
            norm(at, acc, normed)
            logits[...] = jnp.dot(normed[...], head[...], preferred_element_type=jnp.float32)
        row = jnp.zeros((CHUNKS, LANES), jnp.float32)
        for at, _, _, logits in halves:
            row = errors(at, logits, row)
        error_ref[0] = row


def call(kernel, grid, in_specs, out_specs, out_shape, scratch, flops, moved, operands):
    return pl.pallas_call(
        kernel,
        grid_spec=pltpu.PrefetchScalarGridSpec(
            num_scalar_prefetch=1,
            grid=grid,
            in_specs=in_specs,
            out_specs=out_specs,
            scratch_shapes=scratch,
        ),
        out_shape=out_shape,
        compiler_params=pltpu.CompilerParams(
            dimension_semantics=("arbitrary",), vmem_limit_bytes=VMEM_BYTES
        ),
        cost_estimate=pl.CostEstimate(flops=flops // 16, bytes_accessed=moved // 16, transcendentals=0),
    )(*operands)


def whole(shape):
    return pl.BlockSpec(shape, lambda i, meta: (0,) * len(shape))


def by_slot(shape):
    return pl.BlockSpec((1,) + shape, lambda i, meta: (i,) + (0,) * len(shape))


INWARD = [(0, 1), (3, 2)]
ACROSS = [(1, 2), (2, 1)]
BEYOND = [(0, 2), (3, 1)]
OUTWARD = [(1, 0), (2, 3)]
OUT_BEYOND = [(2, 0), (1, 3)]


def along(x, pairs):
    return lax.ppermute(x, "seq", pairs)


def to_mate(x):
    pairs = [(a * 4 + z, (1 - a) * 4 + z) for a in (0, 1) for z in (1, 2)]
    return lax.ppermute(x, ("fsdp", "seq"), pairs)


def seed_swap(x, bit):
    return lax.ppermute(x, "seed", [(i, i ^ bit) for i in range(4)])


def hub_body(
    mel_frames,
    lengths,
    targets,
    frame_mask,
    stem_weight,
    conv_in_weight,
    conv_out_weight,
    depth_weight,
    head_weight,
    norm_gain,
):
    chip = lax.axis_index("seq")
    side = lax.axis_index("fsdp")
    seeds = lax.axis_size("seed")
    rows = targets.shape[1]
    width = stem_weight.shape[2]
    channels = depth_weight.shape[2]
    vocab = head_weight.shape[2]
    step = mel_frames.shape[1] // rows
    tile = rows // 2
    seed = lax.axis_index("seed")
    low = chip == 1
    is_hub = jnp.logical_or(low, chip == 2)

    first = conv_in_weight[0]
    share = rows // seeds
    margin = step * EDGE
    quarter = lax.dynamic_slice_in_dim(mel_frames[0], seed * share * step, share * step, 0).reshape(share, -1)
    edge_out = jnp.where(low, mel_frames[0, -margin:], mel_frames[0, :margin]).reshape(EDGE, -1)
    quarter_in = along(quarter, INWARD)
    edge = along(edge_out, ACROSS)
    first_held, quarter_in, edge, mel_frames, lengths = lax.optimization_barrier(
        (first, quarter_in, edge, mel_frames, lengths)
    )
    near_first, hub_first, far_first = [along(first_held, pairs_) for pairs_ in (INWARD, ACROSS, BEYOND)]
    held = first.shape[0]
    blocks = mel_frames[0].reshape(rows, -1)

    pair, targets, frame_mask = lax.optimization_barrier((seed_swap(quarter_in, 1), targets, frame_mask))
    odd = seed % 2 == 1
    pairs = jnp.concatenate([jnp.where(odd, pair, quarter_in), jnp.where(odd, quarter_in, pair)], axis=0)
    other = seed_swap(pairs, 2)
    upper = seed // 2 == 1
    outer = jnp.concatenate([jnp.where(upper, other, pairs), jnp.where(upper, pairs, other)], axis=0)

    groups = width // vocab
    head_rows = head_weight.shape[1]
    second = jnp.concatenate(
        [
            conv_out_weight[0],
            jnp.concatenate(jnp.split(head_weight[0], groups, axis=0), axis=1),
        ],
        axis=0,
    )
    slots = 4
    deep = tile + 2 * EDGE
    none = jnp.zeros_like(edge)
    frames = jnp.concatenate(
        [
            jnp.where(low, none, edge),
            jnp.where(low, outer, blocks),
            jnp.where(low, blocks, outer),
            jnp.where(low, edge, none),
            none,
        ],
        axis=0,
    )
    pairs = jnp.concatenate([frames[:-1], frames[1:]], axis=1)
    main = pairs[EDGE : EDGE + slots * tile].reshape(slots, CHUNKS, tile // CHUNKS, -1)
    main = main.transpose(0, 2, 1, 3).reshape(slots, tile, -1)
    margins = jnp.stack(
        [
            jnp.concatenate([pairs[k * tile : k * tile + EDGE], pairs[(k + 1) * tile + EDGE : (k + 1) * tile + 2 * EDGE]])
            for k in range(slots)
        ]
    )

    length = lengths[0]
    positions = chip * rows + jnp.arange(rows, dtype=jnp.int32)
    counted = jnp.logical_and(frame_mask[0] > 0, positions < length)
    code = jnp.where(counted, targets[0], -1).reshape(2, CHUNKS, tile // CHUNKS)

    starts = (chip - 1) * 2 * rows + tile * jnp.arange(slots, dtype=jnp.int32)
    alive = jnp.logical_and(is_hub, starts < length).astype(jnp.int32)
    hub = jnp.clip(chip, 1, 2)
    meta = jnp.concatenate(
        [
            starts,
            lengths,
            alive,
            jnp.stack([hub, 3 * (hub - 1), 3 - hub, 3 * (2 - hub), side, jnp.max(alive)]),
        ]
    ).astype(jnp.int32)

    taps = jnp.broadcast_to(
        depth_weight[0].astype(jnp.float32)[:, None, :], (depth_weight.shape[1], CHUNKS, channels)
    )
    main, margins, code, second, taps = lax.optimization_barrier((main, margins, code, second, taps))
    gains = norm_gain[0]
    half = tile // 2
    stem_out, normed = call(
        stem_kernel,
        (slots,),
        [by_slot(main.shape[1:]), by_slot(margins.shape[1:]), whole(stem_weight.shape[1:]), whole(gains.shape)],
        [by_slot((tile, width)), by_slot((deep, width))],
        [
            jax.ShapeDtypeStruct((slots, tile, width), jnp.bfloat16),
            jax.ShapeDtypeStruct((slots, deep, width), jnp.bfloat16),
        ],
        [
            pltpu.VMEM((half, width), jnp.float32),
            pltpu.VMEM((half, width), jnp.float32),
            pltpu.VMEM((2 * EDGE, width), jnp.float32),
        ],
        2 * slots * deep * main.shape[2] * width,
        2 * slots * deep * (main.shape[2] + 2 * width),
        (meta, main, margins, stem_weight[0], gains),
    )
    pinned = pl.BlockSpec(memory_space=pltpu.HBM)

    far_first, normed = lax.optimization_barrier((far_first, normed))
    mine = [first, near_first, hub_first, far_first]
    first_pieces = (*mine, to_mate(jnp.concatenate(mine, axis=0)))
    near_second, hub_second, far_second = [along(second, pairs_) for pairs_ in (INWARD, ACROSS, BEYOND)]
    extent = tile // CHUNKS + depth_weight.shape[1] - 1
    swished = call(
        conv_kernel,
        (slots,),
        [by_slot((deep, width)), whole(taps.shape)] + [pinned] * 5,
        by_slot((tile, channels)),
        jax.ShapeDtypeStruct((slots, tile, channels), jnp.bfloat16),
        [
            pltpu.VMEM((8 * held, width), jnp.bfloat16),
            pltpu.VMEM((deep, 2 * LANES), jnp.float32),
            pltpu.VMEM((deep, 2 * LANES), jnp.float32),
            pltpu.VMEM((extent, CHUNKS, LANES), jnp.float32),
            pltpu.VMEM((2 * EDGE, LANES), jnp.float32),
            pltpu.VMEM((deep, LANES), jnp.float32),
            pltpu.SemaphoreType.DMA((8,)),
        ],
        2 * slots * deep * width * 2 * channels,
        2 * slots * deep * width + 8 * first.size * 2,
        (meta, normed, taps, *first_pieces),
    )

    near_second, hub_second, far_second, code, swished = lax.optimization_barrier(
        (near_second, hub_second, far_second, code, swished)
    )
    outer_code = along(code, INWARD)
    codes = jnp.concatenate([jnp.where(low, outer_code, code), jnp.where(low, code, outer_code)])
    mine = [second, near_second, hub_second, far_second]
    second_pieces = (*mine, to_mate(second), to_mate(jnp.concatenate(mine[1:], axis=0)))
    errors = call(
        head_kernel,
        (slots,),
        [by_slot((tile, channels)), by_slot((tile, width)), by_slot(codes.shape[1:]), whole(gains.shape)]
        + [pinned] * 6,
        by_slot((CHUNKS, LANES)),
        jax.ShapeDtypeStruct((slots, CHUNKS, LANES), jnp.float32),
        [
            pltpu.VMEM((8 * conv_out_weight.shape[1], width), jnp.bfloat16),
            pltpu.VMEM((8 * head_rows, vocab), jnp.bfloat16),
            pltpu.VMEM((half, width), jnp.float32),
            pltpu.VMEM((half, width), jnp.float32),
            pltpu.VMEM((half, width), jnp.bfloat16),
            pltpu.VMEM((half, width), jnp.bfloat16),
            pltpu.VMEM((half, vocab), jnp.float32),
            pltpu.VMEM((half, vocab), jnp.float32),
            pltpu.SemaphoreType.DMA((8, 1 + groups)),
        ],
        2 * slots * tile * (channels + vocab) * width,
        2 * slots * tile * (channels + width),
        (meta, swished, stem_out, codes, gains, *second_pieces),
    )

    one, two, three = [seed_swap(errors, bit) for bit in (1, 2, 3)]
    total = ((errors + one) + (two + three)) / jnp.float32(seeds)
    total = total[:, :, : tile // CHUNKS].reshape(2, rows)
    part = jnp.sum(total).reshape(1)
    outer_half = jnp.where(low, total[0], total[1])
    own_half = jnp.where(low, total[1], total[0])
    from_hub = along(jnp.concatenate([outer_half, part]), OUTWARD)
    parts = [part[0], along(part, ACROSS)[0], along(part, OUT_BEYOND)[0], from_hub[rows]]
    frame_error = jnp.where(is_hub, own_half, from_hub[:rows])
    utt_score = ((parts[0] + parts[3]) + (parts[1] + parts[2])) / length.astype(jnp.float32)
    return (frame_error[None, :], utt_score.reshape(1))


def from_behind(x, axis, by):
    count = lax.axis_size(axis)
    pairs = [(i, i + by) for i in range(count) if 0 <= i + by < count]
    return lax.ppermute(x, axis, pairs)


def extended(x, sides, width):
    for axis, dim in sides:
        count, length = (lax.axis_size(axis), x.shape[dim])
        up = [(i, (i + 1) % count) for i in range(count - 1)]
        down = [(j, i) for i, j in up]
        last = lax.slice_in_dim(x, length - width, length, axis=dim)
        first = lax.slice_in_dim(x, 0, width, axis=dim)
        before = lax.ppermute(last, axis, up)
        after = lax.ppermute(first, axis, down)
        x = jnp.concatenate([before, x, after], axis=dim)
    return x


def layer_norm(values, gain_row):
    row_mean = jnp.mean(values, axis=-1, keepdims=True)
    centred = values - row_mean
    row_var = jnp.mean(centred * centred, axis=-1, keepdims=True)
    return (centred * lax.rsqrt(row_var + 1e-05) * gain_row).astype(jnp.bfloat16)


def block_product(left_rows, right_matrix):
    return jnp.dot(left_rows, right_matrix, preferred_element_type=jnp.float32)


def row_product(activations, shard_piece):
    return block_product(activations, shard_piece[0])


def body(
    mel_frames,
    lengths,
    targets,
    frame_mask,
    stem_weight,
    conv_in_weight,
    conv_out_weight,
    depth_weight,
    head_weight,
    norm_gain,
):
    frame_rows = targets.shape[1]
    blocks = mel_frames[0].reshape(frame_rows, -1)
    next_block = from_behind(blocks[:1], "seq", -1)
    following = jnp.concatenate([blocks[1:], next_block], 0)
    half_width = blocks.shape[1]
    stem_matrix = stem_weight[0]
    stem_out = (
        jnp.dot(blocks, stem_matrix[:half_width], preferred_element_type=jnp.float32)
        + jnp.dot(following, stem_matrix[half_width:], preferred_element_type=jnp.float32)
    ).astype(jnp.bfloat16)
    offset = lax.axis_index("seq") * frame_rows
    length = lengths[0]
    positions = offset + jnp.arange(frame_rows, dtype=jnp.int32)
    frame_live = positions < length
    gain_rows = norm_gain[0]
    normed_one = layer_norm(stem_out.astype(jnp.float32), gain_rows[0])
    tap_count = depth_weight.shape[1]
    channels = depth_weight.shape[2]
    halo_width = tap_count // 2
    conv_input = extended(normed_one, (("seq", 0),), halo_width)
    mixed_rows = row_product(
        conv_input, lax.all_gather(conv_in_weight, ("fsdp", "seq"), axis=1, tiled=True)
    )
    input_positions = offset - halo_width + jnp.arange(conv_input.shape[0], dtype=jnp.int32)
    input_live = jnp.logical_and(input_positions >= 0, input_positions < length)
    gated_rows = (
        mixed_rows[:, :channels]
        * jax.nn.sigmoid(mixed_rows[:, channels:])
        * input_live[:, None].astype(jnp.float32)
    ).astype(jnp.bfloat16)
    depthwise = jnp.zeros((frame_rows, channels), jnp.float32)
    for tap_index in range(tap_count):
        depthwise = depthwise + gated_rows[tap_index : tap_index + frame_rows].astype(
            jnp.float32
        ) * depth_weight[0, tap_index].astype(jnp.float32)
    swished = jax.nn.silu(depthwise).astype(jnp.bfloat16)
    conv_proj = row_product(
        swished, lax.all_gather(conv_out_weight, ("fsdp", "seq"), axis=1, tiled=True)
    )
    after_conv = stem_out.astype(jnp.float32) + conv_proj
    normed_two = layer_norm(after_conv, gain_rows[1])
    logits = row_product(
        normed_two, lax.all_gather(head_weight, ("fsdp", "seq"), axis=1, tiled=True)
    )
    posterior = jax.nn.softmax(logits, axis=-1)
    vocab_size = logits.shape[1]
    onehot = (jnp.arange(vocab_size, dtype=jnp.int32)[None, :] == targets[0][:, None]).astype(
        jnp.float32
    )
    differ = posterior - onehot
    frame_err = (
        jnp.sqrt(jnp.sum(differ * differ, axis=-1))
        * frame_live.astype(jnp.float32)
        * frame_mask[0].astype(jnp.float32)
    )
    seed_count = lax.axis_size("seed")
    frame_error = lax.psum(frame_err, "seed") / jnp.float32(seed_count)
    numerator = lax.psum(jnp.sum(frame_error), "seq")
    utt_score = numerator / length.astype(jnp.float32)
    return (frame_error[None, :], utt_score.reshape(1))


def solution(mesh):
    in_specs = (
        P("fsdp", "seq", None),
        P("fsdp"),
        P("fsdp", "seq"),
        P("fsdp", "seq"),
        P("seed", None, None),
        P("seed", ("fsdp", "seq"), None),
        P("seed", ("fsdp", "seq"), None),
        P("seed", None, None),
        P("seed", ("fsdp", "seq"), None),
        P("seed", None, None),
    )
    out_specs = (P("fsdp", "seq"), P("fsdp"))
    hubs = mesh.shape["seq"] == 4 and mesh.shape["fsdp"] == 2
    return jax.shard_map(
        hub_body if hubs else body, mesh=mesh, in_specs=in_specs, out_specs=out_specs, check_vma=False
    )
```

```python
import jax
import jax.numpy as jnp
from jax import lax
from jax.experimental import pallas as pl
from jax.experimental.pallas import tpu as pltpu
from jax.sharding import PartitionSpec as P

LANES = 128
CHUNKS = 8
EDGE = 16
VMEM_BYTES = 24 * 1024 * 1024


def norm_rows(values, gain_row):
    row_mean = jnp.mean(values, axis=-1, keepdims=True)
    centred = values - row_mean
    row_var = jnp.mean(centred * centred, axis=-1, keepdims=True)
    return (centred * lax.rsqrt(row_var + 1e-05) * gain_row).astype(jnp.bfloat16)


def sigmoid(x):
    return 0.5 * jnp.tanh(0.5 * x) + 0.5


def stem_kernel(
    meta, main_ref, margin_ref, stem_ref, gain_ref, stem_out_ref, normed_ref, acc_a, acc_b, acc_c
):
    slot = pl.program_id(0)
    frames = main_ref.shape[1]
    part = acc_a.shape[0]
    group = 16

    def norm(acc, at, keep):
        for row in range(0, acc.shape[0], group):
            stem_out = acc[row : row + group, :].astype(jnp.bfloat16)
            if keep:
                stem_out_ref[0, at + row : at + row + group, :] = stem_out
            normed_ref[0, at + row : at + row + group, :] = norm_rows(stem_out.astype(jnp.float32), gain_ref[0:1, :])

    @pl.when(meta[5 + slot] > 0)
    def _():
        for acc, left in ((acc_a, main_ref[0, :part, :]), (acc_b, main_ref[0, part:, :]), (acc_c, margin_ref[0])):
            acc[...] = jnp.dot(left, stem_ref[...], preferred_element_type=jnp.float32)
        norm(acc_a, 0, True)
        norm(acc_b, part, True)
        norm(acc_c, frames, False)


def shards(meta, pieces):
    side = meta[13]
    length = pieces[0].shape[0]
    places = [(piece, 0) for piece in pieces[:-1]]
    places += [(pieces[-1], i * length) for i in range(8 - len(places))]
    return [(*place, (side if i < 4 else 1 - side) * 4 + meta[9 + i % 4]) for i, place in enumerate(places)]


def conv_kernel(meta, normed_ref, taps_ref, *rest):
    pieces = rest[:5]
    swished_ref, weight, mixed_a, mixed_b, gated, margin, mask, sems = rest[5:]
    slot = pl.program_id(0)
    rows = normed_ref.shape[1]
    frames = swished_ref.shape[1]
    channels = swished_ref.shape[2]
    tap_count = taps_ref.shape[0]
    reach = tap_count // 2
    piece = weight.shape[0] // 8
    run_length = frames // CHUNKS

    @pl.when(jnp.logical_and(pl.program_id(0) == 0, meta[14] > 0))
    def _():
        copies = [
            pltpu.make_async_copy(
                ref.at[pl.ds(at, piece)], weight.at[pl.ds(pl.multiple_of(block * piece, 16), piece)], sems.at[i]
            )
            for i, (ref, at, block) in enumerate(shards(meta, pieces))
        ]
        for copy in copies:
            copy.start()
        for copy in copies:
            copy.wait()

    @pl.when(meta[5 + slot] > 0)
    def _():
        row = lax.broadcasted_iota(jnp.int32, (rows, LANES), 0)
        inner = (row % CHUNKS) * run_length + row // CHUNKS
        outer = jnp.where(row < frames + EDGE, row - frames - EDGE, row - EDGE)
        at = meta[slot] + jnp.where(row < frames, inner, outer)
        mask[...] = jnp.logical_and(at >= 0, at < meta[4]).astype(jnp.float32)
        sublane = lax.broadcasted_iota(jnp.int32, (CHUNKS, LANES), 0)
        buffers = (mixed_a, mixed_b)

        def mix(block):
            low = block * LANES
            right = jnp.concatenate(
                [weight[:, low : low + LANES], weight[:, channels + low : channels + low + LANES]], axis=1
            )
            buffers[block % 2][...] = jnp.dot(normed_ref[0], right, preferred_element_type=jnp.float32)

        def gate(block):
            mixed = buffers[block % 2]
            group = 32
            for at in range(0, rows, group):
                here = slice(at, at + group)
                made = mixed[here, :LANES] * sigmoid(mixed[here, LANES:]) * mask[here, :]
                made = made.astype(jnp.bfloat16).astype(jnp.float32)
                if at < frames:
                    first = reach + at // CHUNKS
                    gated[first : first + group // CHUNKS] = made.reshape(group // CHUNKS, CHUNKS, LANES)
                else:
                    margin[...] = made
            for i in range(reach):
                before = pltpu.roll(gated[run_length + i], 1, 0)
                edge = margin[EDGE - reach + i : EDGE - reach + i + 1, :]
                gated[i] = jnp.where(sublane == 0, edge, before)
                after = pltpu.roll(gated[reach + i], CHUNKS - 1, 0)
                edge = margin[EDGE + i : EDGE + i + 1, :]
                gated[reach + run_length + i] = jnp.where(sublane == CHUNKS - 1, edge, after)

        def convolve(block):
            low = block * LANES
            run = 16
            for start in range(0, run_length, run):
                sums = [None] * run
                for at in range(start, start + run + tap_count - 1):
                    value = gated[at]
                    for m in range(max(start, at - tap_count + 1), min(start + run, at + 1)):
                        term = value * taps_ref[at - m, :, low : low + LANES]
                        k = m - start
                        sums[k] = term if sums[k] is None else sums[k] + term
                for k in range(0, run, 2):
                    total = jnp.concatenate(sums[k : k + 2], axis=0)
                    first = (start + k) * CHUNKS
                    swished_ref[0, first : first + 2 * CHUNKS, low : low + LANES] = (
                        total * sigmoid(total)
                    ).astype(jnp.bfloat16)

        blocks = channels // LANES
        mix(0)
        for block in range(blocks):
            if block + 1 < blocks:
                mix(block + 1)
            gate(block)
            convolve(block)


def head_kernel(meta, swished_ref, stem_out_ref, code_ref, gain_ref, *rest):
    pieces = rest[:6]
    error_ref, back, head, acc_a, acc_b, norm_a, norm_b, logit_a, logit_b, sems = rest[6:]
    slot = pl.program_id(0)
    frames = swished_ref.shape[1]
    vocab = head.shape[1]
    groups = back.shape[1] // vocab
    back_rows = back.shape[0] // 8
    head_rows = head.shape[0] // 8
    group_rows = head_rows // groups

    @pl.when(jnp.logical_and(pl.program_id(0) == 0, meta[14] > 0))
    def _():
        copies = []
        for i, (ref, at, block) in enumerate(shards(meta, pieces)):
            copies.append(
                pltpu.make_async_copy(
                    ref.at[pl.ds(at, back_rows)],
                    back.at[pl.ds(pl.multiple_of(block * back_rows, 16), back_rows)],
                    sems.at[i, 0],
                )
            )
            for g in range(groups):
                copies.append(
                    pltpu.make_async_copy(
                        ref.at[pl.ds(at + back_rows, group_rows), pl.ds(g * vocab, vocab)],
                        head.at[pl.ds(pl.multiple_of(block * head_rows + g * group_rows, 16), group_rows)],
                        sems.at[i, 1 + g],
                    )
                )
        for copy in copies:
            copy.start()
        for copy in copies:
            copy.wait()

    @pl.when(meta[5 + slot] <= 0)
    def _():
        error_ref[...] = jnp.zeros_like(error_ref)

    @pl.when(meta[5 + slot] > 0)
    def _():
        part = acc_a.shape[0]
        lane = lax.broadcasted_iota(jnp.int32, (CHUNKS, LANES), 1)
        def norm(at, acc, normed):
            group = 16
            for row in range(0, part, group):
                values = acc[row : row + group, :] + stem_out_ref[0, at + row : at + row + group, :].astype(jnp.float32)
                normed[row : row + group, :] = norm_rows(values, gain_ref[1:2, :])

        def errors(at, logits, row):
            group = 32
            token = lax.broadcasted_iota(jnp.int32, (group, vocab), 1)
            for first in range(0, part, group):
                scores = logits[first : first + group, :]
                grown = jnp.exp(scores - jnp.max(scores, axis=-1, keepdims=True))
                posterior = grown * (1.0 / jnp.sum(grown, axis=-1, keepdims=True))
                steps = range((at + first) // CHUNKS, (at + first + group) // CHUNKS)
                code = jnp.concatenate([code_ref[0, :, m : m + 1] for m in steps], axis=0)
                differ = posterior - (token == code).astype(jnp.float32)
                error = jnp.sqrt(jnp.sum(differ * differ, axis=-1, keepdims=True))
                error = jnp.where(code >= 0, error, 0.0)
                for k, m in enumerate(steps):
                    row = jnp.where(lane == m, error[k * CHUNKS : (k + 1) * CHUNKS, :], row)
            return row

        halves = ((0, acc_a, norm_a, logit_a), (part, acc_b, norm_b, logit_b))
        for at, acc, _, _ in halves:
            acc[...] = jnp.dot(swished_ref[0, at : at + part, :], back[...], preferred_element_type=jnp.float32)
        for at, acc, normed, logits in halves:
            norm(at, acc, normed)
            logits[...] = jnp.dot(normed[...], head[...], preferred_element_type=jnp.float32)
        row = jnp.zeros((CHUNKS, LANES), jnp.float32)
        for at, _, _, logits in halves:
            row = errors(at, logits, row)
        error_ref[0] = row


def call(kernel, grid, in_specs, out_specs, out_shape, scratch, flops, moved, operands):
    return pl.pallas_call(
        kernel,
        grid_spec=pltpu.PrefetchScalarGridSpec(
            num_scalar_prefetch=1,
            grid=grid,
            in_specs=in_specs,
            out_specs=out_specs,
            scratch_shapes=scratch,
        ),
        out_shape=out_shape,
        compiler_params=pltpu.CompilerParams(
            dimension_semantics=("arbitrary",), vmem_limit_bytes=VMEM_BYTES
        ),
        cost_estimate=pl.CostEstimate(flops=flops // 16, bytes_accessed=moved // 16, transcendentals=0),
    )(*operands)


def whole(shape):
    return pl.BlockSpec(shape, lambda i, meta: (0,) * len(shape))


def by_slot(shape):
    return pl.BlockSpec((1,) + shape, lambda i, meta: (i,) + (0,) * len(shape))


INWARD = [(0, 1), (3, 2)]
ACROSS = [(1, 2), (2, 1)]
BEYOND = [(0, 2), (3, 1)]
OUTWARD = [(1, 0), (2, 3)]
OUT_BEYOND = [(2, 0), (1, 3)]


def along(x, pairs):
    return lax.ppermute(x, "seq", pairs)


def to_mate(x):
    pairs = [(a * 4 + z, (1 - a) * 4 + z) for a in (0, 1) for z in (1, 2)]
    return lax.ppermute(x, ("fsdp", "seq"), pairs)


def seed_swap(x, bit):
    return lax.ppermute(x, "seed", [(i, i ^ bit) for i in range(4)])


def hub_body(
    mel_frames,
    lengths,
    targets,
    frame_mask,
    stem_weight,
    conv_in_weight,
    conv_out_weight,
    depth_weight,
    head_weight,
    norm_gain,
):
    chip = lax.axis_index("seq")
    side = lax.axis_index("fsdp")
    seeds = lax.axis_size("seed")
    rows = targets.shape[1]
    width = stem_weight.shape[2]
    channels = depth_weight.shape[2]
    vocab = head_weight.shape[2]
    step = mel_frames.shape[1] // rows
    tile = rows // 2
    seed = lax.axis_index("seed")
    low = chip == 1
    is_hub = jnp.logical_or(low, chip == 2)

    first = conv_in_weight[0]
    share = rows // seeds
    margin = step * EDGE
    quarter = lax.dynamic_slice_in_dim(mel_frames[0], seed * share * step, share * step, 0).reshape(share, -1)
    edge_out = jnp.where(low, mel_frames[0, -margin:], mel_frames[0, :margin]).reshape(EDGE, -1)
    quarter_in = along(quarter, INWARD)
    edge = along(edge_out, ACROSS)
    first_held, quarter_in, edge = lax.optimization_barrier((first, quarter_in, edge))
    near_first, hub_first, far_first = [along(first_held, pairs_) for pairs_ in (INWARD, ACROSS, BEYOND)]
    held = first.shape[0]
    blocks = mel_frames[0].reshape(rows, -1)

    pair, targets, frame_mask = lax.optimization_barrier((seed_swap(quarter_in, 1), targets, frame_mask))
    odd = seed % 2 == 1
    pairs = jnp.concatenate([jnp.where(odd, pair, quarter_in), jnp.where(odd, quarter_in, pair)], axis=0)
    other = seed_swap(pairs, 2)
    upper = seed // 2 == 1
    outer = jnp.concatenate([jnp.where(upper, other, pairs), jnp.where(upper, pairs, other)], axis=0)

    groups = width // vocab
    head_rows = head_weight.shape[1]
    second = jnp.concatenate(
        [
            conv_out_weight[0],
            jnp.concatenate(jnp.split(head_weight[0], groups, axis=0), axis=1),
        ],
        axis=0,
    )
    slots = 4
    deep = tile + 2 * EDGE
    none = jnp.zeros_like(edge)
    frames = jnp.concatenate(
        [
            jnp.where(low, none, edge),
            jnp.where(low, outer, blocks),
            jnp.where(low, blocks, outer),
            jnp.where(low, edge, none),
            none,
        ],
        axis=0,
    )
    pairs = jnp.concatenate([frames[:-1], frames[1:]], axis=1)
    main = pairs[EDGE : EDGE + slots * tile].reshape(slots, CHUNKS, tile // CHUNKS, -1)
    main = main.transpose(0, 2, 1, 3).reshape(slots, tile, -1)
    margins = jnp.stack(
        [
            jnp.concatenate([pairs[k * tile : k * tile + EDGE], pairs[(k + 1) * tile + EDGE : (k + 1) * tile + 2 * EDGE]])
            for k in range(slots)
        ]
    )

    length = lengths[0]
    positions = chip * rows + jnp.arange(rows, dtype=jnp.int32)
    counted = jnp.logical_and(frame_mask[0] > 0, positions < length)
    code = jnp.where(counted, targets[0], -1).reshape(2, CHUNKS, tile // CHUNKS)

    starts = (chip - 1) * 2 * rows + tile * jnp.arange(slots, dtype=jnp.int32)
    alive = jnp.logical_and(is_hub, starts < length).astype(jnp.int32)
    hub = jnp.clip(chip, 1, 2)
    meta = jnp.concatenate(
        [
            starts,
            lengths,
            alive,
            jnp.stack([hub, 3 * (hub - 1), 3 - hub, 3 * (2 - hub), side, jnp.max(alive)]),
        ]
    ).astype(jnp.int32)

    taps = jnp.broadcast_to(
        depth_weight[0].astype(jnp.float32)[:, None, :], (depth_weight.shape[1], CHUNKS, channels)
    )
    main, margins, code = lax.optimization_barrier((main, margins, code))
    gains = norm_gain[0]
    half = tile // 2
    stem_out, normed = call(
        stem_kernel,
        (slots,),
        [by_slot(main.shape[1:]), by_slot(margins.shape[1:]), whole(stem_weight.shape[1:]), whole(gains.shape)],
        [by_slot((tile, width)), by_slot((deep, width))],
        [
            jax.ShapeDtypeStruct((slots, tile, width), jnp.bfloat16),
            jax.ShapeDtypeStruct((slots, deep, width), jnp.bfloat16),
        ],
        [
            pltpu.VMEM((half, width), jnp.float32),
            pltpu.VMEM((half, width), jnp.float32),
            pltpu.VMEM((2 * EDGE, width), jnp.float32),
        ],
        2 * slots * deep * main.shape[2] * width,
        2 * slots * deep * (main.shape[2] + 2 * width),
        (meta, main, margins, stem_weight[0], gains),
    )
    pinned = pl.BlockSpec(memory_space=pltpu.HBM)

    far_first, normed = lax.optimization_barrier((far_first, normed))
    mine = [first, near_first, hub_first, far_first]
    first_pieces = (*mine, to_mate(jnp.concatenate(mine, axis=0)))
    near_second, hub_second, far_second = [along(second, pairs_) for pairs_ in (INWARD, ACROSS, BEYOND)]
    extent = tile // CHUNKS + depth_weight.shape[1] - 1
    swished = call(
        conv_kernel,
        (slots,),
        [by_slot((deep, width)), whole(taps.shape)] + [pinned] * 5,
        by_slot((tile, channels)),
        jax.ShapeDtypeStruct((slots, tile, channels), jnp.bfloat16),
        [
            pltpu.VMEM((8 * held, width), jnp.bfloat16),
            pltpu.VMEM((deep, 2 * LANES), jnp.float32),
            pltpu.VMEM((deep, 2 * LANES), jnp.float32),
            pltpu.VMEM((extent, CHUNKS, LANES), jnp.float32),
            pltpu.VMEM((2 * EDGE, LANES), jnp.float32),
            pltpu.VMEM((deep, LANES), jnp.float32),
            pltpu.SemaphoreType.DMA((8,)),
        ],
        2 * slots * deep * width * 2 * channels,
        2 * slots * deep * width + 8 * first.size * 2,
        (meta, normed, taps, *first_pieces),
    )

    near_second, hub_second, far_second, code, swished = lax.optimization_barrier(
        (near_second, hub_second, far_second, code, swished)
    )
    outer_code = along(code, INWARD)
    codes = jnp.concatenate([jnp.where(low, outer_code, code), jnp.where(low, code, outer_code)])
    mine = [second, near_second, hub_second, far_second]
    second_pieces = (*mine, to_mate(second), to_mate(jnp.concatenate(mine[1:], axis=0)))
    errors = call(
        head_kernel,
        (slots,),
        [by_slot((tile, channels)), by_slot((tile, width)), by_slot(codes.shape[1:]), whole(gains.shape)]
        + [pinned] * 6,
        by_slot((CHUNKS, LANES)),
        jax.ShapeDtypeStruct((slots, CHUNKS, LANES), jnp.float32),
        [
            pltpu.VMEM((8 * conv_out_weight.shape[1], width), jnp.bfloat16),
            pltpu.VMEM((8 * head_rows, vocab), jnp.bfloat16),
            pltpu.VMEM((half, width), jnp.float32),
            pltpu.VMEM((half, width), jnp.float32),
            pltpu.VMEM((half, width), jnp.bfloat16),
            pltpu.VMEM((half, width), jnp.bfloat16),
            pltpu.VMEM((half, vocab), jnp.float32),
            pltpu.VMEM((half, vocab), jnp.float32),
            pltpu.SemaphoreType.DMA((8, 1 + groups)),
        ],
        2 * slots * tile * (channels + vocab) * width,
        2 * slots * tile * (channels + width),
        (meta, swished, stem_out, codes, gains, *second_pieces),
    )

    one, two, three = [seed_swap(errors, bit) for bit in (1, 2, 3)]
    total = ((errors + one) + (two + three)) / jnp.float32(seeds)
    total = total[:, :, : tile // CHUNKS].reshape(2, rows)
    part = jnp.sum(total).reshape(1)
    outer_half = jnp.where(low, total[0], total[1])
    own_half = jnp.where(low, total[1], total[0])
    from_hub = along(jnp.concatenate([outer_half, part]), OUTWARD)
    parts = [part[0], along(part, ACROSS)[0], along(part, OUT_BEYOND)[0], from_hub[rows]]
    frame_error = jnp.where(is_hub, own_half, from_hub[:rows])
    utt_score = ((parts[0] + parts[3]) + (parts[1] + parts[2])) / length.astype(jnp.float32)
    return (frame_error[None, :], utt_score.reshape(1))


def from_behind(x, axis, by):
    count = lax.axis_size(axis)
    pairs = [(i, i + by) for i in range(count) if 0 <= i + by < count]
    return lax.ppermute(x, axis, pairs)


def extended(x, sides, width):
    for axis, dim in sides:
        count, length = (lax.axis_size(axis), x.shape[dim])
        up = [(i, (i + 1) % count) for i in range(count - 1)]
        down = [(j, i) for i, j in up]
        last = lax.slice_in_dim(x, length - width, length, axis=dim)
        first = lax.slice_in_dim(x, 0, width, axis=dim)
        before = lax.ppermute(last, axis, up)
        after = lax.ppermute(first, axis, down)
        x = jnp.concatenate([before, x, after], axis=dim)
    return x


def layer_norm(values, gain_row):
    row_mean = jnp.mean(values, axis=-1, keepdims=True)
    centred = values - row_mean
    row_var = jnp.mean(centred * centred, axis=-1, keepdims=True)
    return (centred * lax.rsqrt(row_var + 1e-05) * gain_row).astype(jnp.bfloat16)


def block_product(left_rows, right_matrix):
    return jnp.dot(left_rows, right_matrix, preferred_element_type=jnp.float32)


def row_product(activations, shard_piece):
    return block_product(activations, shard_piece[0])


def body(
    mel_frames,
    lengths,
    targets,
    frame_mask,
    stem_weight,
    conv_in_weight,
    conv_out_weight,
    depth_weight,
    head_weight,
    norm_gain,
):
    frame_rows = targets.shape[1]
    blocks = mel_frames[0].reshape(frame_rows, -1)
    next_block = from_behind(blocks[:1], "seq", -1)
    following = jnp.concatenate([blocks[1:], next_block], 0)
    half_width = blocks.shape[1]
    stem_matrix = stem_weight[0]
    stem_out = (
        jnp.dot(blocks, stem_matrix[:half_width], preferred_element_type=jnp.float32)
        + jnp.dot(following, stem_matrix[half_width:], preferred_element_type=jnp.float32)
    ).astype(jnp.bfloat16)
    offset = lax.axis_index("seq") * frame_rows
    length = lengths[0]
    positions = offset + jnp.arange(frame_rows, dtype=jnp.int32)
    frame_live = positions < length
    gain_rows = norm_gain[0]
    normed_one = layer_norm(stem_out.astype(jnp.float32), gain_rows[0])
    tap_count = depth_weight.shape[1]
    channels = depth_weight.shape[2]
    halo_width = tap_count // 2
    conv_input = extended(normed_one, (("seq", 0),), halo_width)
    mixed_rows = row_product(
        conv_input, lax.all_gather(conv_in_weight, ("fsdp", "seq"), axis=1, tiled=True)
    )
    input_positions = offset - halo_width + jnp.arange(conv_input.shape[0], dtype=jnp.int32)
    input_live = jnp.logical_and(input_positions >= 0, input_positions < length)
    gated_rows = (
        mixed_rows[:, :channels]
        * jax.nn.sigmoid(mixed_rows[:, channels:])
        * input_live[:, None].astype(jnp.float32)
    ).astype(jnp.bfloat16)
    depthwise = jnp.zeros((frame_rows, channels), jnp.float32)
    for tap_index in range(tap_count):
        depthwise = depthwise + gated_rows[tap_index : tap_index + frame_rows].astype(
            jnp.float32
        ) * depth_weight[0, tap_index].astype(jnp.float32)
    swished = jax.nn.silu(depthwise).astype(jnp.bfloat16)
    conv_proj = row_product(
        swished, lax.all_gather(conv_out_weight, ("fsdp", "seq"), axis=1, tiled=True)
    )
    after_conv = stem_out.astype(jnp.float32) + conv_proj
    normed_two = layer_norm(after_conv, gain_rows[1])
    logits = row_product(
        normed_two, lax.all_gather(head_weight, ("fsdp", "seq"), axis=1, tiled=True)
    )
    posterior = jax.nn.softmax(logits, axis=-1)
    vocab_size = logits.shape[1]
    onehot = (jnp.arange(vocab_size, dtype=jnp.int32)[None, :] == targets[0][:, None]).astype(
        jnp.float32
    )
    differ = posterior - onehot
    frame_err = (
        jnp.sqrt(jnp.sum(differ * differ, axis=-1))
        * frame_live.astype(jnp.float32)
        * frame_mask[0].astype(jnp.float32)
    )
    seed_count = lax.axis_size("seed")
    frame_error = lax.psum(frame_err, "seed") / jnp.float32(seed_count)
    numerator = lax.psum(jnp.sum(frame_error), "seq")
    utt_score = numerator / length.astype(jnp.float32)
    return (frame_error[None, :], utt_score.reshape(1))


def solution(mesh):
    in_specs = (
        P("fsdp", "seq", None),
        P("fsdp"),
        P("fsdp", "seq"),
        P("fsdp", "seq"),
        P("seed", None, None),
        P("seed", ("fsdp", "seq"), None),
        P("seed", ("fsdp", "seq"), None),
        P("seed", None, None),
        P("seed", ("fsdp", "seq"), None),
        P("seed", None, None),
    )
    out_specs = (P("fsdp", "seq"), P("fsdp"))
    hubs = mesh.shape["seq"] == 4 and mesh.shape["fsdp"] == 2
    return jax.shard_map(
        hub_body if hubs else body, mesh=mesh, in_specs=in_specs, out_specs=out_specs, check_vma=False
    )
```

```python
import jax
import jax.numpy as jnp
from jax import lax
from jax.experimental import pallas as pl
from jax.experimental.pallas import tpu as pltpu
from jax.sharding import PartitionSpec as P

LANES = 128
CHUNKS = 8
EDGE = 16
VMEM_BYTES = 24 * 1024 * 1024


def norm_rows(values, gain_row):
    row_mean = jnp.mean(values, axis=-1, keepdims=True)
    centred = values - row_mean
    row_var = jnp.mean(centred * centred, axis=-1, keepdims=True)
    return (centred * lax.rsqrt(row_var + 1e-05) * gain_row).astype(jnp.bfloat16)


def sigmoid(x):
    return 0.5 * jnp.tanh(0.5 * x) + 0.5


def stem_kernel(
    meta, main_ref, margin_ref, stem_ref, gain_ref, stem_out_ref, normed_ref, acc_a, acc_b, acc_c
):
    slot = pl.program_id(0)
    frames = main_ref.shape[1]
    part = acc_a.shape[0]
    group = 16

    def norm(acc, at, keep):
        for row in range(0, acc.shape[0], group):
            stem_out = acc[row : row + group, :].astype(jnp.bfloat16)
            if keep:
                stem_out_ref[0, at + row : at + row + group, :] = stem_out
            normed_ref[0, at + row : at + row + group, :] = norm_rows(stem_out.astype(jnp.float32), gain_ref[0:1, :])

    @pl.when(meta[5 + slot] > 0)
    def _():
        for acc, left in ((acc_a, main_ref[0, :part, :]), (acc_b, main_ref[0, part:, :]), (acc_c, margin_ref[0])):
            acc[...] = jnp.dot(left, stem_ref[...], preferred_element_type=jnp.float32)
        norm(acc_a, 0, True)
        norm(acc_b, part, True)
        norm(acc_c, frames, False)


def shards(meta, pieces):
    side = meta[13]
    length = pieces[0].shape[0]
    places = [(piece, 0) for piece in pieces[:-1]]
    places += [(pieces[-1], i * length) for i in range(8 - len(places))]
    return [(*place, (side if i < 4 else 1 - side) * 4 + meta[9 + i % 4]) for i, place in enumerate(places)]


def conv_kernel(meta, normed_ref, taps_ref, *rest):
    pieces = rest[:5]
    swished_ref, weight, mixed_a, mixed_b, gated, margin, mask, sems = rest[5:]
    slot = pl.program_id(0)
    rows = normed_ref.shape[1]
    frames = swished_ref.shape[1]
    channels = swished_ref.shape[2]
    tap_count = taps_ref.shape[0]
    reach = tap_count // 2
    piece = weight.shape[0] // 8
    run_length = frames // CHUNKS

    @pl.when(jnp.logical_and(pl.program_id(0) == 0, meta[14] > 0))
    def _():
        copies = [
            pltpu.make_async_copy(
                ref.at[pl.ds(at, piece)], weight.at[pl.ds(pl.multiple_of(block * piece, 16), piece)], sems.at[i]
            )
            for i, (ref, at, block) in enumerate(shards(meta, pieces))
        ]
        for copy in copies:
            copy.start()
        for copy in copies:
            copy.wait()

    @pl.when(meta[5 + slot] > 0)
    def _():
        row = lax.broadcasted_iota(jnp.int32, (rows, LANES), 0)
        inner = (row % CHUNKS) * run_length + row // CHUNKS
        outer = jnp.where(row < frames + EDGE, row - frames - EDGE, row - EDGE)
        at = meta[slot] + jnp.where(row < frames, inner, outer)
        mask[...] = jnp.logical_and(at >= 0, at < meta[4]).astype(jnp.float32)
        sublane = lax.broadcasted_iota(jnp.int32, (CHUNKS, LANES), 0)
        buffers = (mixed_a, mixed_b)

        def mix(block):
            low = block * LANES
            right = jnp.concatenate(
                [weight[:, low : low + LANES], weight[:, channels + low : channels + low + LANES]], axis=1
            )
            buffers[block % 2][...] = jnp.dot(normed_ref[0], right, preferred_element_type=jnp.float32)

        def gate(block):
            mixed = buffers[block % 2]
            group = 32
            for at in range(0, rows, group):
                here = slice(at, at + group)
                made = mixed[here, :LANES] * sigmoid(mixed[here, LANES:]) * mask[here, :]
                made = made.astype(jnp.bfloat16).astype(jnp.float32)
                if at < frames:
                    first = reach + at // CHUNKS
                    gated[first : first + group // CHUNKS] = made.reshape(group // CHUNKS, CHUNKS, LANES)
                else:
                    margin[...] = made
            for i in range(reach):
                before = pltpu.roll(gated[run_length + i], 1, 0)
                edge = margin[EDGE - reach + i : EDGE - reach + i + 1, :]
                gated[i] = jnp.where(sublane == 0, edge, before)
                after = pltpu.roll(gated[reach + i], CHUNKS - 1, 0)
                edge = margin[EDGE + i : EDGE + i + 1, :]
                gated[reach + run_length + i] = jnp.where(sublane == CHUNKS - 1, edge, after)

        def convolve(block):
            low = block * LANES
            run = 16
            for start in range(0, run_length, run):
                sums = [None] * run
                for at in range(start, start + run + tap_count - 1):
                    value = gated[at]
                    for m in range(max(start, at - tap_count + 1), min(start + run, at + 1)):
                        term = value * taps_ref[at - m, :, low : low + LANES]
                        k = m - start
                        sums[k] = term if sums[k] is None else sums[k] + term
                for k in range(0, run, 2):
                    total = jnp.concatenate(sums[k : k + 2], axis=0)
                    first = (start + k) * CHUNKS
                    swished_ref[0, first : first + 2 * CHUNKS, low : low + LANES] = (
                        total * sigmoid(total)
                    ).astype(jnp.bfloat16)

        blocks = channels // LANES
        mix(0)
        for block in range(blocks):
            if block + 1 < blocks:
                mix(block + 1)
            gate(block)
            convolve(block)


def head_kernel(meta, swished_ref, stem_out_ref, code_ref, gain_ref, *rest):
    pieces = rest[:6]
    error_ref, back, head, acc_a, acc_b, norm_a, norm_b, logit_a, logit_b, sems = rest[6:]
    slot = pl.program_id(0)
    frames = swished_ref.shape[1]
    vocab = head.shape[1]
    groups = back.shape[1] // vocab
    back_rows = back.shape[0] // 8
    head_rows = head.shape[0] // 8
    group_rows = head_rows // groups

    @pl.when(jnp.logical_and(pl.program_id(0) == 0, meta[14] > 0))
    def _():
        copies = []
        for i, (ref, at, block) in enumerate(shards(meta, pieces)):
            copies.append(
                pltpu.make_async_copy(
                    ref.at[pl.ds(at, back_rows)],
                    back.at[pl.ds(pl.multiple_of(block * back_rows, 16), back_rows)],
                    sems.at[i, 0],
                )
            )
            for g in range(groups):
                copies.append(
                    pltpu.make_async_copy(
                        ref.at[pl.ds(at + back_rows, group_rows), pl.ds(g * vocab, vocab)],
                        head.at[pl.ds(pl.multiple_of(block * head_rows + g * group_rows, 16), group_rows)],
                        sems.at[i, 1 + g],
                    )
                )
        for copy in copies:
            copy.start()
        for copy in copies:
            copy.wait()

    @pl.when(meta[5 + slot] <= 0)
    def _():
        error_ref[...] = jnp.zeros_like(error_ref)

    @pl.when(meta[5 + slot] > 0)
    def _():
        part = acc_a.shape[0]
        lane = lax.broadcasted_iota(jnp.int32, (CHUNKS, LANES), 1)
        def norm(at, acc, normed):
            group = 16
            for row in range(0, part, group):
                values = acc[row : row + group, :] + stem_out_ref[0, at + row : at + row + group, :].astype(jnp.float32)
                normed[row : row + group, :] = norm_rows(values, gain_ref[1:2, :])

        def errors(at, logits, row):
            group = 32
            token = lax.broadcasted_iota(jnp.int32, (group, vocab), 1)
            for first in range(0, part, group):
                scores = logits[first : first + group, :]
                grown = jnp.exp(scores - jnp.max(scores, axis=-1, keepdims=True))
                posterior = grown * (1.0 / jnp.sum(grown, axis=-1, keepdims=True))
                steps = range((at + first) // CHUNKS, (at + first + group) // CHUNKS)
                code = jnp.concatenate([code_ref[0, :, m : m + 1] for m in steps], axis=0)
                differ = posterior - (token == code).astype(jnp.float32)
                error = jnp.sqrt(jnp.sum(differ * differ, axis=-1, keepdims=True))
                error = jnp.where(code >= 0, error, 0.0)
                for k, m in enumerate(steps):
                    row = jnp.where(lane == m, error[k * CHUNKS : (k + 1) * CHUNKS, :], row)
            return row

        halves = ((0, acc_a, norm_a, logit_a), (part, acc_b, norm_b, logit_b))
        for at, acc, _, _ in halves:
            acc[...] = jnp.dot(swished_ref[0, at : at + part, :], back[...], preferred_element_type=jnp.float32)
        for at, acc, normed, logits in halves:
            norm(at, acc, normed)
            logits[...] = jnp.dot(normed[...], head[...], preferred_element_type=jnp.float32)
        row = jnp.zeros((CHUNKS, LANES), jnp.float32)
        for at, _, _, logits in halves:
            row = errors(at, logits, row)
        error_ref[0] = row


def call(kernel, grid, in_specs, out_specs, out_shape, scratch, flops, moved, operands):
    return pl.pallas_call(
        kernel,
        grid_spec=pltpu.PrefetchScalarGridSpec(
            num_scalar_prefetch=1,
            grid=grid,
            in_specs=in_specs,
            out_specs=out_specs,
            scratch_shapes=scratch,
        ),
        out_shape=out_shape,
        compiler_params=pltpu.CompilerParams(
            dimension_semantics=("arbitrary",), vmem_limit_bytes=VMEM_BYTES
        ),
        cost_estimate=pl.CostEstimate(flops=flops // 16, bytes_accessed=moved // 16, transcendentals=0),
    )(*operands)


def whole(shape):
    return pl.BlockSpec(shape, lambda i, meta: (0,) * len(shape))


def by_slot(shape):
    return pl.BlockSpec((1,) + shape, lambda i, meta: (i,) + (0,) * len(shape))


INWARD = [(0, 1), (3, 2)]
ACROSS = [(1, 2), (2, 1)]
BEYOND = [(0, 2), (3, 1)]
OUTWARD = [(1, 0), (2, 3)]
OUT_BEYOND = [(2, 0), (1, 3)]


def along(x, pairs):
    return lax.ppermute(x, "seq", pairs)


def to_mate(x):
    pairs = [(a * 4 + z, (1 - a) * 4 + z) for a in (0, 1) for z in (1, 2)]
    return lax.ppermute(x, ("fsdp", "seq"), pairs)


def seed_swap(x, bit):
    return lax.ppermute(x, "seed", [(i, i ^ bit) for i in range(4)])


def hub_body(
    mel_frames,
    lengths,
    targets,
    frame_mask,
    stem_weight,
    conv_in_weight,
    conv_out_weight,
    depth_weight,
    head_weight,
    norm_gain,
):
    chip = lax.axis_index("seq")
    side = lax.axis_index("fsdp")
    seeds = lax.axis_size("seed")
    rows = targets.shape[1]
    width = stem_weight.shape[2]
    channels = depth_weight.shape[2]
    vocab = head_weight.shape[2]
    step = mel_frames.shape[1] // rows
    tile = rows // 2
    seed = lax.axis_index("seed")
    low = chip == 1
    is_hub = jnp.logical_or(low, chip == 2)

    length = lengths[0]
    positions = chip * rows + jnp.arange(rows, dtype=jnp.int32)
    counted = jnp.logical_and(frame_mask[0] > 0, positions < length)
    code = jnp.where(counted, targets[0], -1)
    first = conv_in_weight[0]
    blocks = mel_frames[0].reshape(rows, -1)
    share = rows // seeds
    margin = step * EDGE
    quarter = lax.dynamic_slice_in_dim(mel_frames[0], seed * share * step, share * step, 0).reshape(share, -1)
    edge_out = jnp.where(low, mel_frames[0, -margin:], mel_frames[0, :margin]).reshape(EDGE, -1)
    quarter_in = along(quarter, INWARD)
    edge = along(edge_out, ACROSS)
    outer_code = along(code, INWARD)
    first_held, quarter_in, edge, outer_code = lax.optimization_barrier((first, quarter_in, edge, outer_code))
    near_first, hub_first, far_first = [along(first_held, pairs_) for pairs_ in (INWARD, ACROSS, BEYOND)]
    held = first.shape[0]

    pair = seed_swap(quarter_in, 1)
    odd = seed % 2 == 1
    pairs = jnp.concatenate([jnp.where(odd, pair, quarter_in), jnp.where(odd, quarter_in, pair)], axis=0)
    other = seed_swap(pairs, 2)
    upper = seed // 2 == 1
    outer = jnp.concatenate([jnp.where(upper, other, pairs), jnp.where(upper, pairs, other)], axis=0)

    groups = width // vocab
    head_rows = head_weight.shape[1]
    second = jnp.concatenate(
        [
            conv_out_weight[0],
            jnp.concatenate(jnp.split(head_weight[0], groups, axis=0), axis=1),
        ],
        axis=0,
    )
    slots = 4
    deep = tile + 2 * EDGE
    none = jnp.zeros_like(edge)
    frames = jnp.concatenate(
        [
            jnp.where(low, none, edge),
            jnp.where(low, outer, blocks),
            jnp.where(low, blocks, outer),
            jnp.where(low, edge, none),
            none,
        ],
        axis=0,
    )
    pairs = jnp.concatenate([frames[:-1], frames[1:]], axis=1)
    main = pairs[EDGE : EDGE + slots * tile].reshape(slots, CHUNKS, tile // CHUNKS, -1)
    main = main.transpose(0, 2, 1, 3).reshape(slots, tile, -1)
    margins = jnp.stack(
        [
            jnp.concatenate([pairs[k * tile : k * tile + EDGE], pairs[(k + 1) * tile + EDGE : (k + 1) * tile + 2 * EDGE]])
            for k in range(slots)
        ]
    )

    starts = (chip - 1) * 2 * rows + tile * jnp.arange(slots, dtype=jnp.int32)
    alive = jnp.logical_and(is_hub, starts < length).astype(jnp.int32)
    hub = jnp.clip(chip, 1, 2)
    meta = jnp.concatenate(
        [
            starts,
            lengths,
            alive,
            jnp.stack([hub, 3 * (hub - 1), 3 - hub, 3 * (2 - hub), side, jnp.max(alive)]),
        ]
    ).astype(jnp.int32)

    gains = norm_gain[0]
    half = tile // 2
    stem_out, normed = call(
        stem_kernel,
        (slots,),
        [by_slot(main.shape[1:]), by_slot(margins.shape[1:]), whole(stem_weight.shape[1:]), whole(gains.shape)],
        [by_slot((tile, width)), by_slot((deep, width))],
        [
            jax.ShapeDtypeStruct((slots, tile, width), jnp.bfloat16),
            jax.ShapeDtypeStruct((slots, deep, width), jnp.bfloat16),
        ],
        [
            pltpu.VMEM((half, width), jnp.float32),
            pltpu.VMEM((half, width), jnp.float32),
            pltpu.VMEM((2 * EDGE, width), jnp.float32),
        ],
        2 * slots * deep * main.shape[2] * width,
        2 * slots * deep * (main.shape[2] + 2 * width),
        (meta, main, margins, stem_weight[0], gains),
    )
    pinned = pl.BlockSpec(memory_space=pltpu.HBM)

    codes = jnp.concatenate([jnp.where(low, outer_code, code), jnp.where(low, code, outer_code)])
    codes = codes.reshape(slots, CHUNKS, tile // CHUNKS)
    far_first, normed, codes = lax.optimization_barrier((far_first, normed, codes))
    mine = [first, near_first, hub_first, far_first]
    first_pieces = (*mine, to_mate(jnp.concatenate(mine, axis=0)))
    near_second, hub_second, far_second = [along(second, pairs_) for pairs_ in (INWARD, ACROSS, BEYOND)]
    taps = jnp.broadcast_to(
        depth_weight[0].astype(jnp.float32)[:, None, :], (depth_weight.shape[1], CHUNKS, channels)
    )
    extent = tile // CHUNKS + depth_weight.shape[1] - 1
    swished = call(
        conv_kernel,
        (slots,),
        [by_slot((deep, width)), whole(taps.shape)] + [pinned] * 5,
        by_slot((tile, channels)),
        jax.ShapeDtypeStruct((slots, tile, channels), jnp.bfloat16),
        [
            pltpu.VMEM((8 * held, width), jnp.bfloat16),
            pltpu.VMEM((deep, 2 * LANES), jnp.float32),
            pltpu.VMEM((deep, 2 * LANES), jnp.float32),
            pltpu.VMEM((extent, CHUNKS, LANES), jnp.float32),
            pltpu.VMEM((2 * EDGE, LANES), jnp.float32),
            pltpu.VMEM((deep, LANES), jnp.float32),
            pltpu.SemaphoreType.DMA((8,)),
        ],
        2 * slots * deep * width * 2 * channels,
        2 * slots * deep * width + 8 * first.size * 2,
        (meta, normed, taps, *first_pieces),
    )

    near_second, hub_second, far_second, swished = lax.optimization_barrier(
        (near_second, hub_second, far_second, swished)
    )
    mine = [second, near_second, hub_second, far_second]
    second_pieces = (*mine, to_mate(second), to_mate(jnp.concatenate(mine[1:], axis=0)))
    errors = call(
        head_kernel,
        (slots,),
        [by_slot((tile, channels)), by_slot((tile, width)), by_slot(codes.shape[1:]), whole(gains.shape)]
        + [pinned] * 6,
        by_slot((CHUNKS, LANES)),
        jax.ShapeDtypeStruct((slots, CHUNKS, LANES), jnp.float32),
        [
            pltpu.VMEM((8 * conv_out_weight.shape[1], width), jnp.bfloat16),
            pltpu.VMEM((8 * head_rows, vocab), jnp.bfloat16),
            pltpu.VMEM((half, width), jnp.float32),
            pltpu.VMEM((half, width), jnp.float32),
            pltpu.VMEM((half, width), jnp.bfloat16),
            pltpu.VMEM((half, width), jnp.bfloat16),
            pltpu.VMEM((half, vocab), jnp.float32),
            pltpu.VMEM((half, vocab), jnp.float32),
            pltpu.SemaphoreType.DMA((8, 1 + groups)),
        ],
        2 * slots * tile * (channels + vocab) * width,
        2 * slots * tile * (channels + width),
        (meta, swished, stem_out, codes, gains, *second_pieces),
    )

    one, two, three = [seed_swap(errors, bit) for bit in (1, 2, 3)]
    total = ((errors + one) + (two + three)) / jnp.float32(seeds)
    total = total[:, :, : tile // CHUNKS].reshape(2, rows)
    part = jnp.sum(total).reshape(1)
    outer_half = jnp.where(low, total[0], total[1])
    own_half = jnp.where(low, total[1], total[0])
    from_hub = along(jnp.concatenate([outer_half, part]), OUTWARD)
    parts = [part[0], along(part, ACROSS)[0], along(part, OUT_BEYOND)[0], from_hub[rows]]
    frame_error = jnp.where(is_hub, own_half, from_hub[:rows])
    utt_score = ((parts[0] + parts[3]) + (parts[1] + parts[2])) / length.astype(jnp.float32)
    return (frame_error[None, :], utt_score.reshape(1))


def from_behind(x, axis, by):
    count = lax.axis_size(axis)
    pairs = [(i, i + by) for i in range(count) if 0 <= i + by < count]
    return lax.ppermute(x, axis, pairs)


def extended(x, sides, width):
    for axis, dim in sides:
        count, length = (lax.axis_size(axis), x.shape[dim])
        up = [(i, (i + 1) % count) for i in range(count - 1)]
        down = [(j, i) for i, j in up]
        last = lax.slice_in_dim(x, length - width, length, axis=dim)
        first = lax.slice_in_dim(x, 0, width, axis=dim)
        before = lax.ppermute(last, axis, up)
        after = lax.ppermute(first, axis, down)
        x = jnp.concatenate([before, x, after], axis=dim)
    return x


def layer_norm(values, gain_row):
    row_mean = jnp.mean(values, axis=-1, keepdims=True)
    centred = values - row_mean
    row_var = jnp.mean(centred * centred, axis=-1, keepdims=True)
    return (centred * lax.rsqrt(row_var + 1e-05) * gain_row).astype(jnp.bfloat16)


def block_product(left_rows, right_matrix):
    return jnp.dot(left_rows, right_matrix, preferred_element_type=jnp.float32)


def row_product(activations, shard_piece):
    return block_product(activations, shard_piece[0])


def body(
    mel_frames,
    lengths,
    targets,
    frame_mask,
    stem_weight,
    conv_in_weight,
    conv_out_weight,
    depth_weight,
    head_weight,
    norm_gain,
):
    frame_rows = targets.shape[1]
    blocks = mel_frames[0].reshape(frame_rows, -1)
    next_block = from_behind(blocks[:1], "seq", -1)
    following = jnp.concatenate([blocks[1:], next_block], 0)
    half_width = blocks.shape[1]
    stem_matrix = stem_weight[0]
    stem_out = (
        jnp.dot(blocks, stem_matrix[:half_width], preferred_element_type=jnp.float32)
        + jnp.dot(following, stem_matrix[half_width:], preferred_element_type=jnp.float32)
    ).astype(jnp.bfloat16)
    offset = lax.axis_index("seq") * frame_rows
    length = lengths[0]
    positions = offset + jnp.arange(frame_rows, dtype=jnp.int32)
    frame_live = positions < length
    gain_rows = norm_gain[0]
    normed_one = layer_norm(stem_out.astype(jnp.float32), gain_rows[0])
    tap_count = depth_weight.shape[1]
    channels = depth_weight.shape[2]
    halo_width = tap_count // 2
    conv_input = extended(normed_one, (("seq", 0),), halo_width)
    mixed_rows = row_product(
        conv_input, lax.all_gather(conv_in_weight, ("fsdp", "seq"), axis=1, tiled=True)
    )
    input_positions = offset - halo_width + jnp.arange(conv_input.shape[0], dtype=jnp.int32)
    input_live = jnp.logical_and(input_positions >= 0, input_positions < length)
    gated_rows = (
        mixed_rows[:, :channels]
        * jax.nn.sigmoid(mixed_rows[:, channels:])
        * input_live[:, None].astype(jnp.float32)
    ).astype(jnp.bfloat16)
    depthwise = jnp.zeros((frame_rows, channels), jnp.float32)
    for tap_index in range(tap_count):
        depthwise = depthwise + gated_rows[tap_index : tap_index + frame_rows].astype(
            jnp.float32
        ) * depth_weight[0, tap_index].astype(jnp.float32)
    swished = jax.nn.silu(depthwise).astype(jnp.bfloat16)
    conv_proj = row_product(
        swished, lax.all_gather(conv_out_weight, ("fsdp", "seq"), axis=1, tiled=True)
    )
    after_conv = stem_out.astype(jnp.float32) + conv_proj
    normed_two = layer_norm(after_conv, gain_rows[1])
    logits = row_product(
        normed_two, lax.all_gather(head_weight, ("fsdp", "seq"), axis=1, tiled=True)
    )
    posterior = jax.nn.softmax(logits, axis=-1)
    vocab_size = logits.shape[1]
    onehot = (jnp.arange(vocab_size, dtype=jnp.int32)[None, :] == targets[0][:, None]).astype(
        jnp.float32
    )
    differ = posterior - onehot
    frame_err = (
        jnp.sqrt(jnp.sum(differ * differ, axis=-1))
        * frame_live.astype(jnp.float32)
        * frame_mask[0].astype(jnp.float32)
    )
    seed_count = lax.axis_size("seed")
    frame_error = lax.psum(frame_err, "seed") / jnp.float32(seed_count)
    numerator = lax.psum(jnp.sum(frame_error), "seq")
    utt_score = numerator / length.astype(jnp.float32)
    return (frame_error[None, :], utt_score.reshape(1))


def solution(mesh):
    in_specs = (
        P("fsdp", "seq", None),
        P("fsdp"),
        P("fsdp", "seq"),
        P("fsdp", "seq"),
        P("seed", None, None),
        P("seed", ("fsdp", "seq"), None),
        P("seed", ("fsdp", "seq"), None),
        P("seed", None, None),
        P("seed", ("fsdp", "seq"), None),
        P("seed", None, None),
    )
    out_specs = (P("fsdp", "seq"), P("fsdp"))
    hubs = mesh.shape["seq"] == 4 and mesh.shape["fsdp"] == 2
    return jax.shard_map(
        hub_body if hubs else body, mesh=mesh, in_specs=in_specs, out_specs=out_specs, check_vma=False
    )
```

```python
import jax
import jax.numpy as jnp
from jax import lax
from jax.experimental import pallas as pl
from jax.experimental.pallas import tpu as pltpu
from jax.sharding import PartitionSpec as P

LANES = 128
CHUNKS = 8
EDGE = 16
VMEM_BYTES = 24 * 1024 * 1024


def norm_rows(values, gain_row):
    row_mean = jnp.mean(values, axis=-1, keepdims=True)
    centred = values - row_mean
    row_var = jnp.mean(centred * centred, axis=-1, keepdims=True)
    return (centred * lax.rsqrt(row_var + 1e-05) * gain_row).astype(jnp.bfloat16)


def sigmoid(x):
    return 0.5 * jnp.tanh(0.5 * x) + 0.5


def stem_kernel(
    meta, main_ref, margin_ref, stem_ref, gain_ref, stem_out_ref, normed_ref, acc_a, acc_b, acc_c
):
    slot = pl.program_id(0)
    frames = main_ref.shape[1]
    part = acc_a.shape[0]
    group = 16

    def norm(acc, at, keep):
        for row in range(0, acc.shape[0], group):
            stem_out = acc[row : row + group, :].astype(jnp.bfloat16)
            if keep:
                stem_out_ref[0, at + row : at + row + group, :] = stem_out
            normed_ref[0, at + row : at + row + group, :] = norm_rows(stem_out.astype(jnp.float32), gain_ref[0:1, :])

    @pl.when(meta[5 + slot] > 0)
    def _():
        for acc, left in ((acc_a, main_ref[0, :part, :]), (acc_b, main_ref[0, part:, :]), (acc_c, margin_ref[0])):
            acc[...] = jnp.dot(left, stem_ref[...], preferred_element_type=jnp.float32)
        norm(acc_a, 0, True)
        norm(acc_b, part, True)
        norm(acc_c, frames, False)


def shards(meta, pieces):
    side = meta[13]
    length = pieces[0].shape[0]
    places = [(piece, 0) for piece in pieces[:-1]]
    places += [(pieces[-1], i * length) for i in range(8 - len(places))]
    return [(*place, (side if i < 4 else 1 - side) * 4 + meta[9 + i % 4]) for i, place in enumerate(places)]


def conv_kernel(meta, normed_ref, taps_ref, *rest):
    pieces = rest[:5]
    swished_ref, weight, mixed_a, mixed_b, gated, margin, mask, sems = rest[5:]
    slot = pl.program_id(0)
    rows = normed_ref.shape[1]
    frames = swished_ref.shape[1]
    channels = swished_ref.shape[2]
    tap_count = taps_ref.shape[0]
    reach = tap_count // 2
    piece = weight.shape[0] // 8
    run_length = frames // CHUNKS

    @pl.when(jnp.logical_and(pl.program_id(0) == 0, meta[14] > 0))
    def _():
        copies = [
            pltpu.make_async_copy(
                ref.at[pl.ds(at, piece)], weight.at[pl.ds(pl.multiple_of(block * piece, 16), piece)], sems.at[i]
            )
            for i, (ref, at, block) in enumerate(shards(meta, pieces))
        ]
        for copy in copies:
            copy.start()
        for copy in copies:
            copy.wait()

    @pl.when(meta[5 + slot] > 0)
    def _():
        row = lax.broadcasted_iota(jnp.int32, (rows, LANES), 0)
        inner = (row % CHUNKS) * run_length + row // CHUNKS
        outer = jnp.where(row < frames + EDGE, row - frames - EDGE, row - EDGE)
        at = meta[slot] + jnp.where(row < frames, inner, outer)
        mask[...] = jnp.logical_and(at >= 0, at < meta[4]).astype(jnp.float32)
        sublane = lax.broadcasted_iota(jnp.int32, (CHUNKS, LANES), 0)
        buffers = (mixed_a, mixed_b)

        def mix(block):
            low = block * LANES
            right = jnp.concatenate(
                [weight[:, low : low + LANES], weight[:, channels + low : channels + low + LANES]], axis=1
            )
            buffers[block % 2][...] = jnp.dot(normed_ref[0], right, preferred_element_type=jnp.float32)

        def gate(block):
            mixed = buffers[block % 2]
            group = 32
            for at in range(0, rows, group):
                here = slice(at, at + group)
                made = mixed[here, :LANES] * sigmoid(mixed[here, LANES:]) * mask[here, :]
                made = made.astype(jnp.bfloat16).astype(jnp.float32)
                if at < frames:
                    first = reach + at // CHUNKS
                    gated[first : first + group // CHUNKS] = made.reshape(group // CHUNKS, CHUNKS, LANES)
                else:
                    margin[...] = made
            for i in range(reach):
                before = pltpu.roll(gated[run_length + i], 1, 0)
                edge = margin[EDGE - reach + i : EDGE - reach + i + 1, :]
                gated[i] = jnp.where(sublane == 0, edge, before)
                after = pltpu.roll(gated[reach + i], CHUNKS - 1, 0)
                edge = margin[EDGE + i : EDGE + i + 1, :]
                gated[reach + run_length + i] = jnp.where(sublane == CHUNKS - 1, edge, after)

        def convolve(block):
            low = block * LANES
            run = 16
            for start in range(0, run_length, run):
                sums = [None] * run
                for at in range(start, start + run + tap_count - 1):
                    value = gated[at]
                    for m in range(max(start, at - tap_count + 1), min(start + run, at + 1)):
                        term = value * taps_ref[at - m, :, low : low + LANES]
                        k = m - start
                        sums[k] = term if sums[k] is None else sums[k] + term
                for k in range(0, run, 2):
                    total = jnp.concatenate(sums[k : k + 2], axis=0)
                    first = (start + k) * CHUNKS
                    swished_ref[0, first : first + 2 * CHUNKS, low : low + LANES] = (
                        total * sigmoid(total)
                    ).astype(jnp.bfloat16)

        blocks = channels // LANES
        mix(0)
        for block in range(blocks):
            if block + 1 < blocks:
                mix(block + 1)
            gate(block)
            convolve(block)


def head_kernel(meta, swished_ref, stem_out_ref, code_ref, gain_ref, *rest):
    pieces = rest[:6]
    error_ref, back, head, acc_a, acc_b, norm_a, norm_b, logit_a, logit_b, sems = rest[6:]
    slot = pl.program_id(0)
    frames = swished_ref.shape[1]
    vocab = head.shape[1]
    groups = back.shape[1] // vocab
    back_rows = back.shape[0] // 8
    head_rows = head.shape[0] // 8
    group_rows = head_rows // groups

    @pl.when(jnp.logical_and(pl.program_id(0) == 0, meta[14] > 0))
    def _():
        copies = []
        for i, (ref, at, block) in enumerate(shards(meta, pieces)):
            copies.append(
                pltpu.make_async_copy(
                    ref.at[pl.ds(at, back_rows)],
                    back.at[pl.ds(pl.multiple_of(block * back_rows, 16), back_rows)],
                    sems.at[i, 0],
                )
            )
            for g in range(groups):
                copies.append(
                    pltpu.make_async_copy(
                        ref.at[pl.ds(at + back_rows, group_rows), pl.ds(g * vocab, vocab)],
                        head.at[pl.ds(pl.multiple_of(block * head_rows + g * group_rows, 16), group_rows)],
                        sems.at[i, 1 + g],
                    )
                )
        for copy in copies:
            copy.start()
        for copy in copies:
            copy.wait()

    @pl.when(meta[5 + slot] <= 0)
    def _():
        error_ref[...] = jnp.zeros_like(error_ref)

    @pl.when(meta[5 + slot] > 0)
    def _():
        part = acc_a.shape[0]
        lane = lax.broadcasted_iota(jnp.int32, (CHUNKS, LANES), 1)
        def norm(at, acc, normed):
            group = 16
            for row in range(0, part, group):
                values = acc[row : row + group, :] + stem_out_ref[0, at + row : at + row + group, :].astype(jnp.float32)
                normed[row : row + group, :] = norm_rows(values, gain_ref[1:2, :])

        def errors(at, logits, row):
            group = 32
            token = lax.broadcasted_iota(jnp.int32, (group, vocab), 1)
            for first in range(0, part, group):
                scores = logits[first : first + group, :]
                grown = jnp.exp(scores - jnp.max(scores, axis=-1, keepdims=True))
                posterior = grown * (1.0 / jnp.sum(grown, axis=-1, keepdims=True))
                steps = range((at + first) // CHUNKS, (at + first + group) // CHUNKS)
                code = jnp.concatenate([code_ref[0, :, m : m + 1] for m in steps], axis=0)
                differ = posterior - (token == code).astype(jnp.float32)
                error = jnp.sqrt(jnp.sum(differ * differ, axis=-1, keepdims=True))
                error = jnp.where(code >= 0, error, 0.0)
                for k, m in enumerate(steps):
                    row = jnp.where(lane == m, error[k * CHUNKS : (k + 1) * CHUNKS, :], row)
            return row

        halves = ((0, acc_a, norm_a, logit_a), (part, acc_b, norm_b, logit_b))
        for at, acc, _, _ in halves:
            acc[...] = jnp.dot(swished_ref[0, at : at + part, :], back[...], preferred_element_type=jnp.float32)
        for at, acc, normed, logits in halves:
            norm(at, acc, normed)
            logits[...] = jnp.dot(normed[...], head[...], preferred_element_type=jnp.float32)
        row = jnp.zeros((CHUNKS, LANES), jnp.float32)
        for at, _, _, logits in halves:
            row = errors(at, logits, row)
        error_ref[0] = row


def call(kernel, grid, in_specs, out_specs, out_shape, scratch, flops, moved, operands):
    return pl.pallas_call(
        kernel,
        grid_spec=pltpu.PrefetchScalarGridSpec(
            num_scalar_prefetch=1,
            grid=grid,
            in_specs=in_specs,
            out_specs=out_specs,
            scratch_shapes=scratch,
        ),
        out_shape=out_shape,
        compiler_params=pltpu.CompilerParams(
            dimension_semantics=("arbitrary",), vmem_limit_bytes=VMEM_BYTES
        ),
        cost_estimate=pl.CostEstimate(flops=flops // 16, bytes_accessed=moved // 16, transcendentals=0),
    )(*operands)


def whole(shape):
    return pl.BlockSpec(shape, lambda i, meta: (0,) * len(shape))


def by_slot(shape):
    return pl.BlockSpec((1,) + shape, lambda i, meta: (i,) + (0,) * len(shape))


INWARD = [(0, 1), (3, 2)]
ACROSS = [(1, 2), (2, 1)]
BEYOND = [(0, 2), (3, 1)]
OUTWARD = [(1, 0), (2, 3)]
OUT_BEYOND = [(2, 0), (1, 3)]


def along(x, pairs):
    return lax.ppermute(x, "seq", pairs)


def to_mate(x):
    pairs = [(a * 4 + z, (1 - a) * 4 + z) for a in (0, 1) for z in (1, 2)]
    return lax.ppermute(x, ("fsdp", "seq"), pairs)


def seed_swap(x, bit):
    return lax.ppermute(x, "seed", [(i, i ^ bit) for i in range(4)])


def hub_body(
    mel_frames,
    lengths,
    targets,
    frame_mask,
    stem_weight,
    conv_in_weight,
    conv_out_weight,
    depth_weight,
    head_weight,
    norm_gain,
):
    chip = lax.axis_index("seq")
    side = lax.axis_index("fsdp")
    seeds = lax.axis_size("seed")
    rows = targets.shape[1]
    width = stem_weight.shape[2]
    channels = depth_weight.shape[2]
    vocab = head_weight.shape[2]
    step = mel_frames.shape[1] // rows
    tile = rows // 2
    seed = lax.axis_index("seed")
    low = chip == 1
    is_hub = jnp.logical_or(low, chip == 2)

    length = lengths[0]
    positions = chip * rows + jnp.arange(rows, dtype=jnp.int32)
    counted = jnp.logical_and(frame_mask[0] > 0, positions < length)
    code = jnp.where(counted, targets[0], -1)
    first = conv_in_weight[0]
    blocks = mel_frames[0].reshape(rows, -1)
    share = rows // seeds
    margin = step * EDGE
    quarter = lax.dynamic_slice_in_dim(mel_frames[0], seed * share * step, share * step, 0).reshape(share, -1)
    edge_out = jnp.where(low, mel_frames[0, -margin:], mel_frames[0, :margin]).reshape(EDGE, -1)
    quarter_in = along(quarter, INWARD)
    edge = along(edge_out, ACROSS)
    outer_code = along(code, INWARD)
    first_held, quarter_in, edge, outer_code = lax.optimization_barrier((first, quarter_in, edge, outer_code))
    near_first, hub_first, far_first = [along(first_held, pairs_) for pairs_ in (INWARD, ACROSS, BEYOND)]
    held = first.shape[0]

    odd, upper = seed % 2 == 1, seed // 2 == 1
    beside, above, across = [seed_swap(quarter_in, bit) for bit in (1, 2, 3)]
    even_piece, odd_piece = jnp.where(odd, beside, quarter_in), jnp.where(odd, quarter_in, beside)
    even_other, odd_other = jnp.where(odd, across, above), jnp.where(odd, above, across)
    outer = jnp.concatenate(
        [
            jnp.where(upper, even_other, even_piece),
            jnp.where(upper, odd_other, odd_piece),
            jnp.where(upper, even_piece, even_other),
            jnp.where(upper, odd_piece, odd_other),
        ],
        axis=0,
    )

    groups = width // vocab
    head_rows = head_weight.shape[1]
    second = jnp.concatenate(
        [
            conv_out_weight[0],
            jnp.concatenate(jnp.split(head_weight[0], groups, axis=0), axis=1),
        ],
        axis=0,
    )
    slots = 4
    deep = tile + 2 * EDGE
    none = jnp.zeros_like(edge)
    frames = jnp.concatenate(
        [
            jnp.where(low, none, edge),
            jnp.where(low, outer, blocks),
            jnp.where(low, blocks, outer),
            jnp.where(low, edge, none),
            none,
        ],
        axis=0,
    )
    pairs = jnp.concatenate([frames[:-1], frames[1:]], axis=1)
    main = pairs[EDGE : EDGE + slots * tile].reshape(slots, CHUNKS, tile // CHUNKS, -1)
    main = main.transpose(0, 2, 1, 3).reshape(slots, tile, -1)
    margins = jnp.stack(
        [
            jnp.concatenate([pairs[k * tile : k * tile + EDGE], pairs[(k + 1) * tile + EDGE : (k + 1) * tile + 2 * EDGE]])
            for k in range(slots)
        ]
    )

    starts = (chip - 1) * 2 * rows + tile * jnp.arange(slots, dtype=jnp.int32)
    alive = jnp.logical_and(is_hub, starts < length).astype(jnp.int32)
    hub = jnp.clip(chip, 1, 2)
    meta = jnp.concatenate(
        [
            starts,
            lengths,
            alive,
            jnp.stack([hub, 3 * (hub - 1), 3 - hub, 3 * (2 - hub), side, jnp.max(alive)]),
        ]
    ).astype(jnp.int32)

    gains = norm_gain[0]
    half = tile // 2
    stem_out, normed = call(
        stem_kernel,
        (slots,),
        [by_slot(main.shape[1:]), by_slot(margins.shape[1:]), whole(stem_weight.shape[1:]), whole(gains.shape)],
        [by_slot((tile, width)), by_slot((deep, width))],
        [
            jax.ShapeDtypeStruct((slots, tile, width), jnp.bfloat16),
            jax.ShapeDtypeStruct((slots, deep, width), jnp.bfloat16),
        ],
        [
            pltpu.VMEM((half, width), jnp.float32),
            pltpu.VMEM((half, width), jnp.float32),
            pltpu.VMEM((2 * EDGE, width), jnp.float32),
        ],
        2 * slots * deep * main.shape[2] * width,
        2 * slots * deep * (main.shape[2] + 2 * width),
        (meta, main, margins, stem_weight[0], gains),
    )
    pinned = pl.BlockSpec(memory_space=pltpu.HBM)

    codes = jnp.concatenate([jnp.where(low, outer_code, code), jnp.where(low, code, outer_code)])
    codes = codes.reshape(slots, CHUNKS, tile // CHUNKS)
    far_first, normed, codes = lax.optimization_barrier((far_first, normed, codes))
    mine = [first, near_first, hub_first, far_first]
    first_pieces = (*mine, to_mate(jnp.concatenate(mine, axis=0)))
    near_second, hub_second, far_second = [along(second, pairs_) for pairs_ in (INWARD, ACROSS, BEYOND)]
    taps = jnp.broadcast_to(
        depth_weight[0].astype(jnp.float32)[:, None, :], (depth_weight.shape[1], CHUNKS, channels)
    )
    extent = tile // CHUNKS + depth_weight.shape[1] - 1
    swished = call(
        conv_kernel,
        (slots,),
        [by_slot((deep, width)), whole(taps.shape)] + [pinned] * 5,
        by_slot((tile, channels)),
        jax.ShapeDtypeStruct((slots, tile, channels), jnp.bfloat16),
        [
            pltpu.VMEM((8 * held, width), jnp.bfloat16),
            pltpu.VMEM((deep, 2 * LANES), jnp.float32),
            pltpu.VMEM((deep, 2 * LANES), jnp.float32),
            pltpu.VMEM((extent, CHUNKS, LANES), jnp.float32),
            pltpu.VMEM((2 * EDGE, LANES), jnp.float32),
            pltpu.VMEM((deep, LANES), jnp.float32),
            pltpu.SemaphoreType.DMA((8,)),
        ],
        2 * slots * deep * width * 2 * channels,
        2 * slots * deep * width + 8 * first.size * 2,
        (meta, normed, taps, *first_pieces),
    )

    near_second, hub_second, far_second, swished = lax.optimization_barrier(
        (near_second, hub_second, far_second, swished)
    )
    mine = [second, near_second, hub_second, far_second]
    second_pieces = (*mine, to_mate(second), to_mate(jnp.concatenate(mine[1:], axis=0)))
    errors = call(
        head_kernel,
        (slots,),
        [by_slot((tile, channels)), by_slot((tile, width)), by_slot(codes.shape[1:]), whole(gains.shape)]
        + [pinned] * 6,
        by_slot((CHUNKS, LANES)),
        jax.ShapeDtypeStruct((slots, CHUNKS, LANES), jnp.float32),
        [
            pltpu.VMEM((8 * conv_out_weight.shape[1], width), jnp.bfloat16),
            pltpu.VMEM((8 * head_rows, vocab), jnp.bfloat16),
            pltpu.VMEM((half, width), jnp.float32),
            pltpu.VMEM((half, width), jnp.float32),
            pltpu.VMEM((half, width), jnp.bfloat16),
            pltpu.VMEM((half, width), jnp.bfloat16),
            pltpu.VMEM((half, vocab), jnp.float32),
            pltpu.VMEM((half, vocab), jnp.float32),
            pltpu.SemaphoreType.DMA((8, 1 + groups)),
        ],
        2 * slots * tile * (channels + vocab) * width,
        2 * slots * tile * (channels + width),
        (meta, swished, stem_out, codes, gains, *second_pieces),
    )

    one, two, three = [seed_swap(errors, bit) for bit in (1, 2, 3)]
    total = ((errors + one) + (two + three)) / jnp.float32(seeds)
    total = total[:, :, : tile // CHUNKS].reshape(2, rows)
    part = jnp.sum(total).reshape(1)
    outer_half = jnp.where(low, total[0], total[1])
    own_half = jnp.where(low, total[1], total[0])
    from_hub = along(jnp.concatenate([outer_half, part]), OUTWARD)
    parts = [part[0], along(part, ACROSS)[0], along(part, OUT_BEYOND)[0], from_hub[rows]]
    frame_error = jnp.where(is_hub, own_half, from_hub[:rows])
    utt_score = ((parts[0] + parts[3]) + (parts[1] + parts[2])) / length.astype(jnp.float32)
    return (frame_error[None, :], utt_score.reshape(1))


def from_behind(x, axis, by):
    count = lax.axis_size(axis)
    pairs = [(i, i + by) for i in range(count) if 0 <= i + by < count]
    return lax.ppermute(x, axis, pairs)


def extended(x, sides, width):
    for axis, dim in sides:
        count, length = (lax.axis_size(axis), x.shape[dim])
        up = [(i, (i + 1) % count) for i in range(count - 1)]
        down = [(j, i) for i, j in up]
        last = lax.slice_in_dim(x, length - width, length, axis=dim)
        first = lax.slice_in_dim(x, 0, width, axis=dim)
        before = lax.ppermute(last, axis, up)
        after = lax.ppermute(first, axis, down)
        x = jnp.concatenate([before, x, after], axis=dim)
    return x


def layer_norm(values, gain_row):
    row_mean = jnp.mean(values, axis=-1, keepdims=True)
    centred = values - row_mean
    row_var = jnp.mean(centred * centred, axis=-1, keepdims=True)
    return (centred * lax.rsqrt(row_var + 1e-05) * gain_row).astype(jnp.bfloat16)


def block_product(left_rows, right_matrix):
    return jnp.dot(left_rows, right_matrix, preferred_element_type=jnp.float32)


def row_product(activations, shard_piece):
    return block_product(activations, shard_piece[0])


def body(
    mel_frames,
    lengths,
    targets,
    frame_mask,
    stem_weight,
    conv_in_weight,
    conv_out_weight,
    depth_weight,
    head_weight,
    norm_gain,
):
    frame_rows = targets.shape[1]
    blocks = mel_frames[0].reshape(frame_rows, -1)
    next_block = from_behind(blocks[:1], "seq", -1)
    following = jnp.concatenate([blocks[1:], next_block], 0)
    half_width = blocks.shape[1]
    stem_matrix = stem_weight[0]
    stem_out = (
        jnp.dot(blocks, stem_matrix[:half_width], preferred_element_type=jnp.float32)
        + jnp.dot(following, stem_matrix[half_width:], preferred_element_type=jnp.float32)
    ).astype(jnp.bfloat16)
    offset = lax.axis_index("seq") * frame_rows
    length = lengths[0]
    positions = offset + jnp.arange(frame_rows, dtype=jnp.int32)
    frame_live = positions < length
    gain_rows = norm_gain[0]
    normed_one = layer_norm(stem_out.astype(jnp.float32), gain_rows[0])
    tap_count = depth_weight.shape[1]
    channels = depth_weight.shape[2]
    halo_width = tap_count // 2
    conv_input = extended(normed_one, (("seq", 0),), halo_width)
    mixed_rows = row_product(
        conv_input, lax.all_gather(conv_in_weight, ("fsdp", "seq"), axis=1, tiled=True)
    )
    input_positions = offset - halo_width + jnp.arange(conv_input.shape[0], dtype=jnp.int32)
    input_live = jnp.logical_and(input_positions >= 0, input_positions < length)
    gated_rows = (
        mixed_rows[:, :channels]
        * jax.nn.sigmoid(mixed_rows[:, channels:])
        * input_live[:, None].astype(jnp.float32)
    ).astype(jnp.bfloat16)
    depthwise = jnp.zeros((frame_rows, channels), jnp.float32)
    for tap_index in range(tap_count):
        depthwise = depthwise + gated_rows[tap_index : tap_index + frame_rows].astype(
            jnp.float32
        ) * depth_weight[0, tap_index].astype(jnp.float32)
    swished = jax.nn.silu(depthwise).astype(jnp.bfloat16)
    conv_proj = row_product(
        swished, lax.all_gather(conv_out_weight, ("fsdp", "seq"), axis=1, tiled=True)
    )
    after_conv = stem_out.astype(jnp.float32) + conv_proj
    normed_two = layer_norm(after_conv, gain_rows[1])
    logits = row_product(
        normed_two, lax.all_gather(head_weight, ("fsdp", "seq"), axis=1, tiled=True)
    )
    posterior = jax.nn.softmax(logits, axis=-1)
    vocab_size = logits.shape[1]
    onehot = (jnp.arange(vocab_size, dtype=jnp.int32)[None, :] == targets[0][:, None]).astype(
        jnp.float32
    )
    differ = posterior - onehot
    frame_err = (
        jnp.sqrt(jnp.sum(differ * differ, axis=-1))
        * frame_live.astype(jnp.float32)
        * frame_mask[0].astype(jnp.float32)
    )
    seed_count = lax.axis_size("seed")
    frame_error = lax.psum(frame_err, "seed") / jnp.float32(seed_count)
    numerator = lax.psum(jnp.sum(frame_error), "seq")
    utt_score = numerator / length.astype(jnp.float32)
    return (frame_error[None, :], utt_score.reshape(1))


def solution(mesh):
    in_specs = (
        P("fsdp", "seq", None),
        P("fsdp"),
        P("fsdp", "seq"),
        P("fsdp", "seq"),
        P("seed", None, None),
        P("seed", ("fsdp", "seq"), None),
        P("seed", ("fsdp", "seq"), None),
        P("seed", None, None),
        P("seed", ("fsdp", "seq"), None),
        P("seed", None, None),
    )
    out_specs = (P("fsdp", "seq"), P("fsdp"))
    hubs = mesh.shape["seq"] == 4 and mesh.shape["fsdp"] == 2
    return jax.shard_map(
        hub_body if hubs else body, mesh=mesh, in_specs=in_specs, out_specs=out_specs, check_vma=False
    )
```
